256 devices in a mesh: sup: 32 (over x, z), tm: 8 (over y, core).
Axes of the slice: x: 4, y: 4, z: 8, core: 2. Of those that a mesh axis runs over, the one named last changes fastest.
Arguments:
- factor: bfloat16 [8192, 8192], P('sup'), may hold values from -6 to 6, as said below
- white_noise: bfloat16 [8192, 16384], P('sup', 'tm'), may hold values from -6 to 6
- site_class: int32 [8192], replicated, may hold values from 0 to 3
- site_decay: float32 [2, 4], replicated, may hold values from 2e-05 to 0.02
- site_angle: float32 [2, 4], replicated, may hold values from 0.05 to 0.8
- site_mix: float32 [4, 4], replicated, may hold values from -3 to 3
Outputs:
- motions: float32 [8192, 16384], P('sup', 'tm')
The draws below stay inside these ranges and needn't reach their ends.
Inputs may be any that keep to these rules, and one draw needn't show every extreme that they name: factor is zero above the diagonal and one on it.
All inputs are finite; a program needn't handle non-finite values.
Results may differ from the reference program's by a relative error of at most 0.0045.
Values may be sent and summed in bfloat16 or wider, within the bound.
No kernel may reach another device: no remote copies, remote signals or barrier semaphores. Data moves between devices by JAX's collectives and lax.ppermute only.
A program may use at most 128 MiB of HBM per device.

```python
import math
import jax
import jax.numpy as jnp
from jax import lax

S = 8192
NC = 4
CH = 256
TIME = 16384


def draw_factor(key, part):
    row_index = jnp.arange(S, dtype=jnp.int32)[:, None]
    col_index = jnp.arange(S, dtype=jnp.int32)[None, :]
    values = jax.random.normal(key, (S, S), jnp.float32)
    scaled = jnp.clip(values, -6.0, 6.0) / jnp.sqrt(row_index.astype(jnp.float32) + 1.0)
    lower = jnp.where(col_index < row_index, scaled, 0.0)
    return jnp.where(col_index == row_index, 1.0, lower).astype(jnp.bfloat16)


def with_ends(values, stream_key, smallest, top_value):
    extent = values.shape
    place = [jax.random.randint(jax.random.fold_in(stream_key, axis), (), 0, extent[axis]) for axis in range(len(extent))]
    values = values.at[tuple(place)].set(smallest)
    longest = extent.index(max(extent))
    place[longest] = (place[longest] + 1) % extent[longest]
    return values.at[tuple(place)].set(top_value)


def shard_levels(own_key, dims, split, low, high):
    def one(position, blocks):
        draws = jax.random.uniform(jax.random.fold_in(jax.random.fold_in(own_key, 6), position), (blocks,), jnp.float32, low / len(split), high / len(split))
        return jnp.repeat(jnp.exp(draws), dims[position] // blocks).reshape((-1,) + (1,) * (len(dims) - position - 1))

    loudness = one(*split[0])
    for cut in split[1:]:
        loudness = loudness * one(*cut)
    return loudness


def gaussian(stream_key, dims, spread, limit, cuts=(), held_as=jnp.bfloat16):
    array = spread * jax.random.normal(stream_key, dims, jnp.float32)
    if cuts:
        array = array * shard_levels(stream_key, dims, cuts, -0.22, 0.18)
    return jnp.clip(array, -limit, limit).astype(held_as)


def setup_inputs(seed: int = 0) -> dict:
    arg_keys = jax.random.split(jax.random.key(seed), 7)
    return {
        "factor": draw_factor(jax.random.fold_in(arg_keys[6], 71), 0),
        "white_noise": gaussian(arg_keys[1], (S, TIME), 1.0, 6.0, ((0, 32), (1, 8))),
        "site_class": with_ends(jax.random.randint(arg_keys[2], (S,), 0, NC), jax.random.fold_in(arg_keys[2], 1), 0, NC - 1).astype(jnp.int32),
        "site_decay": jnp.clip(jnp.exp(jax.random.uniform(arg_keys[3], (2, NC), jnp.float32, math.log(1.9999999494757503e-05), math.log(0.02))), 1.9999999494757503e-05, 0.02),
        "site_angle": jnp.clip(jax.random.uniform(arg_keys[4], (2, NC), jnp.float32, 0.05, 0.8), 0.05, 0.8),
        "site_mix": gaussian(arg_keys[5], (4, NC), 1.0, 3.0, (), jnp.float32),
    }


PRECISE = lax.Precision.HIGHEST

def system(site_decay, site_angle, site_mix):
    radius = 1.0 - site_decay
    norm_gain = jnp.sqrt(site_decay * (2.0 - site_decay))
    cos_ground = radius[0] * jnp.cos(site_angle[0])
    sin_ground = radius[0] * jnp.sin(site_angle[0])
    cos_high = radius[1] * jnp.cos(site_angle[1])
    sin_high = radius[1] * jnp.sin(site_angle[1])
    zeros_row = jnp.zeros_like(cos_ground)
    ones_row = jnp.ones_like(cos_ground)
    mix_a, mix_b, out_a, out_b = (site_mix[0], site_mix[1], site_mix[2], site_mix[3])
    row_list = [[cos_ground, -sin_ground, zeros_row, zeros_row], [sin_ground, cos_ground, zeros_row, zeros_row], [norm_gain[0] * (mix_a * cos_ground + mix_b * sin_ground), norm_gain[0] * (mix_b * cos_ground - mix_a * sin_ground), cos_high, -sin_high], [zeros_row, zeros_row, sin_high, cos_high]]
    matrix = jnp.stack([jnp.stack(entries, axis=-1) for entries in row_list], axis=1)
    entry_vec = jnp.stack([ones_row, zeros_row, norm_gain[0] * mix_a, zeros_row], axis=-1)
    readout = jnp.stack([zeros_row, zeros_row, norm_gain[1] * out_a, norm_gain[1] * out_b], axis=-1)
    return (matrix, entry_vec, readout)

def power_table(matrix, length_total):
    powers = matrix[None]
    while powers.shape[0] < length_total:
        top_power = powers[-1]
        further = jnp.einsum('kab,jkbc->jkac', top_power, powers, precision=PRECISE)
        powers = jnp.concatenate([powers, further], axis=0)
    powers = powers[:length_total]
    return (powers[-1], powers)

def tables(site_decay, site_angle, site_mix, length_total, group_len):
    matrix, entry_vec, readout = system(site_decay, site_angle, site_mix)
    classes = matrix.shape[0]
    block_power, powers = power_table(matrix, max(length_total, group_len))
    gains = jnp.einsum('ka,jkab->kbj', readout, powers[:length_total], precision=PRECISE)
    responses = jnp.einsum('jkab,kb->kja', powers[:group_len - 1], entry_vec, precision=PRECISE)
    responses = jnp.concatenate([entry_vec[:, None, :], responses], axis=1)
    impulse = jnp.einsum('ka,kma->km', readout, responses, precision=PRECISE)
    padded_len = 2 * group_len
    padded = jnp.concatenate([impulse, jnp.zeros((classes, group_len), jnp.float32)], axis=1)
    tiled = jnp.tile(padded, (1, group_len))[:, :group_len * (padded_len - 1)]
    toeplitz = tiled.reshape(classes, group_len, padded_len - 1)[:, :, :group_len]
    toeplitz_cat = toeplitz.transpose(1, 0, 2).reshape(group_len, classes * group_len).astype(jnp.bfloat16)
    final_cat = responses[:, ::-1, :].transpose(1, 0, 2).reshape(group_len, classes * 4).astype(jnp.bfloat16)
    group_power = powers[group_len - 1]
    return (toeplitz_cat, gains, final_cat, group_power, powers[length_total - 1])

def filter_group(group_input, onehot, toeplitz_cat, gain_rows, power_rows, final_cat, carry_state):
    row_count = group_input.shape[0]
    group_len = group_input.shape[1]
    classes = onehot.shape[1]
    all_classes = jnp.dot(group_input, toeplitz_cat, preferred_element_type=jnp.float32).reshape(row_count, classes, group_len)
    filtered = lax.optimization_barrier(jnp.sum(onehot[:, :, None] * all_classes, axis=1))
    filtered = filtered + jnp.einsum('rcj,cr->rj', gain_rows, carry_state, precision=PRECISE)
    entered = jnp.dot(group_input, final_cat, preferred_element_type=jnp.float32).reshape(row_count, classes, 4)
    entered = lax.optimization_barrier(jnp.sum(onehot[:, :, None] * entered, axis=1))
    carry_state = jnp.einsum('rca,ar->cr', power_rows, carry_state, precision=PRECISE) + entered.T
    return (filtered, carry_state)

def reference(factor, white_noise, site_class, site_decay, site_angle, site_mix):
    excitation = jnp.dot(factor, white_noise, preferred_element_type=jnp.float32).astype(jnp.bfloat16)
    classes = site_decay.shape[1]
    onehot = (site_class[:, None] == jnp.arange(classes, dtype=jnp.int32)[None, :]).astype(jnp.float32)
    toeplitz_cat, gains, final_cat, group_power, ignored = tables(site_decay, site_angle, site_mix, CH, CH)
    gain_rows = jnp.einsum('rk,kcj->rcj', onehot, gains[:, :, :CH], precision=PRECISE)
    power_rows = jnp.einsum('rk,kab->rab', onehot, group_power, precision=PRECISE)
    group_stack = excitation.reshape(S, TIME // CH, CH).transpose(1, 0, 2)

    def advance(carry_state, group_input):
        filtered, carry_state = filter_group(group_input, onehot, toeplitz_cat, gain_rows, power_rows, final_cat, carry_state)
        return (carry_state, filtered)
    ignored_state, outputs = lax.scan(advance, jnp.zeros((4, S), jnp.float32), group_stack)
    return outputs.transpose(1, 0, 2).reshape(S, TIME)
```

```python
import functools

import jax
import jax.numpy as jnp
from jax import lax
from jax.experimental import pallas as pl
from jax.experimental.pallas import tpu as pltpu
from jax.sharding import Mesh, PartitionSpec as P

CH = 256
NX, NZ, NY, NCORE = 4, 8, 4, 2
ROWS = 256
SLAB = 512
QUARTER = 2048
PACK = 80
F32 = jnp.float32
BF16 = jnp.bfloat16
PRECISE = lax.Precision.HIGHEST


def system(site_decay, site_angle, site_mix):
    radius = 1.0 - site_decay
    norm_gain = jnp.sqrt(site_decay * (2.0 - site_decay))
    cos_ground = radius[0] * jnp.cos(site_angle[0])
    sin_ground = radius[0] * jnp.sin(site_angle[0])
    cos_high = radius[1] * jnp.cos(site_angle[1])
    sin_high = radius[1] * jnp.sin(site_angle[1])
    zeros_row = jnp.zeros_like(cos_ground)
    ones_row = jnp.ones_like(cos_ground)
    mix_a, mix_b, out_a, out_b = (site_mix[0], site_mix[1], site_mix[2], site_mix[3])
    row_list = [
        [cos_ground, -sin_ground, zeros_row, zeros_row],
        [sin_ground, cos_ground, zeros_row, zeros_row],
        [
            norm_gain[0] * (mix_a * cos_ground + mix_b * sin_ground),
            norm_gain[0] * (mix_b * cos_ground - mix_a * sin_ground),
            cos_high,
            -sin_high,
        ],
        [zeros_row, zeros_row, sin_high, cos_high],
    ]
    matrix = jnp.stack([jnp.stack(entries, axis=-1) for entries in row_list], axis=1)
    entry_vec = jnp.stack([ones_row, zeros_row, norm_gain[0] * mix_a, zeros_row], axis=-1)
    readout = jnp.stack([zeros_row, zeros_row, norm_gain[1] * out_a, norm_gain[1] * out_b], axis=-1)
    return (matrix, entry_vec, readout)


def tables(site_decay, site_angle, site_mix):
    matrix, entry_vec, readout = system(site_decay, site_angle, site_mix)
    classes = matrix.shape[0]
    powers = matrix[None]
    while powers.shape[0] < CH:
        further = jnp.einsum("kab,jkbc->jkac", powers[-1], powers, precision=PRECISE)
        powers = jnp.concatenate([powers, further], axis=0)
    gains = jnp.einsum("ka,jkab->kbj", readout, powers, precision=PRECISE)
    responses = jnp.einsum("jkab,kb->kja", powers[: CH - 1], entry_vec, precision=PRECISE)
    responses = jnp.concatenate([entry_vec[:, None, :], responses], axis=1)
    impulse = jnp.einsum("ka,kma->km", readout, responses, precision=PRECISE)
    padded_len = 2 * CH
    padded = jnp.concatenate([impulse, jnp.zeros((classes, CH), F32)], axis=1)
    tiled = jnp.tile(padded, (1, CH))[:, : CH * (padded_len - 1)]
    toeplitz = tiled.reshape(classes, CH, padded_len - 1)[:, :, :CH]
    toeplitz = toeplitz.reshape(classes * CH, CH).astype(BF16)
    final = responses[:, ::-1, :].transpose(0, 2, 1).astype(BF16)
    final = jnp.concatenate([final, jnp.zeros_like(final)], axis=1).reshape(classes * 8, CH)
    gains = gains.reshape(classes * 4, CH)
    gains_hi = gains.astype(BF16)
    gains_lo = (gains - gains_hi.astype(F32)).astype(BF16)
    gain_stack = jnp.concatenate([gains_hi, gains_lo, gains_hi], axis=0)
    power = powers[-1]
    power_two = jnp.einsum("kab,kbc->kac", power, power, precision=PRECISE)
    return toeplitz, final, gain_stack, power, power_two


def per_row(power, onehot):
    return jnp.sum(power.transpose(2, 1, 0)[:, :, :, None] * onehot[None, None], axis=2)


def apply_power(table, state):
    out = table[0] * state[0:1]
    for b in range(1, 4):
        out = out + table[b] * state[b : b + 1]
    return out


def factor_block(g_ref, s):
    parts = [g_ref[s, :, 0:32, :]]
    if s >= 1:
        parts.append(g_ref[s, :, 32:64, :])
    if s >= 2:
        low = g_ref[1, :, 64:80, :] if s == 2 else g_ref[0, :, 32:48, :]
        parts.append(jnp.concatenate([g_ref[s, :, 64:80, :], low], axis=1))
    if s >= 3:
        parts.append(g_ref[0, :, 48:80, :])
    return jnp.concatenate([p.reshape(ROWS, CH) for p in parts], axis=1)


def product_kernel(blocks, has_acc, last, *refs):
    refs = list(refs)
    refs.pop(0)
    acc_ref = refs.pop(0) if has_acc else None
    g_refs = [refs.pop(0) for _ in range(blocks)]
    n_refs = [refs.pop(0) for _ in range(blocks)] if not last else [refs.pop(0), refs.pop(0)]
    if last:
        final_ref, onehot_ref, out_ref, end_ref = refs
    else:
        (out_ref,) = refs
    for s in range(NX):
        rows = pl.ds(s * ROWS, ROWS)
        depth = (s + 1) * ROWS
        total = acc_ref[rows, :] if has_acc else None
        for b in range(blocks):
            if last:
                noise = n_refs[0][0 : min(depth, 512), :]
                if depth > 512:
                    noise = jnp.concatenate([noise, n_refs[1][0 : depth - 512, :]], axis=0)
            else:
                noise = n_refs[b][0:depth, :]
            term = jnp.dot(factor_block(g_refs[b], s), noise, preferred_element_type=F32)
            total = term if total is None else total + term
        if last:
            out_ref[rows, :] = total.astype(BF16)
        else:
            out_ref[rows, :] = total
    if last:
        ends = lax.dot_general(
            final_ref[...], out_ref[...], (((1,), (1,)), ((), ())), preferred_element_type=F32
        )
        picked = onehot_ref[0:1, :] * ends[0:8]
        for k in range(1, 4):
            picked = picked + onehot_ref[k : k + 1, :] * ends[k * 8 : k * 8 + 8]
        end_ref[...] = picked


def product(acc, gathered, where_z, noise_blocks, last=None):
    blocks = len(where_z)
    width = noise_blocks[0].shape[1]
    scalars = jnp.stack(where_z).astype(jnp.int32)

    def g_spec(b):
        return pl.BlockSpec((NX, 8, PACK, CH), lambda i, zs: (0, 0, 0, zs[b]))

    def whole(shape):
        return pl.BlockSpec(shape, lambda i, zs: (0,) * len(shape))

    args, specs = [], []
    if acc is not None:
        args.append(acc)
        specs.append(whole(acc.shape))
    args += [gathered] * blocks
    specs += [g_spec(b) for b in range(blocks)]
    args += noise_blocks
    specs += [whole(n.shape) for n in noise_blocks]
    rows = NX * ROWS
    if last is None:
        out_shape = jax.ShapeDtypeStruct((rows, width), F32)
        out_specs = whole((rows, width))
    else:
        args += list(last)
        specs += [whole(a.shape) for a in last]
        out_shape = (
            jax.ShapeDtypeStruct((rows, width), BF16),
            jax.ShapeDtypeStruct((8, rows), F32),
        )
        out_specs = (whole((rows, width)), whole((8, rows)))
    return pl.pallas_call(
        functools.partial(product_kernel, blocks, acc is not None, last is not None),
        grid_spec=pltpu.PrefetchScalarGridSpec(
            num_scalar_prefetch=1, grid=(1,), in_specs=specs, out_specs=out_specs
        ),
        out_shape=out_shape,
        compiler_params=pltpu.CompilerParams(vmem_limit_bytes=40 * 1024 * 1024),
        cost_estimate=pl.CostEstimate(
            flops=blocks * 2 * 10 * ROWS * CH * width,
            bytes_accessed=blocks * (1310720 + 524288) + 2097152,
            transcendentals=0,
        ),
    )(scalars, *args)


def filter_kernel(
    place, first_ref, second_ref, slabs_ref, mask_ref, onehot_ref, one_ref, two_ref,
    toeplitz_ref, final_ref, gain_ref, out_ref, state_ref,
):
    step = pl.program_id(0)
    one = [one_ref[b] for b in range(4)]

    @pl.when(step == 0)
    def _():
        two = [two_ref[b] for b in range(4)]

        def advance(t, state):
            return apply_power(two, state) + slabs_ref[t]

        state_ref[...] = lax.fori_loop(0, place[0], advance, jnp.zeros((4, ROWS), F32))

    state = state_ref[...]
    for half, ref in enumerate((first_ref, second_ref)):
        local = ref[0]
        masked = jnp.concatenate([local * mask_ref[:, k : k + 1] for k in range(4)], axis=1)
        spread = jnp.concatenate([onehot_ref[k : k + 1, :] * state for k in range(4)], axis=0)
        high = spread.astype(BF16)
        low = (spread - high.astype(F32)).astype(BF16)
        stacked = jnp.concatenate([high, high, low], axis=0)
        carried = lax.dot_general(
            stacked, gain_ref[...], (((0,), (0,)), ((), ())), preferred_element_type=F32
        )
        out_ref[:, half * CH : (half + 1) * CH] = (
            jnp.dot(masked, toeplitz_ref[...], preferred_element_type=F32) + carried
        )
        ends = lax.dot_general(
            final_ref[...], local, (((1,), (1,)), ((), ())), preferred_element_type=F32
        )
        entered = onehot_ref[0:1, :] * ends[0:4]
        for k in range(1, 4):
            entered = entered + onehot_ref[k : k + 1, :] * ends[k * 8 : k * 8 + 4]
        state = apply_power(one, state) + entered
    state_ref[...] = state


def filtered(place, first, second, slabs, mask, onehot, one, two, toeplitz, final, gain):
    def whole(a):
        return pl.BlockSpec(a.shape, lambda i, zs: (0,) * a.ndim)

    piece = pl.BlockSpec((1, ROWS, CH), lambda i, zs: (i, 0, 0))
    rest = (slabs, mask, onehot, one, two, toeplitz, final, gain)
    return pl.pallas_call(
        filter_kernel,
        grid_spec=pltpu.PrefetchScalarGridSpec(
            num_scalar_prefetch=1,
            grid=(NX,),
            in_specs=[piece, piece] + [whole(a) for a in rest],
            out_specs=pl.BlockSpec((ROWS, SLAB), lambda i, zs: (0, i)),
            scratch_shapes=[pltpu.VMEM((4, ROWS), F32)],
        ),
        out_shape=jax.ShapeDtypeStruct((ROWS, NX * SLAB), F32),
        compiler_params=pltpu.CompilerParams(vmem_limit_bytes=40 * 1024 * 1024),
        cost_estimate=pl.CostEstimate(
            flops=8 * 2 * ROWS * CH * 1100, bytes_accessed=4 * 1024 * 1024, transcendentals=0
        ),
    )(place, first, second, *rest)


def ring(value, by):
    return lax.ppermute(value, "z", [(i, (i + by) % NZ) for i in range(NZ)])


def body(factor, white_noise, site_class, site_decay, site_angle, site_mix):
    x = lax.axis_index("x")
    z = lax.axis_index("z")
    tm = lax.axis_index("y") * NCORE + lax.axis_index("c")

    mine = lax.dynamic_slice(factor, (tm * 32, 0), (32, factor.shape[1]))
    quarter = [mine[:, q * QUARTER : (q + 1) * QUARTER] for q in range(4)]
    surplus = jnp.concatenate([quarter[2][16:], quarter[3]], axis=0)
    taken = lax.ppermute(surplus, "x", [(3, 0), (2, 1)])
    share = jnp.concatenate(
        [
            quarter[0],
            jnp.where(x == 0, taken[:32], quarter[1]),
            jnp.where(x == 0, taken[32:48], jnp.where(x == 1, taken[:16], quarter[2][:16])),
        ],
        axis=0,
    )
    gathered = lax.all_gather(share, ("x", "y", "c"))
    gathered = gathered.reshape(NX, 8, PACK, QUARTER)

    toeplitz, final, gain, power, power_two = tables(site_decay, site_angle, site_mix)
    by_block = site_class.reshape(NX, NZ, ROWS)
    ids = jnp.arange(4, dtype=jnp.int32)
    tile_class = lax.dynamic_slice(by_block, (0, z, 0), (NX, 1, ROWS)).reshape(1, NX * ROWS)
    tile_hot = (tile_class == ids[:, None]).astype(F32)
    own_class = lax.dynamic_slice(by_block, (x, z, 0), (1, 1, ROWS)).reshape(1, ROWS)
    own_hot = (own_class == ids[:, None]).astype(F32)
    own_mask = (own_class.reshape(ROWS, 1) == ids[None, :]).astype(BF16)

    cut = white_noise.reshape(ROWS, NX, 2, CH)
    excitation, ends = [], []
    for half in range(2):
        slabs = cut[:, :, half, :].transpose(1, 0, 2).reshape(NX * ROWS, CH)
        own = lax.all_to_all(slabs, "x", 0, 0, tiled=True)
        up1, down1 = ring(own, 1), ring(own, -1)
        up2, down2 = ring(up1, 1), ring(down1, -1)
        up3, down3 = ring(up2, 1), ring(down2, -1)
        up4, down4 = ring(up3[:512], 1), ring(down3[512:], -1)
        total = product(None, gathered, [z, (z + 7) % 8, (z + 1) % 8], [own, up1, down1])
        total = product(total, gathered, [(z + 6) % 8, (z + 2) % 8], [up2, down2])
        total = product(total, gathered, [(z + 5) % 8, (z + 3) % 8], [up3, down3])
        local, end = product(total, gathered, [(z + 4) % 8], [up4, down4], (final, tile_hot))
        ends.append(end[:4])
        excitation.append(
            lax.all_to_all(local, "x", 0, 0, tiled=True).reshape(NX, ROWS, CH)
        )
    slab_end = apply_power(per_row(power, tile_hot), ends[0]) + ends[1]
    all_ends = lax.all_gather(slab_end, ("y", "c", "x"))
    own_ends = lax.dynamic_slice(all_ends, (0, 0, x * ROWS), (32, 4, ROWS))
    return filtered(
        jnp.reshape(tm * NX, (1,)).astype(jnp.int32),
        excitation[0], excitation[1], own_ends, own_mask, own_hot,
        per_row(power, own_hot), per_row(power_two, own_hot), toeplitz, final, gain,
    )


def solution(mesh):
    fine = Mesh(mesh.devices.reshape(NX, NZ, NY, NCORE), ("x", "z", "y", "c"))
    rows = ("x", "z")
    in_specs = (P(rows, None), P(rows, ("y", "c")), P(), P(), P(), P())
    return jax.shard_map(
        body, mesh=fine, in_specs=in_specs, out_specs=P(rows, ("y", "c")), check_vma=False
    )
```

```python
import functools

import jax
import jax.numpy as jnp
from jax import lax
from jax.experimental import pallas as pl
from jax.experimental.pallas import tpu as pltpu
from jax.sharding import Mesh, PartitionSpec as P

CH = 256
NX, NZ, NY, NCORE = 4, 8, 4, 2
ROWS = 256
SLAB = 512
FIRST = (0, 0, 2, 3)
VMEM_LIMIT = 58 * 1024 * 1024
F32 = jnp.float32
BF16 = jnp.bfloat16
PRECISE = lax.Precision.HIGHEST


def system(site_decay, site_angle, site_mix):
    radius = 1.0 - site_decay
    norm_gain = jnp.sqrt(site_decay * (2.0 - site_decay))
    cos_ground = radius[0] * jnp.cos(site_angle[0])
    sin_ground = radius[0] * jnp.sin(site_angle[0])
    cos_high = radius[1] * jnp.cos(site_angle[1])
    sin_high = radius[1] * jnp.sin(site_angle[1])
    zeros_row = jnp.zeros_like(cos_ground)
    ones_row = jnp.ones_like(cos_ground)
    mix_a, mix_b, out_a, out_b = (site_mix[0], site_mix[1], site_mix[2], site_mix[3])
    row_list = [
        [cos_ground, -sin_ground, zeros_row, zeros_row],
        [sin_ground, cos_ground, zeros_row, zeros_row],
        [
            norm_gain[0] * (mix_a * cos_ground + mix_b * sin_ground),
            norm_gain[0] * (mix_b * cos_ground - mix_a * sin_ground),
            cos_high,
            -sin_high,
        ],
        [zeros_row, zeros_row, sin_high, cos_high],
    ]
    matrix = jnp.stack([jnp.stack(entries, axis=-1) for entries in row_list], axis=1)
    entry_vec = jnp.stack([ones_row, zeros_row, norm_gain[0] * mix_a, zeros_row], axis=-1)
    readout = jnp.stack([zeros_row, zeros_row, norm_gain[1] * out_a, norm_gain[1] * out_b], axis=-1)
    return (matrix, entry_vec, readout)


def tables(site_decay, site_angle, site_mix):
    matrix, entry_vec, readout = system(site_decay, site_angle, site_mix)
    classes = matrix.shape[0]
    powers = matrix[None]
    while powers.shape[0] < CH:
        further = jnp.einsum("kab,jkbc->jkac", powers[-1], powers, precision=PRECISE)
        powers = jnp.concatenate([powers, further], axis=0)
    gains = jnp.einsum("ka,jkab->kbj", readout, powers, precision=PRECISE)
    responses = jnp.einsum("jkab,kb->kja", powers[: CH - 1], entry_vec, precision=PRECISE)
    responses = jnp.concatenate([entry_vec[:, None, :], responses], axis=1)
    impulse = jnp.einsum("ka,kma->km", readout, responses, precision=PRECISE)
    padded_len = 2 * CH
    padded = jnp.concatenate([impulse, jnp.zeros((classes, CH), F32)], axis=1)
    tiled = jnp.tile(padded, (1, CH))[:, : CH * (padded_len - 1)]
    toeplitz = tiled.reshape(classes, CH, padded_len - 1)[:, :, :CH]
    toeplitz = toeplitz.reshape(classes * CH, CH).astype(BF16)
    final = responses[:, ::-1, :].transpose(0, 2, 1).astype(BF16)
    final = jnp.concatenate([final, jnp.zeros_like(final)], axis=1).reshape(classes * 8, CH)
    gains = gains.reshape(classes * 4, CH)
    gains_hi = lax.reduce_precision(gains, 8, 7)
    gains_lo = (gains - gains_hi).astype(BF16)
    gains_hi = gains_hi.astype(BF16)
    gain_stack = jnp.concatenate([gains_hi, gains_lo, gains_hi], axis=0)
    power = powers[-1]
    power_two = jnp.einsum("kab,kbc->kac", power, power, precision=PRECISE)
    return toeplitz, final, gain_stack, power, power_two


def per_row(power, onehot):
    return jnp.sum(power.transpose(2, 1, 0)[:, :, :, None] * onehot[None, None], axis=2)


def apply_power(table, state):
    out = table[0] * state[0:1]
    for b in range(1, 4):
        out = out + table[b] * state[b : b + 1]
    return out


def factor_block(g_refs, s):
    parts = [g_refs[q][s - FIRST[q]].reshape(ROWS, CH) for q in range(s + 1)]
    return jnp.concatenate(parts, axis=1) if s else parts[0]


def product_kernel(blocks, has_acc, last, *refs):
    refs = list(refs)
    refs.pop(0)
    acc_ref = refs.pop(0) if has_acc else None
    g_refs = [[refs.pop(0) for _ in range(NX)] for _ in range(blocks)]
    n_refs = [refs.pop(0) for _ in range(blocks)] if not last else [refs.pop(0), refs.pop(0)]
    if last:
        final_ref, onehot_ref, out_ref, end_ref = refs
    else:
        (out_ref,) = refs
    for s in range(NX):
        rows = pl.ds(s * ROWS, ROWS)
        depth = (s + 1) * ROWS
        total = acc_ref[rows, :] if has_acc else None
        for b in range(blocks):
            if last:
                noise = n_refs[0][0 : min(depth, 512), :]
                if depth > 512:
                    noise = jnp.concatenate([noise, n_refs[1][0 : depth - 512, :]], axis=0)
            else:
                noise = n_refs[b][0:depth, :]
            term = jnp.dot(factor_block(g_refs[b], s), noise, preferred_element_type=F32)
            total = term if total is None else total + term
        if last:
            out_ref[rows, :] = total.astype(BF16)
        else:
            out_ref[rows, :] = total
    if last:
        ends = lax.dot_general(
            final_ref[...], out_ref[...], (((1,), (1,)), ((), ())), preferred_element_type=F32
        )
        picked = onehot_ref[0:1, :] * ends[0:8]
        for k in range(1, 4):
            picked = picked + onehot_ref[k : k + 1, :] * ends[k * 8 : k * 8 + 8]
        end_ref[...] = picked


def product(acc, gathered, where_z, noise_blocks, last=None):
    blocks = len(where_z)
    width = noise_blocks[0].shape[1]
    scalars = jnp.stack(where_z).astype(jnp.int32)

    def g_spec(b, q):
        first, count = FIRST[q], NX - FIRST[q]
        return pl.BlockSpec(
            (count, 8, 32, CH), lambda i, zs: (first // count, 0, 0, q * NZ + zs[b])
        )

    def whole(shape):
        return pl.BlockSpec(shape, lambda i, zs: (0,) * len(shape))

    args, specs = [], []
    if acc is not None:
        args.append(acc)
        specs.append(whole(acc.shape))
    args += [gathered] * (blocks * NX)
    specs += [g_spec(b, q) for b in range(blocks) for q in range(NX)]
    args += noise_blocks
    specs += [whole(n.shape) for n in noise_blocks]
    rows = NX * ROWS
    if last is None:
        out_shape = jax.ShapeDtypeStruct((rows, width), F32)
        out_specs = whole((rows, width))
    else:
        args += list(last)
        specs += [whole(a.shape) for a in last]
        out_shape = (
            jax.ShapeDtypeStruct((rows, width), BF16),
            jax.ShapeDtypeStruct((8, rows), F32),
        )
        out_specs = (whole((rows, width)), whole((8, rows)))
    return pl.pallas_call(
        functools.partial(product_kernel, blocks, acc is not None, last is not None),
        grid_spec=pltpu.PrefetchScalarGridSpec(
            num_scalar_prefetch=1, grid=(1,), in_specs=specs, out_specs=out_specs
        ),
        out_shape=out_shape,
        compiler_params=pltpu.CompilerParams(vmem_limit_bytes=VMEM_LIMIT),
        cost_estimate=pl.CostEstimate(
            flops=blocks * 2 * 10 * ROWS * CH * width,
            bytes_accessed=blocks * (1310720 + 524288) + 2097152,
            transcendentals=0,
        ),
    )(scalars, *args)


def filter_kernel(
    place, first_ref, second_ref, slabs_ref, mask_ref, onehot_ref, one_ref, two_ref,
    toeplitz_ref, final_ref, gain_ref, out_ref, state_ref,
):
    step = pl.program_id(0)
    one = [one_ref[b] for b in range(4)]

    @pl.when(step == 0)
    def _():
        two = [two_ref[b] for b in range(4)]

        def advance(t, state):
            return apply_power(two, state) + slabs_ref[t]

        state_ref[...] = lax.fori_loop(0, place[0], advance, jnp.zeros((4, ROWS), F32))

    state = state_ref[...]
    for half, ref in enumerate((first_ref, second_ref)):
        local = ref[0]
        masked = jnp.concatenate([local * mask_ref[:, k : k + 1] for k in range(4)], axis=1)
        spread = jnp.concatenate([onehot_ref[k : k + 1, :] * state for k in range(4)], axis=0)
        high = spread.astype(BF16)
        low = (spread - high.astype(F32)).astype(BF16)
        stacked = jnp.concatenate([high, high, low], axis=0)
        carried = lax.dot_general(
            stacked, gain_ref[...], (((0,), (0,)), ((), ())), preferred_element_type=F32
        )
        out_ref[:, half * CH : (half + 1) * CH] = (
            jnp.dot(masked, toeplitz_ref[...], preferred_element_type=F32) + carried
        )
        ends = lax.dot_general(
            final_ref[...], local, (((1,), (1,)), ((), ())), preferred_element_type=F32
        )
        entered = onehot_ref[0:1, :] * ends[0:4]
        for k in range(1, 4):
            entered = entered + onehot_ref[k : k + 1, :] * ends[k * 8 : k * 8 + 4]
        state = apply_power(one, state) + entered
    state_ref[...] = state


def filtered(place, first, second, slabs, mask, onehot, one, two, toeplitz, final, gain):
    def whole(a):
        return pl.BlockSpec(a.shape, lambda i, zs: (0,) * a.ndim)

    piece = pl.BlockSpec((1, ROWS, CH), lambda i, zs: (i, 0, 0))
    rest = (slabs, mask, onehot, one, two, toeplitz, final, gain)
    return pl.pallas_call(
        filter_kernel,
        grid_spec=pltpu.PrefetchScalarGridSpec(
            num_scalar_prefetch=1,
            grid=(NX,),
            in_specs=[piece, piece] + [whole(a) for a in rest],
            out_specs=pl.BlockSpec((ROWS, SLAB), lambda i, zs: (0, i)),
            scratch_shapes=[pltpu.VMEM((4, ROWS), F32)],
        ),
        out_shape=jax.ShapeDtypeStruct((ROWS, NX * SLAB), F32),
        compiler_params=pltpu.CompilerParams(vmem_limit_bytes=VMEM_LIMIT),
        cost_estimate=pl.CostEstimate(
            flops=8 * 2 * ROWS * CH * 1100, bytes_accessed=4 * 1024 * 1024, transcendentals=0
        ),
    )(place, first, second, *rest)


def ring(value, by):
    return lax.ppermute(value, "z", [(i, (i + by) % NZ) for i in range(NZ)])


def body(factor, white_noise, site_class, site_decay, site_angle, site_mix):
    x = lax.axis_index("x")
    z = lax.axis_index("z")
    tm = lax.axis_index("y") * NCORE + lax.axis_index("c")

    share = lax.dynamic_slice(factor, (tm * 32, 0), (32, factor.shape[1]))
    gathered = lax.all_gather(share, ("x", "y", "c"))
    gathered = gathered.reshape(NX, 8, 32, factor.shape[1])

    own = []
    for half in range(2):
        first = half * CH
        slabs = jnp.concatenate(
            [white_noise[:, s * SLAB + first : s * SLAB + first + CH] for s in range(NX)], axis=0
        )
        own.append(lax.all_to_all(slabs, "x", 0, 0, tiled=True))

    site_class, site_decay, site_angle, site_mix, own[1] = lax.optimization_barrier(
        (site_class, site_decay, site_angle, site_mix, own[1])
    )
    toeplitz, final, gain, power, power_two = tables(site_decay, site_angle, site_mix)
    by_block = site_class.reshape(NX, NZ, ROWS)
    ids = jnp.arange(4, dtype=jnp.int32)
    tile_class = lax.dynamic_slice(by_block, (0, z, 0), (NX, 1, ROWS)).reshape(1, NX * ROWS)
    tile_hot = (tile_class == ids[:, None]).astype(F32)
    own_class = lax.dynamic_slice(by_block, (x, z, 0), (1, 1, ROWS)).reshape(1, ROWS)
    own_hot = (own_class == ids[:, None]).astype(F32)
    own_mask = (own_class.reshape(ROWS, 1) == ids[None, :]).astype(BF16)

    excitation, ends = [], []
    for half in range(2):
        up1, down1 = ring(own[half], 1), ring(own[half], -1)
        up2, down2 = ring(up1, 1), ring(down1, -1)
        up3, down3 = ring(up2, 1), ring(down2, -1)
        total = product(None, gathered, [z, (z + 7) % 8, (z + 1) % 8], [own[half], up1, down1])
        up3, down3, total = lax.optimization_barrier((up3, down3, total))
        up4, down4 = ring(up3[:512], 1), ring(down3[512:], -1)
        total = product(total, gathered, [(z + 6) % 8, (z + 2) % 8], [up2, down2])
        total = product(total, gathered, [(z + 5) % 8, (z + 3) % 8], [up3, down3])
        local, end = product(total, gathered, [(z + 4) % 8], [up4, down4], (final, tile_hot))
        ends.append(end[:4])
        excitation.append(
            lax.all_to_all(local, "x", 0, 0, tiled=True).reshape(NX, ROWS, CH)
        )
    slab_end = apply_power(per_row(power, tile_hot), ends[0]) + ends[1]
    to_send = slab_end.reshape(4, NX, ROWS).transpose(1, 0, 2)
    to_send = jnp.tile(to_send, (NY * NCORE, 1, 1))
    own_ends = lax.all_to_all(to_send, ("y", "c", "x"), 0, 0, tiled=True)
    return filtered(
        jnp.reshape(tm * NX, (1,)).astype(jnp.int32),
        excitation[0], excitation[1], own_ends, own_mask, own_hot,
        per_row(power, own_hot), per_row(power_two, own_hot), toeplitz, final, gain,
    )


def solution(mesh):
    fine = Mesh(mesh.devices.reshape(NX, NZ, NY, NCORE), ("x", "z", "y", "c"))
    rows = ("x", "z")
    in_specs = (P(rows, None), P(rows, ("y", "c")), P(), P(), P(), P())
    return jax.shard_map(
        body, mesh=fine, in_specs=in_specs, out_specs=P(rows, ("y", "c")), check_vma=False
    )
```

```python
import functools

import jax
import jax.numpy as jnp
from jax import lax
from jax.experimental import pallas as pl
from jax.experimental.pallas import tpu as pltpu
from jax.sharding import Mesh, PartitionSpec as P

CH = 256
NX, NZ, NY, NCORE = 4, 8, 4, 2
ROWS = 256
SLAB = 512
VMEM_LIMIT = 58 * 1024 * 1024
F32 = jnp.float32
BF16 = jnp.bfloat16
PRECISE = lax.Precision.HIGHEST


def system(site_decay, site_angle, site_mix):
    radius = 1.0 - site_decay
    norm_gain = jnp.sqrt(site_decay * (2.0 - site_decay))
    cos_ground = radius[0] * jnp.cos(site_angle[0])
    sin_ground = radius[0] * jnp.sin(site_angle[0])
    cos_high = radius[1] * jnp.cos(site_angle[1])
    sin_high = radius[1] * jnp.sin(site_angle[1])
    zeros_row = jnp.zeros_like(cos_ground)
    ones_row = jnp.ones_like(cos_ground)
    mix_a, mix_b, out_a, out_b = (site_mix[0], site_mix[1], site_mix[2], site_mix[3])
    row_list = [
        [cos_ground, -sin_ground, zeros_row, zeros_row],
        [sin_ground, cos_ground, zeros_row, zeros_row],
        [
            norm_gain[0] * (mix_a * cos_ground + mix_b * sin_ground),
            norm_gain[0] * (mix_b * cos_ground - mix_a * sin_ground),
            cos_high,
            -sin_high,
        ],
        [zeros_row, zeros_row, sin_high, cos_high],
    ]
    matrix = jnp.stack([jnp.stack(entries, axis=-1) for entries in row_list], axis=1)
    entry_vec = jnp.stack([ones_row, zeros_row, norm_gain[0] * mix_a, zeros_row], axis=-1)
    readout = jnp.stack([zeros_row, zeros_row, norm_gain[1] * out_a, norm_gain[1] * out_b], axis=-1)
    return (matrix, entry_vec, readout)


def tables(site_decay, site_angle, site_mix):
    matrix, entry_vec, readout = system(site_decay, site_angle, site_mix)
    classes = matrix.shape[0]
    powers = matrix[None]
    while powers.shape[0] < CH:
        further = jnp.einsum("kab,jkbc->jkac", powers[-1], powers, precision=PRECISE)
        powers = jnp.concatenate([powers, further], axis=0)
    gains = jnp.einsum("ka,jkab->kbj", readout, powers, precision=PRECISE)
    responses = jnp.einsum("jkab,kb->kja", powers[: CH - 1], entry_vec, precision=PRECISE)
    responses = jnp.concatenate([entry_vec[:, None, :], responses], axis=1)
    impulse = jnp.einsum("ka,kma->km", readout, responses, precision=PRECISE)
    padded_len = 2 * CH
    padded = jnp.concatenate([impulse, jnp.zeros((classes, CH), F32)], axis=1)
    tiled = jnp.tile(padded, (1, CH))[:, : CH * (padded_len - 1)]
    toeplitz = tiled.reshape(classes, CH, padded_len - 1)[:, :, :CH]
    toeplitz = toeplitz.reshape(classes * CH, CH).astype(BF16)
    final = responses[:, ::-1, :].transpose(0, 2, 1).astype(BF16)
    final = jnp.concatenate([final, jnp.zeros_like(final)], axis=1).reshape(classes * 8, CH)
    gains = gains.reshape(classes * 4, CH)
    gains_hi = lax.reduce_precision(gains, 8, 7)
    gains_lo = (gains - gains_hi).astype(BF16)
    gains_hi = gains_hi.astype(BF16)
    gain_stack = jnp.concatenate([gains_hi, gains_lo, gains_hi], axis=0)
    power = powers[-1]
    power_two = jnp.einsum("kab,kbc->kac", power, power, precision=PRECISE)
    return toeplitz, final, gain_stack, power, power_two


def per_row(power, onehot):
    return jnp.sum(power.transpose(2, 1, 0)[:, :, :, None] * onehot[None, None], axis=2)


def apply_power(table, state):
    out = table[0] * state[0:1]
    for b in range(1, 4):
        out = out + table[b] * state[b : b + 1]
    return out


def load(zs, where, g_ref, noise_refs, held, noise, sems):
    waits = []
    for b, z in enumerate(where):
        copies = []
        for q in range(NX):
            columns = pl.ds(pl.multiple_of(q * NZ * CH + zs[z] * CH, CH), CH)
            copies.append(
                pltpu.make_async_copy(
                    g_ref.at[pl.ds(q, NX - q), :, columns], held[q].at[b], sems.at[b, q]
                )
            )
        first = 0
        for j, ref in enumerate(noise_refs[b]):
            rows = pl.ds(first, ref.shape[0])
            copies.append(pltpu.make_async_copy(ref, noise.at[b, rows], sems.at[b, NX + j]))
            first += ref.shape[0]
        for copy in copies:
            copy.start()
        waits.append(copies)
    return waits


def term(held, noise, b, s):
    parts = [held[q][b, s - q] for q in range(s + 1)]
    rows = jnp.concatenate(parts, axis=1) if s else parts[0]
    return jnp.dot(rows, noise[b, 0 : (s + 1) * ROWS, :], preferred_element_type=F32)


def product_kernel(blocks, zs, g_ref, *refs):
    noise_refs, (out_ref, *held, noise, sems) = refs[:blocks], refs[blocks:]
    waits = load(zs, range(blocks), g_ref, [[r] for r in noise_refs], held, noise, sems)
    for b in range(blocks):
        for copy in waits[b]:
            copy.wait()
        for s in range(NX):
            rows = pl.ds(s * ROWS, ROWS)
            value = term(held, noise, b, s)
            out_ref[rows, :] = value if b == 0 else out_ref[rows, :] + value


def scratch(blocks):
    return [pltpu.VMEM((blocks, NX - q, ROWS, CH), BF16) for q in range(NX)] + [
        pltpu.VMEM((blocks, NX * ROWS, CH), BF16),
        pltpu.SemaphoreType.DMA((blocks, NX + 2)),
    ]


def whole(a):
    return pl.BlockSpec(a.shape, lambda i, zs: (0,) * len(a.shape))


ANYWHERE = pl.BlockSpec(memory_space=pl.ANY)


def product(gathered, where_z, noise_blocks):
    blocks = len(where_z)
    out = jax.ShapeDtypeStruct((NX * ROWS, CH), F32)
    return pl.pallas_call(
        functools.partial(product_kernel, blocks),
        grid_spec=pltpu.PrefetchScalarGridSpec(
            num_scalar_prefetch=1,
            grid=(1,),
            in_specs=[ANYWHERE] * (1 + blocks),
            out_specs=whole(out),
            scratch_shapes=scratch(blocks),
        ),
        out_shape=out,
        compiler_params=pltpu.CompilerParams(vmem_limit_bytes=VMEM_LIMIT),
        cost_estimate=pl.CostEstimate(
            flops=blocks * 2 * 10 * ROWS * CH * CH,
            bytes_accessed=blocks * (1310720 + 524288) + 1048576,
            transcendentals=0,
        ),
    )(jnp.stack(where_z).astype(jnp.int32), gathered, *noise_blocks)


def last_kernel(second, zs, g_ref, up_ref, down_ref, acc_ref, final_ref, onehot_ref, *refs):
    refs = list(refs)
    if second:
        end_ref, power_ref = refs.pop(0), refs.pop(0)
        piece_refs, send_ref = refs[:NX], refs[NX]
        refs = refs[NX + 1 :]
        local = refs.pop(0)
    else:
        local, end_out = refs.pop(0), refs.pop(0)
    *held, noise, sems = refs
    waits = load(zs, range(1), g_ref, [[up_ref, down_ref]], held, noise, sems)
    for copy in waits[0]:
        copy.wait()
    for s in range(NX):
        rows = pl.ds(s * ROWS, ROWS)
        local[rows, :] = (acc_ref[rows, :] + term(held, noise, 0, s)).astype(BF16)
    ends = lax.dot_general(
        final_ref[...], local[...], (((1,), (1,)), ((), ())), preferred_element_type=F32
    )
    picked = onehot_ref[0:1, :] * ends[0:4]
    for k in range(1, 4):
        picked = picked + onehot_ref[k : k + 1, :] * ends[k * 8 : k * 8 + 4]
    if not second:
        end_out[...] = picked
        return
    for d in range(NX):
        to = pl.multiple_of(lax.rem(zs[1] + d, NX) * ROWS, ROWS)
        piece_refs[d][...] = local[pl.ds(to, ROWS), :]
    slab_end = apply_power([power_ref[b] for b in range(4)], end_ref[...]) + picked
    for t in range(NY * NCORE * NX):
        block = t % NX
        send_ref[t] = slab_end[:, block * ROWS : (block + 1) * ROWS]


def last_product(scalars, gathered, up, down, acc, final, onehot, earlier=None):
    second = earlier is not None
    args = [acc, final, onehot] + (list(earlier) if second else [])
    if second:
        out_shape = [jax.ShapeDtypeStruct((ROWS, CH), BF16)] * NX
        out_shape.append(jax.ShapeDtypeStruct((NY * NCORE * NX, 4, ROWS), F32))
        extra = [pltpu.VMEM((NX * ROWS, CH), BF16)]
    else:
        out_shape = [
            jax.ShapeDtypeStruct((NX * ROWS, CH), BF16),
            jax.ShapeDtypeStruct((4, NX * ROWS), F32),
        ]
        extra = []
    return pl.pallas_call(
        functools.partial(last_kernel, second),
        grid_spec=pltpu.PrefetchScalarGridSpec(
            num_scalar_prefetch=1,
            grid=(1,),
            in_specs=[ANYWHERE] * 3 + [whole(a) for a in args],
            out_specs=[whole(a) for a in out_shape],
            scratch_shapes=extra + scratch(1),
        ),
        out_shape=out_shape,
        compiler_params=pltpu.CompilerParams(vmem_limit_bytes=VMEM_LIMIT),
        cost_estimate=pl.CostEstimate(
            flops=2 * 11 * ROWS * CH * CH, bytes_accessed=4 * 1048576, transcendentals=0
        ),
    )(scalars, gathered, up, down, *args)


def filter_kernel(
    place, first_ref, own_ref, by_one_ref, by_two_ref, by_three_ref, slabs_ref, mask_ref, onehot_ref, one_ref, two_ref,
    toeplitz_ref, final_ref, gain_ref, out_ref, state_ref, second_ref,
):
    step = pl.program_id(0)
    one = [one_ref[b] for b in range(4)]

    @pl.when(step == 0)
    def _():
        for d, ref in enumerate((own_ref, by_one_ref, by_two_ref, by_three_ref)):
            second_ref[lax.rem(place[1] + NX - d, NX)] = ref[...]
        two = [two_ref[b] for b in range(4)]

        def advance(t, state):
            return apply_power(two, state) + slabs_ref[t]

        state_ref[...] = lax.fori_loop(0, place[0], advance, jnp.zeros((4, ROWS), F32))

    state = state_ref[...]
    for half in range(2):
        local = second_ref[step] if half else first_ref[0]
        masked = jnp.concatenate([local * mask_ref[:, k : k + 1] for k in range(4)], axis=1)
        spread = jnp.concatenate([onehot_ref[k : k + 1, :] * state for k in range(4)], axis=0)
        high = spread.astype(BF16)
        low = (spread - high.astype(F32)).astype(BF16)
        stacked = jnp.concatenate([high, high, low], axis=0)
        carried = lax.dot_general(
            stacked, gain_ref[...], (((0,), (0,)), ((), ())), preferred_element_type=F32
        )
        out_ref[:, half * CH : (half + 1) * CH] = (
            jnp.dot(masked, toeplitz_ref[...], preferred_element_type=F32) + carried
        )
        ends = lax.dot_general(
            final_ref[...], local, (((1,), (1,)), ((), ())), preferred_element_type=F32
        )
        entered = onehot_ref[0:1, :] * ends[0:4]
        for k in range(1, 4):
            entered = entered + onehot_ref[k : k + 1, :] * ends[k * 8 : k * 8 + 4]
        state = apply_power(one, state) + entered
    state_ref[...] = state


def filtered(place, first, second, slabs, mask, onehot, one, two, toeplitz, final, gain):
    piece = pl.BlockSpec((1, ROWS, CH), lambda i, zs: (i, 0, 0))
    rest = (*second, slabs, mask, onehot, one, two, toeplitz, final, gain)
    return pl.pallas_call(
        filter_kernel,
        grid_spec=pltpu.PrefetchScalarGridSpec(
            num_scalar_prefetch=1,
            grid=(NX,),
            in_specs=[piece] + [whole(a) for a in rest],
            out_specs=pl.BlockSpec((ROWS, SLAB), lambda i, zs: (0, i)),
            scratch_shapes=[pltpu.VMEM((4, ROWS), F32), pltpu.VMEM((NX, ROWS, CH), BF16)],
        ),
        out_shape=jax.ShapeDtypeStruct((ROWS, NX * SLAB), F32),
        compiler_params=pltpu.CompilerParams(vmem_limit_bytes=VMEM_LIMIT),
        cost_estimate=pl.CostEstimate(
            flops=8 * 2 * ROWS * CH * 1100, bytes_accessed=4 * 1024 * 1024, transcendentals=0
        ),
    )(place, first, *rest)


def ring(value, by):
    return lax.ppermute(value, "z", [(i, (i + by) % NZ) for i in range(NZ)])


def body(factor, white_noise, site_class, site_decay, site_angle, site_mix):
    x = lax.axis_index("x")
    z = lax.axis_index("z")
    tm = lax.axis_index("y") * NCORE + lax.axis_index("c")

    share = lax.dynamic_slice(factor, (tm * 32, 0), (32, factor.shape[1]))
    gathered = lax.all_gather(share, ("x", "y", "c"), tiled=True)
    gathered = gathered.reshape(NX, ROWS, factor.shape[1])

    steps = []
    for half in range(2):
        first = half * CH
        slabs = jnp.concatenate(
            [white_noise[:, s * SLAB + first : s * SLAB + first + CH] for s in range(NX)], axis=0
        )
        own = lax.all_to_all(slabs, "x", 0, 0, tiled=True)
        up1, down1 = ring(own, 1), ring(own, -1)
        if half == 0:
            site_class, site_decay, site_angle, site_mix, up1 = lax.optimization_barrier(
                (site_class, site_decay, site_angle, site_mix, up1)
            )
        up2, down2 = ring(up1, 1), ring(down1, -1)
        up3, down3 = ring(up2, 1), ring(down2, -1)
        up4, down4 = ring(up3[:512], 1), ring(down3[512:], -1)
        steps.append(((own, up1, down1, up2, down2, up3, down3), up4, down4))

    toeplitz, final, gain, power, power_two = tables(site_decay, site_angle, site_mix)
    by_block = site_class.reshape(NX, NZ, ROWS)
    ids = jnp.arange(4, dtype=jnp.int32)
    tile_class = lax.dynamic_slice(by_block, (0, z, 0), (NX, 1, ROWS)).reshape(1, NX * ROWS)
    tile_hot = (tile_class == ids[:, None]).astype(F32)
    own_class = lax.dynamic_slice(by_block, (x, z, 0), (1, 1, ROWS)).reshape(1, ROWS)
    own_hot = (own_class == ids[:, None]).astype(F32)
    own_mask = (own_class.reshape(ROWS, 1) == ids[None, :]).astype(BF16)

    where_z = [(z + by) % NZ for by in (0, 7, 1, 6, 2, 5, 3)]
    scalars = jnp.stack([(z + 4) % NZ, x]).astype(jnp.int32)
    total = product(gathered, where_z, steps[0][0])
    local, end = last_product(
        scalars, gathered, steps[0][1], steps[0][2], total, final, tile_hot
    )
    first_part = lax.all_to_all(local, "x", 0, 0, tiled=True).reshape(NX, ROWS, CH)
    total = product(gathered, where_z, steps[1][0])
    first_part, total = lax.optimization_barrier((first_part, total))
    *pieces, to_send = last_product(
        scalars, gathered, steps[1][1], steps[1][2], total, final, tile_hot,
        (end, per_row(power, tile_hot)),
    )
    second_part = [pieces[0]] + [
        lax.ppermute(pieces[d], "x", [(i, (i + d) % NX) for i in range(NX)]) for d in (1, 2, 3)
    ]
    own_ends = lax.all_to_all(to_send, ("y", "c", "x"), 0, 0, tiled=True)
    return filtered(
        jnp.stack([tm * NX, x]).astype(jnp.int32),
        first_part, second_part, own_ends, own_mask, own_hot,
        per_row(power, own_hot), per_row(power_two, own_hot), toeplitz, final, gain,
    )


def solution(mesh):
    fine = Mesh(mesh.devices.reshape(NX, NZ, NY, NCORE), ("x", "z", "y", "c"))
    rows = ("x", "z")
    in_specs = (P(rows, None), P(rows, ("y", "c")), P(), P(), P(), P())
    return jax.shard_map(
        body, mesh=fine, in_specs=in_specs, out_specs=P(rows, ("y", "c")), check_vma=False
    )
```

```python
import functools

import jax
import jax.numpy as jnp
from jax import lax
from jax.experimental import pallas as pl
from jax.experimental.pallas import tpu as pltpu
from jax.sharding import Mesh, PartitionSpec as P

CH = 256
NX, NZ, NY, NCORE = 4, 8, 4, 2
ROWS = 256
SLAB = 512
AWAY = (0, 7, 1, 6, 2, 5, 3)
VMEM_LIMIT = 58 * 1024 * 1024
F32 = jnp.float32
BF16 = jnp.bfloat16
PRECISE = lax.Precision.HIGHEST


def system(site_decay, site_angle, site_mix):
    radius = 1.0 - site_decay
    norm_gain = jnp.sqrt(site_decay * (2.0 - site_decay))
    cos_ground = radius[0] * jnp.cos(site_angle[0])
    sin_ground = radius[0] * jnp.sin(site_angle[0])
    cos_high = radius[1] * jnp.cos(site_angle[1])
    sin_high = radius[1] * jnp.sin(site_angle[1])
    zeros_row = jnp.zeros_like(cos_ground)
    ones_row = jnp.ones_like(cos_ground)
    mix_a, mix_b, out_a, out_b = (site_mix[0], site_mix[1], site_mix[2], site_mix[3])
    row_list = [
        [cos_ground, -sin_ground, zeros_row, zeros_row],
        [sin_ground, cos_ground, zeros_row, zeros_row],
        [
            norm_gain[0] * (mix_a * cos_ground + mix_b * sin_ground),
            norm_gain[0] * (mix_b * cos_ground - mix_a * sin_ground),
            cos_high,
            -sin_high,
        ],
        [zeros_row, zeros_row, sin_high, cos_high],
    ]
    matrix = jnp.stack([jnp.stack(entries, axis=-1) for entries in row_list], axis=1)
    entry_vec = jnp.stack([ones_row, zeros_row, norm_gain[0] * mix_a, zeros_row], axis=-1)
    readout = jnp.stack([zeros_row, zeros_row, norm_gain[1] * out_a, norm_gain[1] * out_b], axis=-1)
    return (matrix, entry_vec, readout)


def tables(site_decay, site_angle, site_mix):
    matrix, entry_vec, readout = system(site_decay, site_angle, site_mix)
    classes = matrix.shape[0]
    powers = matrix[None]
    while powers.shape[0] < CH:
        further = jnp.einsum("kab,jkbc->jkac", powers[-1], powers, precision=PRECISE)
        powers = jnp.concatenate([powers, further], axis=0)
    gains = jnp.einsum("ka,jkab->kbj", readout, powers, precision=PRECISE)
    responses = jnp.einsum("jkab,kb->kja", powers[: CH - 1], entry_vec, precision=PRECISE)
    responses = jnp.concatenate([entry_vec[:, None, :], responses], axis=1)
    impulse = jnp.einsum("ka,kma->km", readout, responses, precision=PRECISE)
    padded_len = 2 * CH
    padded = jnp.concatenate([impulse, jnp.zeros((classes, CH), F32)], axis=1)
    tiled = jnp.tile(padded, (1, CH))[:, : CH * (padded_len - 1)]
    toeplitz = tiled.reshape(classes, CH, padded_len - 1)[:, :, :CH]
    toeplitz = toeplitz.reshape(classes * CH, CH).astype(BF16)
    final = responses[:, ::-1, :].transpose(0, 2, 1).astype(BF16)
    final = jnp.concatenate([final, jnp.zeros_like(final)], axis=1).reshape(classes * 8, CH)
    gains = gains.reshape(classes * 4, CH)
    gains_hi = lax.reduce_precision(gains, 8, 7)
    gains_lo = (gains - gains_hi).astype(BF16)
    gains_hi = gains_hi.astype(BF16)
    gain_stack = jnp.concatenate([gains_hi, gains_lo, gains_hi], axis=0)
    power = powers[-1]
    twice = [power]
    for _ in range(3):
        twice.append(jnp.einsum("kab,kbc->kac", twice[-1], twice[-1], precision=PRECISE))
    return toeplitz, final, gain_stack, power, twice[1], twice[3]


def per_row(power, onehot):
    return jnp.sum(power.transpose(2, 1, 0)[:, :, :, None] * onehot[None, None], axis=2)


def apply_power(table, state):
    out = table[0] * state[0:1]
    for b in range(1, 4):
        out = out + table[b] * state[b : b + 1]
    return out


def load(zs, where, g_ref, noise, held, block, sems):
    waits = []
    for b, z in enumerate(where):
        copies = []
        for q in range(NX):
            columns = pl.ds(pl.multiple_of(q * NZ * CH + zs[z] * CH, CH), CH)
            copies.append(
                pltpu.make_async_copy(
                    g_ref.at[pl.ds(q, NX - q), :, columns], held[q].at[b], sems.at[b, q]
                )
            )
        for j, (ref, first, count, by, to, left) in enumerate(noise[b]):
            owner = lax.rem(zs[0] + NX - by, NX)
            refs = ref if isinstance(ref, tuple) else (ref,)
            pair = [
                pltpu.make_async_copy(
                    r.at[pl.ds(first, count)],
                    block.at[b, owner, pl.ds(to, count), pl.ds(left, r.shape[1])],
                    sems.at[b, NX + j],
                )
                for r in refs
            ]
            copies.append(pair if len(pair) == 2 else pair[0])
        for copy in copies:
            if isinstance(copy, list):
                pl.when(zs[1] == 0)(copy[0].start)
                pl.when(zs[1] == 1)(copy[1].start)
            else:
                copy.start()
        waits.append([c[0] if isinstance(c, list) else c for c in copies])
    return waits


def term(held, block, b, s):
    parts = [held[q][b, s - q] for q in range(s + 1)]
    rows = jnp.concatenate(parts, axis=1) if s else parts[0]
    noise = block[b, 0 : s + 1].reshape((s + 1) * ROWS, SLAB)
    return jnp.dot(rows, noise, preferred_element_type=F32)


def product_kernel(zs, g_ref, *refs):
    own_refs, rest_refs = refs[:NZ], refs[NZ : NZ + 14]
    out_ref, *held, block, sems = refs[NZ + 14 :]
    noise = []
    for b, by in enumerate(AWAY):
        own = (own_refs[(NZ - by) % NZ], own_refs[by]) if by else own_refs[0]
        parts = [(own, 0, ROWS, 0, 0, 0)]
        for half in range(2):
            parts += [
                (rest_refs[2 * b + half], (d - 1) * ROWS, ROWS, d, 0, half * CH) for d in (1, 2, 3)
            ]
        noise.append(parts)
    waits = load(zs, range(2, 9), g_ref, noise, held, block, sems)
    for b in range(len(AWAY)):
        for copy in waits[b]:
            copy.wait()
        for s in range(NX):
            rows = pl.ds(s * ROWS, ROWS)
            value = term(held, block, b, s)
            out_ref[rows, :] = value if b == 0 else out_ref[rows, :] + value


def scratch(blocks):
    return [pltpu.VMEM((blocks, NX - q, ROWS, CH), BF16) for q in range(NX)] + [
        pltpu.VMEM((blocks, NX, ROWS, SLAB), BF16),
        pltpu.SemaphoreType.DMA((blocks, NX + 9)),
    ]


def whole(a):
    return pl.BlockSpec(a.shape, lambda i, zs: (0,) * len(a.shape))


ANYWHERE = pl.BlockSpec(memory_space=pl.ANY)


def product(scalars, gathered, own_blocks, rest_blocks):
    out = jax.ShapeDtypeStruct((NX * ROWS, SLAB), F32)
    return pl.pallas_call(
        product_kernel,
        grid_spec=pltpu.PrefetchScalarGridSpec(
            num_scalar_prefetch=1,
            grid=(1,),
            in_specs=[ANYWHERE] * (1 + len(own_blocks) + len(rest_blocks)),
            out_specs=whole(out),
            scratch_shapes=scratch(len(AWAY)),
        ),
        out_shape=out,
        compiler_params=pltpu.CompilerParams(vmem_limit_bytes=VMEM_LIMIT),
        cost_estimate=pl.CostEstimate(
            flops=7 * 2 * 10 * ROWS * CH * SLAB, bytes_accessed=19 * 1048576, transcendentals=0
        ),
    )(scalars, gathered, *own_blocks, *rest_blocks)


def last_kernel(
    zs, g_ref, own_ref, up_one, down_one, up_two, down_two, acc_ref, final_ref, onehot_ref,
    power_ref, *refs,
):
    piece_refs, (send_ref, local, *held, block, sems) = refs[:NX], refs[NX:]
    noise = [(own_ref, 0, ROWS, 0, 0, 0)]
    for left, up, down in ((0, up_one, down_one), (CH, up_two, down_two)):
        noise += [
            (up, 0, 256, 1, 0, left),
            (up, 256, 128, 2, 0, left),
            (down, 0, 128, 2, 128, left),
            (down, 128, 256, 3, 0, left),
        ]
    (waits,) = load(zs, (9,), g_ref, [noise], held, block, sems)
    for copy in waits:
        copy.wait()
    for s in range(NX):
        rows = pl.ds(s * ROWS, ROWS)
        local[s] = (acc_ref[rows, :] + term(held, block, 0, s)).astype(BF16)
    for d in range(NX):
        piece_refs[d][...] = local[lax.rem(zs[0] + d, NX)]
    for s in range(NX):
        rows = slice(s * ROWS, (s + 1) * ROWS)
        end = None
        for half in range(2):
            ends = lax.dot_general(
                final_ref[...], local[s, :, half * CH : (half + 1) * CH],
                (((1,), (1,)), ((), ())), preferred_element_type=F32,
            )
            picked = onehot_ref[0:1, rows] * ends[0:4]
            for k in range(1, 4):
                picked = picked + onehot_ref[k : k + 1, rows] * ends[k * 8 : k * 8 + 4]
            end = (
                apply_power([power_ref[b, :, rows] for b in range(4)], end) + picked
                if half
                else picked
            )
        for t in range(s, NY * NCORE * NX, NX):
            send_ref[t] = end


def last_product(scalars, gathered, noise, *args):
    out_shape = [jax.ShapeDtypeStruct((ROWS, SLAB), BF16)] * NX
    out_shape.append(jax.ShapeDtypeStruct((NY * NCORE * NX, 4, ROWS), F32))
    return pl.pallas_call(
        last_kernel,
        grid_spec=pltpu.PrefetchScalarGridSpec(
            num_scalar_prefetch=1,
            grid=(1,),
            in_specs=[ANYWHERE] * 6 + [whole(a) for a in args],
            out_specs=[whole(a) for a in out_shape],
            scratch_shapes=[pltpu.VMEM((NX, ROWS, SLAB), BF16)] + scratch(1),
        ),
        out_shape=out_shape,
        compiler_params=pltpu.CompilerParams(vmem_limit_bytes=VMEM_LIMIT),
        cost_estimate=pl.CostEstimate(
            flops=2 * 11 * ROWS * CH * SLAB, bytes_accessed=6 * 1048576, transcendentals=0
        ),
    )(scalars, gathered, *noise, *args)


def filter_kernel(
    place, own_ref, by_one_ref, by_two_ref, by_three_ref, slabs_ref, mask_ref, onehot_ref,
    one_ref, two_ref, eight_ref, toeplitz_ref, final_ref, gain_ref, out_ref, state_ref, local_ref,
):
    step = pl.program_id(0)

    @pl.when(step == 0)
    def _():
        for d, ref in enumerate((own_ref, by_one_ref, by_two_ref, by_three_ref)):
            local_ref[lax.rem(place[1] + NX - d, NX)] = ref[...]
        slabs = slabs_ref[...].reshape(NY * NCORE, NX, 4, ROWS)
        ends = slabs[:, 0]
        for s in range(1, NX):
            moved = slabs[:, s]
            for b in range(4):
                moved = moved + two_ref[b][None] * ends[:, b : b + 1, :]
            ends = moved
        eight = [eight_ref[b] for b in range(4)]
        state = jnp.zeros((4, ROWS), F32)
        for t in range(NY * NCORE - 1):
            state = jnp.where(t < place[0], apply_power(eight, state) + ends[t], state)
        state_ref[...] = state

    one = [one_ref[b] for b in range(4)]
    state = state_ref[...]
    for half in range(2):
        local = local_ref[step, :, half * CH : (half + 1) * CH]
        masked = jnp.concatenate([local * mask_ref[:, k : k + 1] for k in range(4)], axis=1)
        spread = jnp.concatenate([onehot_ref[k : k + 1, :] * state for k in range(4)], axis=0)
        high = spread.astype(BF16)
        low = (spread - high.astype(F32)).astype(BF16)
        stacked = jnp.concatenate([high, high, low], axis=0)
        carried = lax.dot_general(
            stacked, gain_ref[...], (((0,), (0,)), ((), ())), preferred_element_type=F32
        )
        out_ref[:, half * CH : (half + 1) * CH] = (
            jnp.dot(masked, toeplitz_ref[...], preferred_element_type=F32) + carried
        )
        ends = lax.dot_general(
            final_ref[...], local, (((1,), (1,)), ((), ())), preferred_element_type=F32
        )
        entered = onehot_ref[0:1, :] * ends[0:4]
        for k in range(1, 4):
            entered = entered + onehot_ref[k : k + 1, :] * ends[k * 8 : k * 8 + 4]
        state = apply_power(one, state) + entered
    state_ref[...] = state


def filtered(place, *args):
    return pl.pallas_call(
        filter_kernel,
        grid_spec=pltpu.PrefetchScalarGridSpec(
            num_scalar_prefetch=1,
            grid=(NX,),
            in_specs=[whole(a) for a in args],
            out_specs=pl.BlockSpec((ROWS, SLAB), lambda i, zs: (0, i)),
            scratch_shapes=[pltpu.VMEM((4, ROWS), F32), pltpu.VMEM((NX, ROWS, SLAB), BF16)],
        ),
        out_shape=jax.ShapeDtypeStruct((ROWS, NX * SLAB), F32),
        compiler_params=pltpu.CompilerParams(vmem_limit_bytes=VMEM_LIMIT),
        cost_estimate=pl.CostEstimate(
            flops=8 * 2 * ROWS * CH * 1100, bytes_accessed=4 * 1024 * 1024, transcendentals=0
        ),
    )(place, *args)


def ring(value, by):
    return lax.ppermute(value, "z", [(i, (i + by) % NZ) for i in range(NZ)])


def ring_by_core(value):
    pairs = [
        (i * NCORE + c, (i + (1, -1)[c]) % NZ * NCORE + c) for i in range(NZ) for c in range(NCORE)
    ]
    return lax.ppermute(value, ("z", "c"), pairs)


def round_x(value, by):
    return lax.ppermute(value, "x", [(i, (i + by) % NX) for i in range(NX)])


def body(factor, white_noise, site_class, site_decay, site_angle, site_mix):
    x = lax.axis_index("x")
    z = lax.axis_index("z")
    tm = lax.axis_index("y") * NCORE + lax.axis_index("c")

    share = lax.dynamic_slice(factor, (tm * 32, 0), (32, factor.shape[1]))
    gathered = lax.all_gather(share, ("x", "y", "c"), tiled=True)
    gathered = gathered.reshape(NX, ROWS, factor.shape[1])

    def slab(owner):
        return lax.dynamic_slice(white_noise, (0, owner * SLAB), (ROWS, SLAB))

    own = [slab(x)]
    for _ in range(NZ - 1):
        own.append(ring_by_core(own[-1]))
    others = [round_x(slab((x + d) % NX), d) for d in (1, 2, 3)]
    rest, opposite = [], []
    for half in range(2):
        columns = slice(half * CH, (half + 1) * CH)
        start = jnp.concatenate([o[:, columns] for o in others], axis=0)
        up, down, blocks = start, start, [start]
        for step in range(3):
            up, down = ring(up, 1), ring(down, -1)
            if step == 0 and half == 0:
                site_class, site_decay, site_angle, site_mix, up, down = lax.optimization_barrier(
                    (site_class, site_decay, site_angle, site_mix, up, down)
                )
            blocks += [up, down]
        rest.append(blocks)
        opposite += [ring(up[:384], 1), ring(down[384:], -1)]

    toeplitz, final, gain, one, two, eight = tables(site_decay, site_angle, site_mix)
    by_block = site_class.reshape(NX, NZ, ROWS)
    ids = jnp.arange(4, dtype=jnp.int32)
    tile_class = lax.dynamic_slice(by_block, (0, z, 0), (NX, 1, ROWS)).reshape(1, NX * ROWS)
    tile_hot = (tile_class == ids[:, None]).astype(F32)
    own_class = lax.dynamic_slice(by_block, (x, z, 0), (1, 1, ROWS)).reshape(1, ROWS)
    own_hot = (own_class == ids[:, None]).astype(F32)
    own_mask = (own_class.reshape(ROWS, 1) == ids[None, :]).astype(BF16)

    scalars = jnp.stack([x, lax.axis_index("c")] + [(z + by) % NZ for by in AWAY + (4,)])
    scalars = scalars.astype(jnp.int32)
    total = product(scalars, gathered, own, [r for pair in zip(*rest) for r in pair])
    *pieces, to_send = last_product(
        scalars, gathered, [own[4]] + opposite, total, final, tile_hot, per_row(one, tile_hot)
    )
    excitation = [pieces[0]] + [round_x(pieces[d], d) for d in (1, 2, 3)]
    own_ends = lax.all_to_all(to_send, ("y", "c", "x"), 0, 0, tiled=True)
    return filtered(
        jnp.stack([tm, x]).astype(jnp.int32),
        *excitation, own_ends, own_mask, own_hot,
        per_row(one, own_hot), per_row(two, own_hot), per_row(eight, own_hot),
        toeplitz, final, gain,
    )


def solution(mesh):
    fine = Mesh(mesh.devices.reshape(NX, NZ, NY, NCORE), ("x", "z", "y", "c"))
    rows = ("x", "z")
    in_specs = (P(rows, None), P(rows, ("y", "c")), P(), P(), P(), P())
    return jax.shard_map(
        body, mesh=fine, in_specs=in_specs, out_specs=P(rows, ("y", "c")), check_vma=False
    )
```

```python
import functools

import jax
import jax.numpy as jnp
from jax import lax
from jax.experimental import pallas as pl
from jax.experimental.pallas import tpu as pltpu
from jax.sharding import Mesh, PartitionSpec as P

CH = 256
NX, NZ, NY, NCORE = 4, 8, 4, 2
ROWS = 256
SLAB = 512
AWAY = (0, 7, 1, 6, 2, 5, 3)
VMEM_LIMIT = 58 * 1024 * 1024
F32 = jnp.float32
BF16 = jnp.bfloat16
PRECISE = lax.Precision.HIGHEST


def system(site_decay, site_angle, site_mix):
    radius = 1.0 - site_decay
    norm_gain = jnp.sqrt(site_decay * (2.0 - site_decay))
    cos_ground = radius[0] * jnp.cos(site_angle[0])
    sin_ground = radius[0] * jnp.sin(site_angle[0])
    cos_high = radius[1] * jnp.cos(site_angle[1])
    sin_high = radius[1] * jnp.sin(site_angle[1])
    zeros_row = jnp.zeros_like(cos_ground)
    ones_row = jnp.ones_like(cos_ground)
    mix_a, mix_b, out_a, out_b = (site_mix[0], site_mix[1], site_mix[2], site_mix[3])
    row_list = [
        [cos_ground, -sin_ground, zeros_row, zeros_row],
        [sin_ground, cos_ground, zeros_row, zeros_row],
        [
            norm_gain[0] * (mix_a * cos_ground + mix_b * sin_ground),
            norm_gain[0] * (mix_b * cos_ground - mix_a * sin_ground),
            cos_high,
            -sin_high,
        ],
        [zeros_row, zeros_row, sin_high, cos_high],
    ]
    matrix = jnp.stack([jnp.stack(entries, axis=-1) for entries in row_list], axis=1)
    entry_vec = jnp.stack([ones_row, zeros_row, norm_gain[0] * mix_a, zeros_row], axis=-1)
    readout = jnp.stack([zeros_row, zeros_row, norm_gain[1] * out_a, norm_gain[1] * out_b], axis=-1)
    return (matrix, entry_vec, readout)


def tables(site_decay, site_angle, site_mix):
    matrix, entry_vec, readout = system(site_decay, site_angle, site_mix)
    classes = matrix.shape[0]
    powers = matrix[None]
    while powers.shape[0] < CH:
        further = jnp.einsum("kab,jkbc->jkac", powers[-1], powers, precision=PRECISE)
        powers = jnp.concatenate([powers, further], axis=0)
    gains = jnp.einsum("ka,jkab->kbj", readout, powers, precision=PRECISE)
    responses = jnp.einsum("jkab,kb->kja", powers[: CH - 1], entry_vec, precision=PRECISE)
    responses = jnp.concatenate([entry_vec[:, None, :], responses], axis=1)
    impulse = jnp.einsum("ka,kma->km", readout, responses, precision=PRECISE)
    padded_len = 2 * CH
    padded = jnp.concatenate([impulse, jnp.zeros((classes, CH), F32)], axis=1)
    tiled = jnp.tile(padded, (1, CH))[:, : CH * (padded_len - 1)]
    toeplitz = tiled.reshape(classes, CH, padded_len - 1)[:, :, :CH]
    toeplitz = toeplitz.reshape(classes * CH, CH).astype(BF16)
    final = responses[:, ::-1, :].transpose(0, 2, 1).astype(BF16)
    final = jnp.concatenate([final, jnp.zeros_like(final)], axis=1).reshape(classes * 8, CH)
    gains = gains.reshape(classes * 4, CH)
    gains_hi = lax.reduce_precision(gains, 8, 7)
    gains_lo = (gains - gains_hi).astype(BF16)
    gains_hi = gains_hi.astype(BF16)
    gain_stack = jnp.concatenate([gains_hi, gains_lo, gains_hi], axis=0)
    power = powers[-1]
    twice = [power]
    for _ in range(3):
        twice.append(jnp.einsum("kab,kbc->kac", twice[-1], twice[-1], precision=PRECISE))
    return toeplitz, final, gain_stack, power, twice[1], twice[3]


def per_row(power, onehot):
    return jnp.sum(power.transpose(2, 1, 0)[:, :, :, None] * onehot[None, None], axis=2)


def apply_power(table, state):
    out = table[0] * state[0:1]
    for b in range(1, 4):
        out = out + table[b] * state[b : b + 1]
    return out


def load(zs, where, g_ref, noise, held, block, sems):
    waits = []
    for b, z in enumerate(where):
        copies = []
        for q in range(NX):
            columns = pl.ds(pl.multiple_of(q * NZ * CH + zs[z] * CH, CH), CH)
            copies.append(
                pltpu.make_async_copy(
                    g_ref.at[pl.ds(q, NX - q), :, columns], held[q].at[b], sems.at[b, q]
                )
            )
        for j, (ref, first, count, by, to, left) in enumerate(noise[b]):
            owner = lax.rem(zs[0] + NX - by, NX)
            copies.append(
                pltpu.make_async_copy(
                    ref.at[pl.ds(first, count)],
                    block.at[b, owner, pl.ds(to, count), pl.ds(left, CH)],
                    sems.at[b, NX + j],
                )
            )
        for copy in copies:
            copy.start()
        waits.append(copies)
    return waits


def term(held, block, b, s):
    parts = [held[q][b, s - q] for q in range(s + 1)]
    rows = jnp.concatenate(parts, axis=1) if s else parts[0]
    noise = block[b, 0 : s + 1].reshape((s + 1) * ROWS, SLAB)
    return jnp.dot(rows, noise, preferred_element_type=F32)


def product_kernel(zs, g_ref, *refs):
    count = 2 * len(AWAY)
    noise_refs, (out_ref, *held, block, sems) = refs[:count], refs[count:]
    noise = [
        [
            (noise_refs[2 * b + half], d * ROWS, ROWS, d, 0, half * CH)
            for half in range(2)
            for d in range(NX)
        ]
        for b in range(len(AWAY))
    ]
    waits = load(zs, range(1, 8), g_ref, noise, held, block, sems)
    for b in range(len(AWAY)):
        for copy in waits[b]:
            copy.wait()
        for s in range(NX):
            rows = pl.ds(s * ROWS, ROWS)
            value = term(held, block, b, s)
            out_ref[rows, :] = value if b == 0 else out_ref[rows, :] + value


def scratch(blocks):
    return [pltpu.VMEM((blocks, NX - q, ROWS, CH), BF16) for q in range(NX)] + [
        pltpu.VMEM((blocks, NX, ROWS, SLAB), BF16),
        pltpu.SemaphoreType.DMA((blocks, 4 * NX)),
    ]


def whole(a):
    return pl.BlockSpec(a.shape, lambda i, zs: (0,) * len(a.shape))


ANYWHERE = pl.BlockSpec(memory_space=pl.ANY)


def product(scalars, gathered, noise_blocks):
    out = jax.ShapeDtypeStruct((NX * ROWS, SLAB), F32)
    return pl.pallas_call(
        product_kernel,
        grid_spec=pltpu.PrefetchScalarGridSpec(
            num_scalar_prefetch=1,
            grid=(1,),
            in_specs=[ANYWHERE] * (1 + len(noise_blocks)),
            out_specs=whole(out),
            scratch_shapes=scratch(len(AWAY)),
        ),
        out_shape=out,
        compiler_params=pltpu.CompilerParams(vmem_limit_bytes=VMEM_LIMIT),
        cost_estimate=pl.CostEstimate(
            flops=7 * 2 * 10 * ROWS * CH * SLAB, bytes_accessed=19 * 1048576, transcendentals=0
        ),
    )(scalars, gathered, *noise_blocks)


def last_kernel(
    zs, g_ref, up_one, down_one, up_two, down_two, total_ref, final_ref, onehot_ref,
    power_ref, *refs,
):
    piece_refs, (send_ref, local, acc_ref, *held, block, sems) = refs[:NX], refs[NX:]
    noise = []
    for left, up, down in ((0, up_one, down_one), (CH, up_two, down_two)):
        for d in range(NX):
            noise.append(((up, down)[d // 2], d % 2 * ROWS, ROWS, d, 0, left))
    (waits,) = load(zs, (8,), g_ref, [noise], held, block, sems)
    fetch = []
    for s in range(NX):
        rows = pl.ds(s * ROWS, ROWS)
        fetch.append(
            pltpu.make_async_copy(total_ref.at[rows], acc_ref.at[rows], sems.at[0, 3 * NX + s])
        )
        fetch[s].start()
    for copy in waits[NX:]:
        copy.wait()
    for s in range(NX):
        waits[s].wait()
        fetch[s].wait()
        rows = pl.ds(s * ROWS, ROWS)
        local[s] = (acc_ref[rows, :] + term(held, block, 0, s)).astype(BF16)
    for d in range(NX):
        piece_refs[d][...] = local[lax.rem(zs[0] + d, NX)]
    for s in range(NX):
        rows = slice(s * ROWS, (s + 1) * ROWS)
        end = None
        for half in range(2):
            ends = lax.dot_general(
                final_ref[...], local[s, :, half * CH : (half + 1) * CH],
                (((1,), (1,)), ((), ())), preferred_element_type=F32,
            )
            picked = onehot_ref[0:1, rows] * ends[0:4]
            for k in range(1, 4):
                picked = picked + onehot_ref[k : k + 1, rows] * ends[k * 8 : k * 8 + 4]
            end = (
                apply_power([power_ref[b, :, rows] for b in range(4)], end) + picked
                if half
                else picked
            )
        for t in range(s, NY * NCORE * NX, NX):
            send_ref[t] = end


def last_product(scalars, gathered, noise, total, *args):
    out_shape = [jax.ShapeDtypeStruct((ROWS, SLAB), BF16)] * NX
    out_shape.append(jax.ShapeDtypeStruct((NY * NCORE * NX, 4, ROWS), F32))
    return pl.pallas_call(
        last_kernel,
        grid_spec=pltpu.PrefetchScalarGridSpec(
            num_scalar_prefetch=1,
            grid=(1,),
            in_specs=[ANYWHERE] * 6 + [whole(a) for a in args],
            out_specs=[whole(a) for a in out_shape],
            scratch_shapes=[
                pltpu.VMEM((NX, ROWS, SLAB), BF16),
                pltpu.VMEM((NX * ROWS, SLAB), F32),
                *scratch(1),
            ],
        ),
        out_shape=out_shape,
        compiler_params=pltpu.CompilerParams(vmem_limit_bytes=VMEM_LIMIT),
        cost_estimate=pl.CostEstimate(
            flops=2 * 11 * ROWS * CH * SLAB, bytes_accessed=6 * 1048576, transcendentals=0
        ),
    )(scalars, gathered, *noise, total, *args)


def filter_kernel(
    place, own_ref, by_one_ref, by_two_ref, by_three_ref, slabs_ref, mask_ref, onehot_ref,
    one_ref, two_ref, eight_ref, toeplitz_ref, final_ref, gain_ref, out_ref, state_ref, local_ref, spread_ref,
):
    step = pl.program_id(0)

    @pl.when(step == 0)
    def _():
        for d, ref in enumerate((own_ref, by_one_ref, by_two_ref, by_three_ref)):
            local_ref[lax.rem(place[1] + NX - d, NX)] = ref[...]
        for k in range(4):
            spread_ref[k] = jnp.broadcast_to(mask_ref[:, k : k + 1], (ROWS, CH))
        slabs = slabs_ref[...].reshape(NY * NCORE, NX, 4, ROWS)
        ends = slabs[:, 0]
        for s in range(1, NX):
            moved = slabs[:, s]
            for b in range(4):
                moved = moved + two_ref[b][None] * ends[:, b : b + 1, :]
            ends = moved
        eight = [eight_ref[b] for b in range(4)]
        state = jnp.zeros((4, ROWS), F32)
        for t in range(NY * NCORE - 1):
            state = jnp.where(t < place[0], apply_power(eight, state) + ends[t], state)
        state_ref[...] = state

    one = [one_ref[b] for b in range(4)]
    state = state_ref[...]
    for half in range(2):
        local = local_ref[step, :, half * CH : (half + 1) * CH]
        masked = jnp.concatenate([local * spread_ref[k] for k in range(4)], axis=1)
        spread = jnp.concatenate([onehot_ref[k : k + 1, :] * state for k in range(4)], axis=0)
        high = spread.astype(BF16)
        low = (spread - high.astype(F32)).astype(BF16)
        stacked = jnp.concatenate([high, high, low], axis=0)
        carried = lax.dot_general(
            stacked, gain_ref[...], (((0,), (0,)), ((), ())), preferred_element_type=F32
        )
        out_ref[:, half * CH : (half + 1) * CH] = (
            jnp.dot(masked, toeplitz_ref[...], preferred_element_type=F32) + carried
        )
        ends = lax.dot_general(
            final_ref[...], local, (((1,), (1,)), ((), ())), preferred_element_type=F32
        )
        entered = onehot_ref[0:1, :] * ends[0:4]
        for k in range(1, 4):
            entered = entered + onehot_ref[k : k + 1, :] * ends[k * 8 : k * 8 + 4]
        state = apply_power(one, state) + entered
    state_ref[...] = state


def filtered(place, *args):
    return pl.pallas_call(
        filter_kernel,
        grid_spec=pltpu.PrefetchScalarGridSpec(
            num_scalar_prefetch=1,
            grid=(NX,),
            in_specs=[whole(a) for a in args],
            out_specs=pl.BlockSpec((ROWS, SLAB), lambda i, zs: (0, i)),
            scratch_shapes=[
                pltpu.VMEM((4, ROWS), F32),
                pltpu.VMEM((NX, ROWS, SLAB), BF16),
                pltpu.VMEM((4, ROWS, CH), BF16),
            ],
        ),
        out_shape=jax.ShapeDtypeStruct((ROWS, NX * SLAB), F32),
        compiler_params=pltpu.CompilerParams(vmem_limit_bytes=VMEM_LIMIT),
        cost_estimate=pl.CostEstimate(
            flops=8 * 2 * ROWS * CH * 1100, bytes_accessed=4 * 1024 * 1024, transcendentals=0
        ),
    )(place, *args)


def ring(value, by):
    return lax.ppermute(value, "z", [(i, (i + by) % NZ) for i in range(NZ)])


def round_x(value, by):
    return lax.ppermute(value, "x", [(i, (i + by) % NX) for i in range(NX)])


def body(factor, white_noise, site_class, site_decay, site_angle, site_mix):
    x = lax.axis_index("x")
    z = lax.axis_index("z")
    tm = lax.axis_index("y") * NCORE + lax.axis_index("c")

    share = lax.dynamic_slice(factor, (tm * 32, 0), (32, factor.shape[1]))
    gathered = lax.all_gather(share, ("x", "y", "c"), tiled=True)
    gathered = gathered.reshape(NX, ROWS, factor.shape[1])

    def cut(by, half):
        first = lax.rem(x + by, NX) * SLAB + half * CH
        return lax.dynamic_slice(white_noise, (0, first), (ROWS, CH))

    steps = []
    for half in range(2):
        start = jnp.concatenate(
            [cut(0, half)] + [round_x(cut(d, half), d) for d in (1, 2, 3)], axis=0
        )
        blocks = [start, ring(start, 1), ring(start, -1)]
        if half == 0:
            site_class, site_decay, site_angle, site_mix, *blocks[1:] = lax.optimization_barrier(
                (site_class, site_decay, site_angle, site_mix, *blocks[1:])
            )
        for _ in range(2):
            blocks += [ring(blocks[-2], 1), ring(blocks[-1], -1)]
        steps.append(blocks)

    toeplitz, final, gain, one, two, eight = tables(site_decay, site_angle, site_mix)
    by_block = site_class.reshape(NX, NZ, ROWS)
    ids = jnp.arange(4, dtype=jnp.int32)
    tile_class = lax.dynamic_slice(by_block, (0, z, 0), (NX, 1, ROWS)).reshape(1, NX * ROWS)
    tile_hot = (tile_class == ids[:, None]).astype(F32)
    own_class = lax.dynamic_slice(by_block, (x, z, 0), (1, 1, ROWS)).reshape(1, ROWS)
    own_hot = (own_class == ids[:, None]).astype(F32)
    own_mask = (own_class.reshape(ROWS, 1) == ids[None, :]).astype(BF16)
    scalars = jnp.stack([x] + [(z + by) % NZ for by in AWAY + (4,)]).astype(jnp.int32)
    place = jnp.stack([tm, x]).astype(jnp.int32)
    for_last = (final, tile_hot, per_row(one, tile_hot))
    for_filter = (
        own_mask, own_hot, per_row(one, own_hot), per_row(two, own_hot), per_row(eight, own_hot),
        toeplitz, final, gain,
    )
    scalars, place, for_last, for_filter, *steps[1][5:] = lax.optimization_barrier(
        (scalars, place, for_last, for_filter, *steps[1][5:])
    )
    opposite = []
    for blocks in steps:
        opposite += [ring(blocks[5][:512], 1), ring(blocks[6][512:], -1)]

    total = product(scalars, gathered, [n for pair in zip(*steps) for n in pair])
    *pieces, to_send = last_product(scalars, gathered, opposite, total, *for_last)
    excitation = [pieces[0]] + [round_x(pieces[d], d) for d in (1, 2, 3)]
    own_ends = lax.all_to_all(to_send, ("y", "c", "x"), 0, 0, tiled=True)
    return filtered(place, *excitation, own_ends, *for_filter)


def solution(mesh):
    fine = Mesh(mesh.devices.reshape(NX, NZ, NY, NCORE), ("x", "z", "y", "c"))
    rows = ("x", "z")
    in_specs = (P(rows, None), P(rows, ("y", "c")), P(), P(), P(), P())
    return jax.shard_map(
        body, mesh=fine, in_specs=in_specs, out_specs=P(rows, ("y", "c")), check_vma=False
    )
```

```python
import functools

import jax
import jax.numpy as jnp
from jax import lax
from jax.experimental import pallas as pl
from jax.experimental.pallas import tpu as pltpu
from jax.sharding import Mesh, PartitionSpec as P

CH = 256
NX, NZ, NY, NCORE = 4, 8, 4, 2
ROWS = 256
SLAB = 512
AWAY = (0, 7, 1, 6, 2, 5, 3)
AHEAD = 3
VMEM_LIMIT = 58 * 1024 * 1024
F32 = jnp.float32
BF16 = jnp.bfloat16
PRECISE = lax.Precision.HIGHEST


def system(site_decay, site_angle, site_mix):
    radius = 1.0 - site_decay
    norm_gain = jnp.sqrt(site_decay * (2.0 - site_decay))
    cos_ground = radius[0] * jnp.cos(site_angle[0])
    sin_ground = radius[0] * jnp.sin(site_angle[0])
    cos_high = radius[1] * jnp.cos(site_angle[1])
    sin_high = radius[1] * jnp.sin(site_angle[1])
    zeros_row = jnp.zeros_like(cos_ground)
    ones_row = jnp.ones_like(cos_ground)
    mix_a, mix_b, out_a, out_b = (site_mix[0], site_mix[1], site_mix[2], site_mix[3])
    row_list = [
        [cos_ground, -sin_ground, zeros_row, zeros_row],
        [sin_ground, cos_ground, zeros_row, zeros_row],
        [
            norm_gain[0] * (mix_a * cos_ground + mix_b * sin_ground),
            norm_gain[0] * (mix_b * cos_ground - mix_a * sin_ground),
            cos_high,
            -sin_high,
        ],
        [zeros_row, zeros_row, sin_high, cos_high],
    ]
    matrix = jnp.stack([jnp.stack(entries, axis=-1) for entries in row_list], axis=1)
    entry_vec = jnp.stack([ones_row, zeros_row, norm_gain[0] * mix_a, zeros_row], axis=-1)
    readout = jnp.stack([zeros_row, zeros_row, norm_gain[1] * out_a, norm_gain[1] * out_b], axis=-1)
    return (matrix, entry_vec, readout)


def tables(site_decay, site_angle, site_mix):
    matrix, entry_vec, readout = system(site_decay, site_angle, site_mix)
    classes = matrix.shape[0]
    powers = matrix[None]
    while powers.shape[0] < CH:
        further = jnp.einsum("kab,jkbc->jkac", powers[-1], powers, precision=PRECISE)
        powers = jnp.concatenate([powers, further], axis=0)
    gains = jnp.einsum("ka,jkab->kbj", readout, powers, precision=PRECISE)
    responses = jnp.einsum("jkab,kb->kja", powers[: CH - 1], entry_vec, precision=PRECISE)
    responses = jnp.concatenate([entry_vec[:, None, :], responses], axis=1)
    impulse = jnp.einsum("ka,kma->km", readout, responses, precision=PRECISE)
    padded_len = 2 * CH
    padded = jnp.concatenate([impulse, jnp.zeros((classes, CH), F32)], axis=1)
    tiled = jnp.tile(padded, (1, CH))[:, : CH * (padded_len - 1)]
    toeplitz = tiled.reshape(classes, CH, padded_len - 1)[:, :, :CH]
    toeplitz = toeplitz.reshape(classes * CH, CH).astype(BF16)
    final = responses[:, ::-1, :].transpose(0, 2, 1).astype(BF16)
    final = jnp.concatenate([final, jnp.zeros_like(final)], axis=1).reshape(classes * 8, CH)
    gains = gains.reshape(classes * 4, CH)
    gains_hi = lax.reduce_precision(gains, 8, 7)
    gains_lo = (gains - gains_hi).astype(BF16)
    gains_hi = gains_hi.astype(BF16)
    gain_stack = jnp.concatenate([gains_hi, gains_lo, gains_hi], axis=0)
    power = powers[-1]
    twice = [power]
    for _ in range(3):
        twice.append(jnp.einsum("kab,kbc->kac", twice[-1], twice[-1], precision=PRECISE))
    return toeplitz, final, gain_stack, power, twice[1], twice[3]


def per_row(power, onehot):
    return jnp.sum(power.transpose(2, 1, 0)[:, :, :, None] * onehot[None, None], axis=2)


def apply_power(table, state):
    out = table[0] * state[0:1]
    for b in range(1, 4):
        out = out + table[b] * state[b : b + 1]
    return out


def load(zs, where, g_ref, noise, held, block, sems):
    every = []
    for b, z in enumerate(where):
        copies = []
        for q in range(NX):
            columns = pl.ds(pl.multiple_of(q * NZ * CH + zs[z] * CH, CH), CH)
            copies.append(
                pltpu.make_async_copy(
                    g_ref.at[pl.ds(q, NX - q), :, columns], held[q].at[b], sems.at[b, q]
                )
            )
        for j, (ref, first, count, by, to, left) in enumerate(noise[b]):
            owner = lax.rem(zs[0] + NX - by, NX)
            copies.append(
                pltpu.make_async_copy(
                    ref.at[pl.ds(first, count)],
                    block.at[b, owner, pl.ds(to, count), pl.ds(left, CH)],
                    sems.at[b, NX + j],
                )
            )
        every.append(copies)
    return every


def term(held, block, b, s):
    parts = [held[q][b, s - q] for q in range(s + 1)]
    rows = jnp.concatenate(parts, axis=1) if s else parts[0]
    noise = block[b, 0 : s + 1].reshape((s + 1) * ROWS, SLAB)
    return jnp.dot(rows, noise, preferred_element_type=F32)


def product_kernel(zs, g_ref, *refs):
    count = 2 * len(AWAY)
    noise_refs, (out_ref, *held, block, sems) = refs[:count], refs[count:]
    noise = [
        [
            (noise_refs[2 * b + half], d * ROWS, ROWS, d, 0, half * CH)
            for half in range(2)
            for d in range(NX)
        ]
        for b in range(len(AWAY))
    ]
    copies = load(zs, range(1, 8), g_ref, noise, held, block, sems)
    for b in range(AHEAD):
        for copy in copies[b]:
            copy.start()
    for b in range(len(AWAY)):
        for copy in copies[b]:
            copy.wait()
        if b + AHEAD < len(AWAY):
            for copy in copies[b + AHEAD]:
                copy.start()
        for s in range(NX):
            rows = pl.ds(s * ROWS, ROWS)
            value = term(held, block, b, s)
            out_ref[rows, :] = value if b == 0 else out_ref[rows, :] + value


def scratch(blocks):
    return [pltpu.VMEM((blocks, NX - q, ROWS, CH), BF16) for q in range(NX)] + [
        pltpu.VMEM((blocks, NX, ROWS, SLAB), BF16),
        pltpu.SemaphoreType.DMA((blocks, 4 * NX)),
    ]


def whole(a):
    return pl.BlockSpec(a.shape, lambda i, zs: (0,) * len(a.shape))


ANYWHERE = pl.BlockSpec(memory_space=pl.ANY)


def product(scalars, gathered, noise_blocks):
    out = jax.ShapeDtypeStruct((NX * ROWS, SLAB), F32)
    return pl.pallas_call(
        product_kernel,
        grid_spec=pltpu.PrefetchScalarGridSpec(
            num_scalar_prefetch=1,
            grid=(1,),
            in_specs=[ANYWHERE] * (1 + len(noise_blocks)),
            out_specs=whole(out),
            scratch_shapes=scratch(len(AWAY)),
        ),
        out_shape=out,
        compiler_params=pltpu.CompilerParams(vmem_limit_bytes=VMEM_LIMIT),
        cost_estimate=pl.CostEstimate(
            flops=7 * 2 * 10 * ROWS * CH * SLAB, bytes_accessed=19 * 1048576, transcendentals=0
        ),
    )(scalars, gathered, *noise_blocks)


def last_kernel(
    zs, g_ref, up_one, down_one, up_two, down_two, total_ref, final_ref, onehot_ref,
    power_ref, *refs,
):
    piece_refs, (send_ref, local, acc_ref, *held, block, sems) = refs[:NX], refs[NX:]
    noise = []
    for left, up, down in ((0, up_one, down_one), (CH, up_two, down_two)):
        for d in range(NX):
            noise.append(((up, down)[d // 2], d % 2 * ROWS, ROWS, d, 0, left))
    (waits,) = load(zs, (8,), g_ref, [noise], held, block, sems)
    for copy in waits[NX:] + waits[:NX]:
        copy.start()
    fetch = []
    for s in range(NX):
        rows = pl.ds(s * ROWS, ROWS)
        fetch.append(
            pltpu.make_async_copy(total_ref.at[rows], acc_ref.at[rows], sems.at[0, 3 * NX + s])
        )
        fetch[s].start()
    for copy in waits[NX:]:
        copy.wait()
    for s in range(NX):
        waits[s].wait()
        fetch[s].wait()
        rows = pl.ds(s * ROWS, ROWS)
        local[s] = (acc_ref[rows, :] + term(held, block, 0, s)).astype(BF16)
    for d in range(NX):
        piece_refs[d][...] = local[lax.rem(zs[0] + d, NX)]
    for s in range(NX):
        rows = slice(s * ROWS, (s + 1) * ROWS)
        end = None
        for half in range(2):
            ends = lax.dot_general(
                final_ref[...], local[s, :, half * CH : (half + 1) * CH],
                (((1,), (1,)), ((), ())), preferred_element_type=F32,
            )
            picked = onehot_ref[0:1, rows] * ends[0:4]
            for k in range(1, 4):
                picked = picked + onehot_ref[k : k + 1, rows] * ends[k * 8 : k * 8 + 4]
            end = (
                apply_power([power_ref[b, :, rows] for b in range(4)], end) + picked
                if half
                else picked
            )
        for t in range(s, NY * NCORE * NX, NX):
            send_ref[t] = end


def last_product(scalars, gathered, noise, total, *args):
    out_shape = [jax.ShapeDtypeStruct((ROWS, SLAB), BF16)] * NX
    out_shape.append(jax.ShapeDtypeStruct((NY * NCORE * NX, 4, ROWS), F32))
    return pl.pallas_call(
        last_kernel,
        grid_spec=pltpu.PrefetchScalarGridSpec(
            num_scalar_prefetch=1,
            grid=(1,),
            in_specs=[ANYWHERE] * 6 + [whole(a) for a in args],
            out_specs=[whole(a) for a in out_shape],
            scratch_shapes=[
                pltpu.VMEM((NX, ROWS, SLAB), BF16),
                pltpu.VMEM((NX * ROWS, SLAB), F32),
                *scratch(1),
            ],
        ),
        out_shape=out_shape,
        compiler_params=pltpu.CompilerParams(vmem_limit_bytes=VMEM_LIMIT),
        cost_estimate=pl.CostEstimate(
            flops=2 * 11 * ROWS * CH * SLAB, bytes_accessed=6 * 1048576, transcendentals=0
        ),
    )(scalars, gathered, *noise, total, *args)


def filter_kernel(
    place, own_ref, by_one_ref, by_two_ref, by_three_ref, slabs_ref, mask_ref, onehot_ref,
    one_ref, two_ref, eight_ref, toeplitz_ref, final_ref, gain_ref, out_ref, state_ref, local_ref, spread_ref,
):
    step = pl.program_id(0)

    @pl.when(step == 0)
    def _():
        for d, ref in enumerate((own_ref, by_one_ref, by_two_ref, by_three_ref)):
            local_ref[lax.rem(place[1] + NX - d, NX)] = ref[...]
        for k in range(4):
            spread_ref[k] = jnp.broadcast_to(mask_ref[:, k : k + 1], (ROWS, CH))
        slabs = slabs_ref[...].reshape(NY * NCORE, NX, 4, ROWS)
        ends = slabs[:, 0]
        for s in range(1, NX):
            moved = slabs[:, s]
            for b in range(4):
                moved = moved + two_ref[b][None] * ends[:, b : b + 1, :]
            ends = moved
        eight = [eight_ref[b] for b in range(4)]
        state = jnp.zeros((4, ROWS), F32)
        for t in range(NY * NCORE - 1):
            state = jnp.where(t < place[0], apply_power(eight, state) + ends[t], state)
        state_ref[...] = state

    one = [one_ref[b] for b in range(4)]
    state = state_ref[...]
    for half in range(2):
        local = local_ref[step, :, half * CH : (half + 1) * CH]
        masked = jnp.concatenate([local * spread_ref[k] for k in range(4)], axis=1)
        spread = jnp.concatenate([onehot_ref[k : k + 1, :] * state for k in range(4)], axis=0)
        high = spread.astype(BF16)
        low = (spread - high.astype(F32)).astype(BF16)
        stacked = jnp.concatenate([high, high, low], axis=0)
        carried = lax.dot_general(
            stacked, gain_ref[...], (((0,), (0,)), ((), ())), preferred_element_type=F32
        )
        out_ref[:, half * CH : (half + 1) * CH] = (
            jnp.dot(masked, toeplitz_ref[...], preferred_element_type=F32) + carried
        )
        ends = lax.dot_general(
            final_ref[...], local, (((1,), (1,)), ((), ())), preferred_element_type=F32
        )
        entered = onehot_ref[0:1, :] * ends[0:4]
        for k in range(1, 4):
            entered = entered + onehot_ref[k : k + 1, :] * ends[k * 8 : k * 8 + 4]
        state = apply_power(one, state) + entered
    state_ref[...] = state


def filtered(place, *args):
    return pl.pallas_call(
        filter_kernel,
        grid_spec=pltpu.PrefetchScalarGridSpec(
            num_scalar_prefetch=1,
            grid=(NX,),
            in_specs=[whole(a) for a in args],
            out_specs=pl.BlockSpec((ROWS, SLAB), lambda i, zs: (0, i)),
            scratch_shapes=[
                pltpu.VMEM((4, ROWS), F32),
                pltpu.VMEM((NX, ROWS, SLAB), BF16),
                pltpu.VMEM((4, ROWS, CH), BF16),
            ],
        ),
        out_shape=jax.ShapeDtypeStruct((ROWS, NX * SLAB), F32),
        compiler_params=pltpu.CompilerParams(vmem_limit_bytes=VMEM_LIMIT),
        cost_estimate=pl.CostEstimate(
            flops=8 * 2 * ROWS * CH * 1100, bytes_accessed=4 * 1024 * 1024, transcendentals=0
        ),
    )(place, *args)


def ring(value, by):
    return lax.ppermute(value, "z", [(i, (i + by) % NZ) for i in range(NZ)])


def round_x(value, by):
    return lax.ppermute(value, "x", [(i, (i + by) % NX) for i in range(NX)])


def together(*lists):
    return lax.optimization_barrier(lists)


def body(factor, white_noise, site_class, site_decay, site_angle, site_mix):
    x = lax.axis_index("x")
    z = lax.axis_index("z")
    tm = lax.axis_index("y") * NCORE + lax.axis_index("c")

    share = lax.dynamic_slice(factor, (tm * 32, 0), (32, factor.shape[1]))
    gathered = lax.all_gather(share, ("x", "y", "c"), tiled=True)
    gathered = gathered.reshape(NX, ROWS, factor.shape[1])

    def cut(by, half):
        first = lax.rem(x + by, NX) * SLAB + half * CH
        return lax.dynamic_slice(white_noise, (0, first), (ROWS, CH))

    steps = []
    for half in range(2):
        start = jnp.concatenate(
            [cut(0, half)] + [round_x(cut(d, half), d) for d in (1, 2, 3)], axis=0
        )
        steps.append([start, ring(start, 1), ring(start, -1)])
    first, second = steps
    site_class, site_decay, site_angle, site_mix, *first[1:] = lax.optimization_barrier(
        (site_class, site_decay, site_angle, site_mix, *first[1:])
    )
    for _ in range(2):
        first += [ring(first[-2], 1), ring(first[-1], -1)]
        second[-2:], first[-4:-2] = together(second[-2:], first[-4:-2])
        second += [ring(second[-2], 1), ring(second[-1], -1)]
        first[-2:], second[-4:-2] = together(first[-2:], second[-4:-2])

    toeplitz, final, gain, one, two, eight = tables(site_decay, site_angle, site_mix)
    by_block = site_class.reshape(NX, NZ, ROWS)
    ids = jnp.arange(4, dtype=jnp.int32)
    tile_class = lax.dynamic_slice(by_block, (0, z, 0), (NX, 1, ROWS)).reshape(1, NX * ROWS)
    tile_hot = (tile_class == ids[:, None]).astype(F32)
    own_class = lax.dynamic_slice(by_block, (x, z, 0), (1, 1, ROWS)).reshape(1, ROWS)
    own_hot = (own_class == ids[:, None]).astype(F32)
    own_mask = (own_class.reshape(ROWS, 1) == ids[None, :]).astype(BF16)
    scalars = jnp.stack([x] + [(z + by) % NZ for by in AWAY + (4,)]).astype(jnp.int32)
    place = jnp.stack([tm, x]).astype(jnp.int32)
    for_last = (final, tile_hot, per_row(one, tile_hot))
    for_filter = (
        own_mask, own_hot, per_row(one, own_hot), per_row(two, own_hot), per_row(eight, own_hot),
        toeplitz, final, gain,
    )
    scalars, place, for_last, for_filter, *first[5:] = lax.optimization_barrier(
        (scalars, place, for_last, for_filter, *first[5:])
    )
    second[5:], _ = together(second[5:], first[5:])
    opposite = []
    for blocks in steps:
        opposite += [ring(blocks[5][:512], 1), ring(blocks[6][512:], -1)]

    total = product(scalars, gathered, [n for pair in zip(*steps) for n in pair])
    *pieces, to_send = last_product(scalars, gathered, opposite, total, *for_last)
    excitation = [pieces[0]] + [round_x(pieces[d], d) for d in (1, 2, 3)]
    own_ends = lax.all_to_all(to_send, ("y", "c", "x"), 0, 0, tiled=True)
    return filtered(place, *excitation, own_ends, *for_filter)


def solution(mesh):
    fine = Mesh(mesh.devices.reshape(NX, NZ, NY, NCORE), ("x", "z", "y", "c"))
    rows = ("x", "z")
    in_specs = (P(rows, None), P(rows, ("y", "c")), P(), P(), P(), P())
    return jax.shard_map(
        body, mesh=fine, in_specs=in_specs, out_specs=P(rows, ("y", "c")), check_vma=False
    )
```

```python
import functools

import jax
import jax.numpy as jnp
from jax import lax
from jax.experimental import pallas as pl
from jax.experimental.pallas import tpu as pltpu
from jax.sharding import Mesh, PartitionSpec as P

CH = 256
NX, NZ, NY, NCORE = 4, 8, 4, 2
ROWS = 256
SLAB = 512
AWAY = (0, 7, 1, 6, 2, 5, 3)
AHEAD = 3
VMEM_LIMIT = 58 * 1024 * 1024
F32 = jnp.float32
BF16 = jnp.bfloat16
PRECISE = lax.Precision.HIGHEST


def system(site_decay, site_angle, site_mix):
    radius = 1.0 - site_decay
    norm_gain = jnp.sqrt(site_decay * (2.0 - site_decay))
    cos_ground = radius[0] * jnp.cos(site_angle[0])
    sin_ground = radius[0] * jnp.sin(site_angle[0])
    cos_high = radius[1] * jnp.cos(site_angle[1])
    sin_high = radius[1] * jnp.sin(site_angle[1])
    zeros_row = jnp.zeros_like(cos_ground)
    ones_row = jnp.ones_like(cos_ground)
    mix_a, mix_b, out_a, out_b = (site_mix[0], site_mix[1], site_mix[2], site_mix[3])
    row_list = [
        [cos_ground, -sin_ground, zeros_row, zeros_row],
        [sin_ground, cos_ground, zeros_row, zeros_row],
        [
            norm_gain[0] * (mix_a * cos_ground + mix_b * sin_ground),
            norm_gain[0] * (mix_b * cos_ground - mix_a * sin_ground),
            cos_high,
            -sin_high,
        ],
        [zeros_row, zeros_row, sin_high, cos_high],
    ]
    matrix = jnp.stack([jnp.stack(entries, axis=-1) for entries in row_list], axis=1)
    entry_vec = jnp.stack([ones_row, zeros_row, norm_gain[0] * mix_a, zeros_row], axis=-1)
    readout = jnp.stack([zeros_row, zeros_row, norm_gain[1] * out_a, norm_gain[1] * out_b], axis=-1)
    return (matrix, entry_vec, readout)


def tables(site_decay, site_angle, site_mix):
    matrix, entry_vec, readout = system(site_decay, site_angle, site_mix)
    classes = matrix.shape[0]
    powers = matrix[None]
    while powers.shape[0] < CH:
        further = jnp.einsum("kab,jkbc->jkac", powers[-1], powers, precision=PRECISE)
        powers = jnp.concatenate([powers, further], axis=0)
    gains = jnp.einsum("ka,jkab->kbj", readout, powers, precision=PRECISE)
    responses = jnp.einsum("jkab,kb->kja", powers[: CH - 1], entry_vec, precision=PRECISE)
    responses = jnp.concatenate([entry_vec[:, None, :], responses], axis=1)
    impulse = jnp.einsum("ka,kma->km", readout, responses, precision=PRECISE)
    padded_len = 2 * CH
    padded = jnp.concatenate([impulse, jnp.zeros((classes, CH), F32)], axis=1)
    tiled = jnp.tile(padded, (1, CH))[:, : CH * (padded_len - 1)]
    toeplitz = tiled.reshape(classes, CH, padded_len - 1)[:, :, :CH]
    toeplitz = toeplitz.reshape(classes * CH, CH).astype(BF16)
    final = responses[:, ::-1, :].transpose(0, 2, 1).astype(BF16)
    final = jnp.concatenate([final, jnp.zeros_like(final)], axis=1).reshape(classes * 8, CH)
    gains = gains.reshape(classes * 4, CH)
    gains_hi = lax.reduce_precision(gains, 8, 7)
    gains_lo = (gains - gains_hi).astype(BF16)
    gains_hi = gains_hi.astype(BF16)
    gain_stack = jnp.concatenate([gains_hi, gains_lo, gains_hi], axis=0)
    power = powers[-1]
    twice = [power]
    for _ in range(3):
        twice.append(jnp.einsum("kab,kbc->kac", twice[-1], twice[-1], precision=PRECISE))
    return toeplitz, final, gain_stack, power, twice[1], twice[3]


def per_row(power, onehot):
    return jnp.sum(power.transpose(2, 1, 0)[:, :, :, None] * onehot[None, None], axis=2)


def apply_power(table, state):
    out = table[0] * state[0:1]
    for b in range(1, 4):
        out = out + table[b] * state[b : b + 1]
    return out


def load(zs, where, g_ref, noise, held, block, sems):
    every = []
    for b, z in enumerate(where):
        copies = []
        for q in range(NX):
            copies.append(
                pltpu.make_async_copy(
                    g_ref.at[pl.ds(8 * q, 8 * (NX - q)), q * NZ + zs[z]],
                    held[q].at[b],
                    sems.at[b, q],
                )
            )
        for j, (ref, first, count, by, to, left) in enumerate(noise[b]):
            owner = lax.rem(zs[0] + NX - by, NX)
            copies.append(
                pltpu.make_async_copy(
                    ref.at[pl.ds(first, count)],
                    block.at[b, owner, pl.ds(to, count), pl.ds(left, CH)],
                    sems.at[b, NX + j],
                )
            )
        every.append(copies)
    return every


def term(held, block, b, s):
    parts = [
        held[q][b, 8 * (s - q) : 8 * (s - q + 1)].reshape(ROWS, CH) for q in range(s + 1)
    ]
    rows = jnp.concatenate(parts, axis=1) if s else parts[0]
    noise = block[b, 0 : s + 1].reshape((s + 1) * ROWS, SLAB)
    return jnp.dot(rows, noise, preferred_element_type=F32)


def product_kernel(zs, g_ref, *refs):
    count = 2 * len(AWAY)
    noise_refs, (out_ref, *held, block, sems) = refs[:count], refs[count:]
    noise = [
        [
            (noise_refs[2 * b + half], d * ROWS, ROWS, d, 0, half * CH)
            for half in range(2)
            for d in range(NX)
        ]
        for b in range(len(AWAY))
    ]
    copies = load(zs, range(1, 8), g_ref, noise, held, block, sems)
    for b in range(AHEAD):
        for copy in copies[b]:
            copy.start()
    for b in range(len(AWAY)):
        for copy in copies[b]:
            copy.wait()
        if b + AHEAD < len(AWAY):
            for copy in copies[b + AHEAD]:
                copy.start()
        for s in range(NX):
            rows = pl.ds(s * ROWS, ROWS)
            value = term(held, block, b, s)
            out_ref[rows, :] = value if b == 0 else out_ref[rows, :] + value


def scratch(blocks):
    return [pltpu.VMEM((blocks, 8 * (NX - q), 32, CH), BF16) for q in range(NX)] + [
        pltpu.VMEM((blocks, NX, ROWS, SLAB), BF16),
        pltpu.SemaphoreType.DMA((blocks, 4 * NX)),
    ]


def whole(a):
    return pl.BlockSpec(a.shape, lambda i, zs: (0,) * len(a.shape))


ANYWHERE = pl.BlockSpec(memory_space=pl.ANY)


def product(scalars, gathered, noise_blocks):
    out = jax.ShapeDtypeStruct((NX * ROWS, SLAB), F32)
    return pl.pallas_call(
        product_kernel,
        grid_spec=pltpu.PrefetchScalarGridSpec(
            num_scalar_prefetch=1,
            grid=(1,),
            in_specs=[ANYWHERE] * (1 + len(noise_blocks)),
            out_specs=whole(out),
            scratch_shapes=scratch(len(AWAY)),
        ),
        out_shape=out,
        compiler_params=pltpu.CompilerParams(vmem_limit_bytes=VMEM_LIMIT),
        cost_estimate=pl.CostEstimate(
            flops=7 * 2 * 10 * ROWS * CH * SLAB, bytes_accessed=19 * 1048576, transcendentals=0
        ),
    )(scalars, gathered, *noise_blocks)


def last_kernel(
    zs, g_ref, first_ref, second_ref, total_ref, final_ref, onehot_ref,
    power_ref, *refs,
):
    piece_refs, (send_ref, local, acc_ref, *held, block, sems) = refs[:NX], refs[NX:]
    noise = [
        (ref, d * ROWS, ROWS, d, 0, left)
        for left, ref in ((0, first_ref), (CH, second_ref))
        for d in range(NX)
    ]
    (waits,) = load(zs, (8,), g_ref, [noise], held, block, sems)
    for copy in waits[NX:] + waits[:NX]:
        copy.start()
    fetch = []
    for s in range(NX):
        rows = pl.ds(s * ROWS, ROWS)
        fetch.append(
            pltpu.make_async_copy(total_ref.at[rows], acc_ref.at[rows], sems.at[0, 3 * NX + s])
        )
        fetch[s].start()
    for copy in waits[NX:]:
        copy.wait()
    for s in range(NX):
        waits[s].wait()
        fetch[s].wait()
        rows = pl.ds(s * ROWS, ROWS)
        local[s] = (acc_ref[rows, :] + term(held, block, 0, s)).astype(BF16)
    for d in range(NX):
        piece_refs[d][...] = local[lax.rem(zs[0] + d, NX)]
    for s in range(NX):
        rows = slice(s * ROWS, (s + 1) * ROWS)
        end = None
        for half in range(2):
            ends = lax.dot_general(
                final_ref[...], local[s, :, half * CH : (half + 1) * CH],
                (((1,), (1,)), ((), ())), preferred_element_type=F32,
            )
            picked = onehot_ref[0:1, rows] * ends[0:4]
            for k in range(1, 4):
                picked = picked + onehot_ref[k : k + 1, rows] * ends[k * 8 : k * 8 + 4]
            end = (
                apply_power([power_ref[b, :, rows] for b in range(4)], end) + picked
                if half
                else picked
            )
        for t in range(s, NY * NCORE * NX, NX):
            send_ref[t] = end


def last_product(scalars, gathered, noise, total, *args):
    out_shape = [jax.ShapeDtypeStruct((ROWS, SLAB), BF16)] * NX
    out_shape.append(jax.ShapeDtypeStruct((NY * NCORE * NX, 4, ROWS), F32))
    return pl.pallas_call(
        last_kernel,
        grid_spec=pltpu.PrefetchScalarGridSpec(
            num_scalar_prefetch=1,
            grid=(1,),
            in_specs=[ANYWHERE] * 4 + [whole(a) for a in args],
            out_specs=[whole(a) for a in out_shape],
            scratch_shapes=[
                pltpu.VMEM((NX, ROWS, SLAB), BF16),
                pltpu.VMEM((NX * ROWS, SLAB), F32),
                *scratch(1),
            ],
        ),
        out_shape=out_shape,
        compiler_params=pltpu.CompilerParams(vmem_limit_bytes=VMEM_LIMIT),
        cost_estimate=pl.CostEstimate(
            flops=2 * 11 * ROWS * CH * SLAB, bytes_accessed=6 * 1048576, transcendentals=0
        ),
    )(scalars, gathered, *noise, total, *args)


def filter_kernel(
    place, own_ref, by_one_ref, by_two_ref, by_three_ref, slabs_ref, mask_ref, onehot_ref,
    one_ref, two_ref, eight_ref, toeplitz_ref, final_ref, gain_ref, out_ref, state_ref, local_ref, spread_ref,
):
    step = pl.program_id(0)

    @pl.when(step == 0)
    def _():
        for d, ref in enumerate((own_ref, by_one_ref, by_two_ref, by_three_ref)):
            local_ref[lax.rem(place[1] + NX - d, NX)] = ref[...]
        for k in range(4):
            spread_ref[k] = jnp.broadcast_to(mask_ref[:, k : k + 1], (ROWS, CH))
        slabs = slabs_ref[...].reshape(NY * NCORE, NX, 4, ROWS)
        ends = slabs[:, 0]
        for s in range(1, NX):
            moved = slabs[:, s]
            for b in range(4):
                moved = moved + two_ref[b][None] * ends[:, b : b + 1, :]
            ends = moved
        eight = [eight_ref[b] for b in range(4)]
        state = jnp.zeros((4, ROWS), F32)
        for t in range(NY * NCORE - 1):
            state = jnp.where(t < place[0], apply_power(eight, state) + ends[t], state)
        state_ref[...] = state

    one = [one_ref[b] for b in range(4)]
    state = state_ref[...]
    for half in range(2):
        local = local_ref[step, :, half * CH : (half + 1) * CH]
        masked = jnp.concatenate([local * spread_ref[k] for k in range(4)], axis=1)
        spread = jnp.concatenate([onehot_ref[k : k + 1, :] * state for k in range(4)], axis=0)
        high = spread.astype(BF16)
        low = (spread - high.astype(F32)).astype(BF16)
        stacked = jnp.concatenate([high, high, low], axis=0)
        carried = lax.dot_general(
            stacked, gain_ref[...], (((0,), (0,)), ((), ())), preferred_element_type=F32
        )
        out_ref[:, half * CH : (half + 1) * CH] = (
            jnp.dot(masked, toeplitz_ref[...], preferred_element_type=F32) + carried
        )
        ends = lax.dot_general(
            final_ref[...], local, (((1,), (1,)), ((), ())), preferred_element_type=F32
        )
        entered = onehot_ref[0:1, :] * ends[0:4]
        for k in range(1, 4):
            entered = entered + onehot_ref[k : k + 1, :] * ends[k * 8 : k * 8 + 4]
        state = apply_power(one, state) + entered
    state_ref[...] = state


def filtered(place, *args):
    return pl.pallas_call(
        filter_kernel,
        grid_spec=pltpu.PrefetchScalarGridSpec(
            num_scalar_prefetch=1,
            grid=(NX,),
            in_specs=[whole(a) for a in args],
            out_specs=pl.BlockSpec((ROWS, SLAB), lambda i, zs: (0, i)),
            scratch_shapes=[
                pltpu.VMEM((4, ROWS), F32),
                pltpu.VMEM((NX, ROWS, SLAB), BF16),
                pltpu.VMEM((4, ROWS, CH), BF16),
            ],
        ),
        out_shape=jax.ShapeDtypeStruct((ROWS, NX * SLAB), F32),
        compiler_params=pltpu.CompilerParams(vmem_limit_bytes=VMEM_LIMIT),
        cost_estimate=pl.CostEstimate(
            flops=8 * 2 * ROWS * CH * 1100, bytes_accessed=4 * 1024 * 1024, transcendentals=0
        ),
    )(place, *args)


def ring(value, by):
    return lax.ppermute(value, "z", [(i, (i + by) % NZ) for i in range(NZ)])


def round_x(value, by):
    return lax.ppermute(value, "x", [(i, (i + by) % NX) for i in range(NX)])


def together(*lists):
    return lax.optimization_barrier(lists)


def body(factor, white_noise, site_class, site_decay, site_angle, site_mix):
    x = lax.axis_index("x")
    z = lax.axis_index("z")
    tm = lax.axis_index("y") * NCORE + lax.axis_index("c")

    share = lax.dynamic_slice(factor, (tm * 32, 0), (32, factor.shape[1]))
    share = jnp.concatenate([share[:, b * CH : (b + 1) * CH] for b in range(NX * NZ)], axis=0)
    gathered = lax.all_gather(share, ("x", "y", "c"), tiled=True)
    gathered = gathered.reshape(32, NX * NZ, 32, CH)

    def cut(by):
        first = lax.rem(x + by, NX) * SLAB
        return lax.dynamic_slice(white_noise, (0, first), (ROWS, SLAB))

    parts = [cut(0)] + [round_x(cut(d), d) for d in (1, 2, 3)]
    steps = []
    for half in range(2):
        start = jnp.concatenate([p[:, half * CH : (half + 1) * CH] for p in parts], axis=0)
        steps.append([start, ring(start, 1), ring(start, -1)])
    first, second = steps
    site_class, site_decay, site_angle, site_mix, *first[1:] = lax.optimization_barrier(
        (site_class, site_decay, site_angle, site_mix, *first[1:])
    )
    for _ in range(2):
        first += [ring(first[-2], 1), ring(first[-1], -1)]
        second[-2:], first[-4:-2] = together(second[-2:], first[-4:-2])
        second += [ring(second[-2], 1), ring(second[-1], -1)]
        first[-2:], second[-4:-2] = together(first[-2:], second[-4:-2])

    toeplitz, final, gain, one, two, eight = tables(site_decay, site_angle, site_mix)
    by_block = site_class.reshape(NX, NZ, ROWS)
    ids = jnp.arange(4, dtype=jnp.int32)
    tile_class = lax.dynamic_slice(by_block, (0, z, 0), (NX, 1, ROWS)).reshape(1, NX * ROWS)
    tile_hot = (tile_class == ids[:, None]).astype(F32)
    own_class = lax.dynamic_slice(by_block, (x, z, 0), (1, 1, ROWS)).reshape(1, ROWS)
    own_hot = (own_class == ids[:, None]).astype(F32)
    own_mask = (own_class.reshape(ROWS, 1) == ids[None, :]).astype(BF16)
    scalars = jnp.stack([x] + [(z + by) % NZ for by in AWAY + (4,)]).astype(jnp.int32)
    place = jnp.stack([tm, x]).astype(jnp.int32)
    for_last = (final, tile_hot, per_row(one, tile_hot))
    for_filter = (
        own_mask, own_hot, per_row(one, own_hot), per_row(two, own_hot), per_row(eight, own_hot),
        toeplitz, final, gain,
    )
    scalars, place, for_last, for_filter, first[5] = lax.optimization_barrier(
        (scalars, place, for_last, for_filter, first[5])
    )
    second[6], _ = together(second[6], first[5])
    opposite = [ring(first[5], 1), ring(second[6], -1)]

    total = product(scalars, gathered, [n for pair in zip(*steps) for n in pair])
    *pieces, to_send = last_product(scalars, gathered, opposite, total, *for_last)
    excitation = [pieces[0]] + [round_x(pieces[d], d) for d in (1, 2, 3)]
    own_ends = lax.all_to_all(to_send, ("y", "c", "x"), 0, 0, tiled=True)
    return filtered(place, *excitation, own_ends, *for_filter)


def solution(mesh):
    fine = Mesh(mesh.devices.reshape(NX, NZ, NY, NCORE), ("x", "z", "y", "c"))
    rows = ("x", "z")
    in_specs = (P(rows, None), P(rows, ("y", "c")), P(), P(), P(), P())
    return jax.shard_map(
        body, mesh=fine, in_specs=in_specs, out_specs=P(rows, ("y", "c")), check_vma=False
    )
```

```python
import functools

import jax
import jax.numpy as jnp
from jax import lax
from jax.experimental import pallas as pl
from jax.experimental.pallas import tpu as pltpu
from jax.sharding import Mesh, PartitionSpec as P

CH = 256
NX, NZ, NY, NCORE = 4, 8, 4, 2
ROWS = 256
SLAB = 512
AWAY = (0, 7, 1, 6, 2, 5, 3)
AHEAD = 3
VMEM_LIMIT = 58 * 1024 * 1024
F32 = jnp.float32
BF16 = jnp.bfloat16
PRECISE = lax.Precision.HIGHEST


def system(site_decay, site_angle, site_mix):
    radius = 1.0 - site_decay
    norm_gain = jnp.sqrt(site_decay * (2.0 - site_decay))
    cos_ground = radius[0] * jnp.cos(site_angle[0])
    sin_ground = radius[0] * jnp.sin(site_angle[0])
    cos_high = radius[1] * jnp.cos(site_angle[1])
    sin_high = radius[1] * jnp.sin(site_angle[1])
    zeros_row = jnp.zeros_like(cos_ground)
    ones_row = jnp.ones_like(cos_ground)
    mix_a, mix_b, out_a, out_b = (site_mix[0], site_mix[1], site_mix[2], site_mix[3])
    row_list = [
        [cos_ground, -sin_ground, zeros_row, zeros_row],
        [sin_ground, cos_ground, zeros_row, zeros_row],
        [
            norm_gain[0] * (mix_a * cos_ground + mix_b * sin_ground),
            norm_gain[0] * (mix_b * cos_ground - mix_a * sin_ground),
            cos_high,
            -sin_high,
        ],
        [zeros_row, zeros_row, sin_high, cos_high],
    ]
    matrix = jnp.stack([jnp.stack(entries, axis=-1) for entries in row_list], axis=1)
    entry_vec = jnp.stack([ones_row, zeros_row, norm_gain[0] * mix_a, zeros_row], axis=-1)
    readout = jnp.stack([zeros_row, zeros_row, norm_gain[1] * out_a, norm_gain[1] * out_b], axis=-1)
    return (matrix, entry_vec, readout)


def tables(site_decay, site_angle, site_mix):
    matrix, entry_vec, readout = system(site_decay, site_angle, site_mix)
    classes = matrix.shape[0]
    powers = matrix[None]
    while powers.shape[0] < CH:
        further = jnp.einsum("kab,jkbc->jkac", powers[-1], powers, precision=PRECISE)
        powers = jnp.concatenate([powers, further], axis=0)
    gains = jnp.einsum("ka,jkab->kbj", readout, powers, precision=PRECISE)
    responses = jnp.einsum("jkab,kb->kja", powers[: CH - 1], entry_vec, precision=PRECISE)
    responses = jnp.concatenate([entry_vec[:, None, :], responses], axis=1)
    impulse = jnp.einsum("ka,kma->km", readout, responses, precision=PRECISE)
    padded_len = 2 * CH
    padded = jnp.concatenate([impulse, jnp.zeros((classes, CH), F32)], axis=1)
    tiled = jnp.tile(padded, (1, CH))[:, : CH * (padded_len - 1)]
    toeplitz = tiled.reshape(classes, CH, padded_len - 1)[:, :, :CH]
    toeplitz = toeplitz.reshape(classes * CH, CH).astype(BF16)
    final = responses[:, ::-1, :].transpose(0, 2, 1).astype(BF16)
    final = jnp.concatenate([final, jnp.zeros_like(final)], axis=1).reshape(classes * 8, CH)
    gains = gains.reshape(classes * 4, CH)
    gains_hi = lax.reduce_precision(gains, 8, 7)
    gains_lo = (gains - gains_hi).astype(BF16)
    gains_hi = gains_hi.astype(BF16)
    gain_stack = jnp.concatenate([gains_hi, gains_lo, gains_hi], axis=0)
    power = powers[-1]
    twice = [power]
    for _ in range(3):
        twice.append(jnp.einsum("kab,kbc->kac", twice[-1], twice[-1], precision=PRECISE))
    return toeplitz, final, gain_stack, power, twice[1], twice[3]


def per_row(power, onehot):
    return jnp.sum(power.transpose(2, 1, 0)[:, :, :, None] * onehot[None, None], axis=2)


def apply_power(table, state):
    out = table[0] * state[0:1]
    for b in range(1, 4):
        out = out + table[b] * state[b : b + 1]
    return out


def load(zs, where, g_ref, noise, held, block, sems):
    every = []
    for b, z in enumerate(where):
        copies = []
        for q in range(NX):
            columns = pl.ds(pl.multiple_of(q * NZ * CH + zs[z] * CH, CH), CH)
            copies.append(
                pltpu.make_async_copy(
                    g_ref.at[pl.ds(q, NX - q), :, columns], held[q].at[b], sems.at[b, q]
                )
            )
        for half in range(2):
            copies.append(
                pltpu.make_async_copy(
                    noise[2 * b + half], block.at[b, half], sems.at[b, NX + half]
                )
            )
        every.append(copies)
    return every


def term(zs, held, block, b, s):
    parts = [held[q][b, s - q] for q in range(s + 1)]
    rows = jnp.concatenate(parts, axis=1) if s else parts[0]
    turns = [pl.multiple_of(lax.rem(zs[0] + NX - q, NX) * ROWS, ROWS) for q in range(s + 1)]
    noise = jnp.concatenate(
        [
            jnp.concatenate([block[b, half, pl.ds(t, ROWS), :] for half in range(2)], axis=1)
            for t in turns
        ],
        axis=0,
    )
    return jnp.dot(rows, noise, preferred_element_type=F32)


def product_kernel(zs, g_ref, *refs):
    count = 2 * len(AWAY)
    noise_refs, (out_ref, *held, block, sems) = refs[:count], refs[count:]
    copies = load(zs, range(1, 8), g_ref, noise_refs, held, block, sems)
    for b in range(AHEAD):
        for copy in copies[b]:
            copy.start()
    for b in range(len(AWAY)):
        for copy in copies[b]:
            copy.wait()
        if b + AHEAD < len(AWAY):
            for copy in copies[b + AHEAD]:
                copy.start()
        for s in range(NX):
            rows = pl.ds(s * ROWS, ROWS)
            value = term(zs, held, block, b, s)
            out_ref[rows, :] = value if b == 0 else out_ref[rows, :] + value


def scratch(blocks):
    return [pltpu.VMEM((blocks, NX - q, ROWS, CH), BF16) for q in range(NX)] + [
        pltpu.VMEM((blocks, 2, NX * ROWS, CH), BF16),
        pltpu.SemaphoreType.DMA((blocks, 3 * NX)),
    ]


def whole(a):
    return pl.BlockSpec(a.shape, lambda i, zs: (0,) * len(a.shape))


ANYWHERE = pl.BlockSpec(memory_space=pl.ANY)


def product(scalars, gathered, noise_blocks):
    out = jax.ShapeDtypeStruct((NX * ROWS, SLAB), F32)
    return pl.pallas_call(
        product_kernel,
        grid_spec=pltpu.PrefetchScalarGridSpec(
            num_scalar_prefetch=1,
            grid=(1,),
            in_specs=[ANYWHERE] * (1 + len(noise_blocks)),
            out_specs=whole(out),
            scratch_shapes=scratch(len(AWAY)),
        ),
        out_shape=out,
        compiler_params=pltpu.CompilerParams(vmem_limit_bytes=VMEM_LIMIT),
        cost_estimate=pl.CostEstimate(
            flops=7 * 2 * 10 * ROWS * CH * SLAB, bytes_accessed=19 * 1048576, transcendentals=0
        ),
    )(scalars, gathered, *noise_blocks)


def last_kernel(
    zs, g_ref, first_ref, second_ref, total_ref, final_ref, onehot_ref,
    power_ref, *refs,
):
    piece_refs, (send_ref, local, acc_ref, *held, block, sems) = refs[:NX], refs[NX:]
    (waits,) = load(zs, (8,), g_ref, (first_ref, second_ref), held, block, sems)
    for copy in waits[NX:] + waits[:NX]:
        copy.start()
    fetch = []
    for s in range(NX):
        rows = pl.ds(s * ROWS, ROWS)
        fetch.append(
            pltpu.make_async_copy(total_ref.at[rows], acc_ref.at[rows], sems.at[0, 2 * NX + s])
        )
        fetch[s].start()
    for copy in waits[NX:]:
        copy.wait()
    for s in range(NX):
        waits[s].wait()
        fetch[s].wait()
        rows = pl.ds(s * ROWS, ROWS)
        local[s] = (acc_ref[rows, :] + term(zs, held, block, 0, s)).astype(BF16)
    for d in range(NX):
        piece_refs[d][...] = local[lax.rem(zs[0] + d, NX)]
    for s in range(NX):
        rows = slice(s * ROWS, (s + 1) * ROWS)
        end = None
        for half in range(2):
            ends = lax.dot_general(
                final_ref[...], local[s, :, half * CH : (half + 1) * CH],
                (((1,), (1,)), ((), ())), preferred_element_type=F32,
            )
            picked = onehot_ref[0:1, rows] * ends[0:4]
            for k in range(1, 4):
                picked = picked + onehot_ref[k : k + 1, rows] * ends[k * 8 : k * 8 + 4]
            end = (
                apply_power([power_ref[b, :, rows] for b in range(4)], end) + picked
                if half
                else picked
            )
        for t in range(s, NY * NCORE * NX, NX):
            send_ref[t] = end


def last_product(scalars, gathered, noise, total, *args):
    out_shape = [jax.ShapeDtypeStruct((ROWS, SLAB), BF16)] * NX
    out_shape.append(jax.ShapeDtypeStruct((NY * NCORE * NX, 4, ROWS), F32))
    return pl.pallas_call(
        last_kernel,
        grid_spec=pltpu.PrefetchScalarGridSpec(
            num_scalar_prefetch=1,
            grid=(1,),
            in_specs=[ANYWHERE] * 4 + [whole(a) for a in args],
            out_specs=[whole(a) for a in out_shape],
            scratch_shapes=[
                pltpu.VMEM((NX, ROWS, SLAB), BF16),
                pltpu.VMEM((NX * ROWS, SLAB), F32),
                *scratch(1),
            ],
        ),
        out_shape=out_shape,
        compiler_params=pltpu.CompilerParams(vmem_limit_bytes=VMEM_LIMIT),
        cost_estimate=pl.CostEstimate(
            flops=2 * 11 * ROWS * CH * SLAB, bytes_accessed=6 * 1048576, transcendentals=0
        ),
    )(scalars, gathered, *noise, total, *args)


def filter_kernel(
    place, own_ref, by_one_ref, by_two_ref, by_three_ref, slabs_ref, mask_ref, onehot_ref,
    one_ref, two_ref, eight_ref, toeplitz_ref, final_ref, gain_ref, out_ref, state_ref, local_ref, spread_ref,
):
    step = pl.program_id(0)

    @pl.when(step == 0)
    def _():
        for d, ref in enumerate((own_ref, by_one_ref, by_two_ref, by_three_ref)):
            local_ref[lax.rem(place[1] + NX - d, NX)] = ref[...]
        for k in range(4):
            spread_ref[k] = jnp.broadcast_to(mask_ref[:, k : k + 1], (ROWS, CH))
        slabs = slabs_ref[...].reshape(NY * NCORE, NX, 4, ROWS)
        ends = slabs[:, 0]
        for s in range(1, NX):
            moved = slabs[:, s]
            for b in range(4):
                moved = moved + two_ref[b][None] * ends[:, b : b + 1, :]
            ends = moved
        eight = [eight_ref[b] for b in range(4)]
        state = jnp.zeros((4, ROWS), F32)
        for t in range(NY * NCORE - 1):
            state = jnp.where(t < place[0], apply_power(eight, state) + ends[t], state)
        state_ref[...] = state

    one = [one_ref[b] for b in range(4)]
    state = state_ref[...]
    for half in range(2):
        local = local_ref[step, :, half * CH : (half + 1) * CH]
        masked = jnp.concatenate([local * spread_ref[k] for k in range(4)], axis=1)
        spread = jnp.concatenate([onehot_ref[k : k + 1, :] * state for k in range(4)], axis=0)
        high = spread.astype(BF16)
        low = (spread - high.astype(F32)).astype(BF16)
        stacked = jnp.concatenate([high, high, low], axis=0)
        carried = lax.dot_general(
            stacked, gain_ref[...], (((0,), (0,)), ((), ())), preferred_element_type=F32
        )
        out_ref[:, half * CH : (half + 1) * CH] = (
            jnp.dot(masked, toeplitz_ref[...], preferred_element_type=F32) + carried
        )
        ends = lax.dot_general(
            final_ref[...], local, (((1,), (1,)), ((), ())), preferred_element_type=F32
        )
        entered = onehot_ref[0:1, :] * ends[0:4]
        for k in range(1, 4):
            entered = entered + onehot_ref[k : k + 1, :] * ends[k * 8 : k * 8 + 4]
        state = apply_power(one, state) + entered
    state_ref[...] = state


def filtered(place, *args):
    return pl.pallas_call(
        filter_kernel,
        grid_spec=pltpu.PrefetchScalarGridSpec(
            num_scalar_prefetch=1,
            grid=(NX,),
            in_specs=[whole(a) for a in args],
            out_specs=pl.BlockSpec((ROWS, SLAB), lambda i, zs: (0, i)),
            scratch_shapes=[
                pltpu.VMEM((4, ROWS), F32),
                pltpu.VMEM((NX, ROWS, SLAB), BF16),
                pltpu.VMEM((4, ROWS, CH), BF16),
            ],
        ),
        out_shape=jax.ShapeDtypeStruct((ROWS, NX * SLAB), F32),
        compiler_params=pltpu.CompilerParams(vmem_limit_bytes=VMEM_LIMIT),
        cost_estimate=pl.CostEstimate(
            flops=8 * 2 * ROWS * CH * 1100, bytes_accessed=4 * 1024 * 1024, transcendentals=0
        ),
    )(place, *args)


def ring(value, by):
    return lax.ppermute(value, "z", [(i, (i + by) % NZ) for i in range(NZ)])


def round_x(value, by):
    return lax.ppermute(value, "x", [(i, (i + by) % NX) for i in range(NX)])


def together(*lists):
    return lax.optimization_barrier(lists)


def body(factor, white_noise, site_class, site_decay, site_angle, site_mix):
    x = lax.axis_index("x")
    z = lax.axis_index("z")
    tm = lax.axis_index("y") * NCORE + lax.axis_index("c")

    share = lax.dynamic_slice(factor, (tm * 32, 0), (32, factor.shape[1]))
    gathered = lax.all_gather(share, ("x", "y", "c"), tiled=True)
    gathered = gathered.reshape(NX, ROWS, factor.shape[1])

    def cut(by):
        first = lax.rem(x + by, NX) * SLAB
        return lax.dynamic_slice(white_noise, (0, first), (ROWS, SLAB))

    parts = [cut(0)] + [round_x(cut(d), d) for d in (1, 2, 3)]
    steps = []
    for half in range(2):
        start = jnp.concatenate([p[:, half * CH : (half + 1) * CH] for p in parts], axis=0)
        steps.append([start, ring(start, 1), ring(start, -1)])
    first, second = steps
    site_class, site_decay, site_angle, site_mix, *first[1:] = lax.optimization_barrier(
        (site_class, site_decay, site_angle, site_mix, *first[1:])
    )
    for _ in range(2):
        first += [ring(first[-2], 1), ring(first[-1], -1)]
        second[-2:], first[-4:-2] = together(second[-2:], first[-4:-2])
        second += [ring(second[-2], 1), ring(second[-1], -1)]
        first[-2:], second[-4:-2] = together(first[-2:], second[-4:-2])

    toeplitz, final, gain, one, two, eight = tables(site_decay, site_angle, site_mix)
    by_block = site_class.reshape(NX, NZ, ROWS)
    ids = jnp.arange(4, dtype=jnp.int32)
    tile_class = lax.dynamic_slice(by_block, (0, z, 0), (NX, 1, ROWS)).reshape(1, NX * ROWS)
    tile_hot = (tile_class == ids[:, None]).astype(F32)
    own_class = lax.dynamic_slice(by_block, (x, z, 0), (1, 1, ROWS)).reshape(1, ROWS)
    own_hot = (own_class == ids[:, None]).astype(F32)
    own_mask = (own_class.reshape(ROWS, 1) == ids[None, :]).astype(BF16)
    scalars = jnp.stack([x] + [(z + by) % NZ for by in AWAY + (4,)]).astype(jnp.int32)
    place = jnp.stack([tm, x]).astype(jnp.int32)
    for_last = (final, tile_hot, per_row(one, tile_hot))
    for_filter = (
        own_mask, own_hot, per_row(one, own_hot), per_row(two, own_hot), per_row(eight, own_hot),
        toeplitz, final, gain,
    )
    scalars, place, for_last, for_filter, first[5] = lax.optimization_barrier(
        (scalars, place, for_last, for_filter, first[5])
    )
    second[6], _ = together(second[6], first[5])
    opposite = [ring(first[5], 1), ring(second[6], -1)]

    total = product(scalars, gathered, [n for pair in zip(*steps) for n in pair])
    *pieces, to_send = last_product(scalars, gathered, opposite, total, *for_last)
    excitation = [pieces[0]] + [round_x(pieces[d], d) for d in (1, 2, 3)]
    own_ends = lax.all_to_all(to_send, ("y", "c", "x"), 0, 0, tiled=True)
    return filtered(place, *excitation, own_ends, *for_filter)


def solution(mesh):
    fine = Mesh(mesh.devices.reshape(NX, NZ, NY, NCORE), ("x", "z", "y", "c"))
    rows = ("x", "z")
    in_specs = (P(rows, None), P(rows, ("y", "c")), P(), P(), P(), P())
    return jax.shard_map(
        body, mesh=fine, in_specs=in_specs, out_specs=P(rows, ("y", "c")), check_vma=False
    )
```

```python
import functools

import jax
import jax.numpy as jnp
from jax import lax
from jax.experimental import pallas as pl
from jax.experimental.pallas import tpu as pltpu
from jax.sharding import Mesh, PartitionSpec as P

CH = 256
NX, NZ, NY, NCORE = 4, 8, 4, 2
ROWS = 256
SLAB = 512
AWAY = (0, 7, 1, 6, 2, 5, 3)
AHEAD = 3
VMEM_LIMIT = 58 * 1024 * 1024
F32 = jnp.float32
BF16 = jnp.bfloat16
PRECISE = lax.Precision.HIGHEST


def system(site_decay, site_angle, site_mix):
    radius = 1.0 - site_decay
    norm_gain = jnp.sqrt(site_decay * (2.0 - site_decay))
    cos_ground = radius[0] * jnp.cos(site_angle[0])
    sin_ground = radius[0] * jnp.sin(site_angle[0])
    cos_high = radius[1] * jnp.cos(site_angle[1])
    sin_high = radius[1] * jnp.sin(site_angle[1])
    zeros_row = jnp.zeros_like(cos_ground)
    ones_row = jnp.ones_like(cos_ground)
    mix_a, mix_b, out_a, out_b = (site_mix[0], site_mix[1], site_mix[2], site_mix[3])
    row_list = [
        [cos_ground, -sin_ground, zeros_row, zeros_row],
        [sin_ground, cos_ground, zeros_row, zeros_row],
        [
            norm_gain[0] * (mix_a * cos_ground + mix_b * sin_ground),
            norm_gain[0] * (mix_b * cos_ground - mix_a * sin_ground),
            cos_high,
            -sin_high,
        ],
        [zeros_row, zeros_row, sin_high, cos_high],
    ]
    matrix = jnp.stack([jnp.stack(entries, axis=-1) for entries in row_list], axis=1)
    entry_vec = jnp.stack([ones_row, zeros_row, norm_gain[0] * mix_a, zeros_row], axis=-1)
    readout = jnp.stack([zeros_row, zeros_row, norm_gain[1] * out_a, norm_gain[1] * out_b], axis=-1)
    return (matrix, entry_vec, readout)


def tables(site_decay, site_angle, site_mix):
    matrix, entry_vec, readout = system(site_decay, site_angle, site_mix)
    classes = matrix.shape[0]
    powers = matrix[None]
    while powers.shape[0] < CH:
        further = jnp.einsum("kab,jkbc->jkac", powers[-1], powers, precision=PRECISE)
        powers = jnp.concatenate([powers, further], axis=0)
    gains = jnp.einsum("ka,jkab->kbj", readout, powers, precision=PRECISE)
    responses = jnp.einsum("jkab,kb->kja", powers[: CH - 1], entry_vec, precision=PRECISE)
    responses = jnp.concatenate([entry_vec[:, None, :], responses], axis=1)
    impulse = jnp.einsum("ka,kma->km", readout, responses, precision=PRECISE)
    padded_len = 2 * CH
    padded = jnp.concatenate([impulse, jnp.zeros((classes, CH), F32)], axis=1)
    tiled = jnp.tile(padded, (1, CH))[:, : CH * (padded_len - 1)]
    toeplitz = tiled.reshape(classes, CH, padded_len - 1)[:, :, :CH]
    toeplitz = toeplitz.reshape(classes * CH, CH).astype(BF16)
    final = responses[:, ::-1, :].transpose(0, 2, 1).astype(BF16)
    final = jnp.concatenate([final, jnp.zeros_like(final)], axis=1).reshape(classes * 8, CH)
    gains = gains.reshape(classes * 4, CH)
    gains_hi = lax.reduce_precision(gains, 8, 7)
    gains_lo = (gains - gains_hi).astype(BF16)
    gains_hi = gains_hi.astype(BF16)
    gain_stack = jnp.concatenate([gains_hi, gains_lo, gains_hi], axis=0)
    power = powers[-1]
    twice = [power]
    for _ in range(3):
        twice.append(jnp.einsum("kab,kbc->kac", twice[-1], twice[-1], precision=PRECISE))
    return toeplitz, final, gain_stack, power, twice[1], twice[3]


def per_row(power, onehot):
    return jnp.sum(power.transpose(2, 1, 0)[:, :, :, None] * onehot[None, None], axis=2)


def apply_power(table, state):
    out = table[0] * state[0:1]
    for b in range(1, 4):
        out = out + table[b] * state[b : b + 1]
    return out


def load(zs, where, g_ref, noise, held, block, sems):
    every = []
    for b, z in enumerate(where):
        copies = []
        for q in range(NX):
            columns = pl.ds(pl.multiple_of(q * NZ * CH + zs[z] * CH, CH), CH)
            copies.append(
                pltpu.make_async_copy(
                    g_ref.at[pl.ds(q, NX - q), :, columns], held[q].at[b], sems.at[b, q]
                )
            )
        for half, ref in enumerate(noise[2 * b : 2 * b + 2]):
            copies.append(
                pltpu.make_async_copy(ref, block.at[b, half], sems.at[b, NX + half])
            )
        every.append(copies)
    return every


def term(zs, held, block, b, s):
    parts = [held[q][b, s - q] for q in range(s + 1)]
    rows = jnp.concatenate(parts, axis=1) if s else parts[0]
    turns = [pl.multiple_of(lax.rem(zs[0] + NX - q, NX) * ROWS, ROWS) for q in range(s + 1)]
    noise = jnp.concatenate(
        [
            jnp.concatenate([block[b, half, pl.ds(t, ROWS), :] for half in range(2)], axis=1)
            for t in turns
        ],
        axis=0,
    )
    return jnp.dot(rows, noise, preferred_element_type=F32)


def product_kernel(blocks, has_acc, zs, g_ref, *refs):
    count = 2 * blocks
    noise_refs, refs = refs[:count], refs[count:]
    acc_ref, refs = (refs[0], refs[1:]) if has_acc else (None, refs)
    out_ref, *held, block, sems = refs
    if has_acc:
        fetch = pltpu.make_async_copy(acc_ref, out_ref, sems.at[0, 2 * NX])
        fetch.start()
    copies = load(zs, range(1, 1 + blocks), g_ref, noise_refs, held, block, sems)
    ahead = min(AHEAD, blocks)
    for b in range(ahead):
        for copy in copies[b]:
            copy.start()
    if has_acc:
        fetch.wait()
    for b in range(blocks):
        for copy in copies[b]:
            copy.wait()
        if b + ahead < blocks:
            for copy in copies[b + ahead]:
                copy.start()
        for s in range(NX):
            rows = pl.ds(s * ROWS, ROWS)
            value = term(zs, held, block, b, s)
            first = b == 0 and not has_acc
            out_ref[rows, :] = value if first else out_ref[rows, :] + value


def scratch(blocks):
    return [pltpu.VMEM((blocks, NX - q, ROWS, CH), BF16) for q in range(NX)] + [
        pltpu.VMEM((blocks, 2, NX * ROWS, CH), BF16),
        pltpu.SemaphoreType.DMA((blocks, 3 * NX)),
    ]


def whole(a):
    return pl.BlockSpec(a.shape, lambda i, zs: (0,) * len(a.shape))


ANYWHERE = pl.BlockSpec(memory_space=pl.ANY)


def product(where_z, gathered, noise_blocks, acc=None):
    blocks = len(noise_blocks) // 2
    out = jax.ShapeDtypeStruct((NX * ROWS, SLAB), F32)
    args = [*noise_blocks] + ([] if acc is None else [acc])
    return pl.pallas_call(
        functools.partial(product_kernel, blocks, acc is not None),
        grid_spec=pltpu.PrefetchScalarGridSpec(
            num_scalar_prefetch=1,
            grid=(1,),
            in_specs=[ANYWHERE] * (1 + len(args)),
            out_specs=whole(out),
            scratch_shapes=scratch(blocks),
        ),
        out_shape=out,
        compiler_params=pltpu.CompilerParams(vmem_limit_bytes=VMEM_LIMIT),
        cost_estimate=pl.CostEstimate(
            flops=blocks * 2 * 10 * ROWS * CH * SLAB,
            bytes_accessed=(3 * blocks + 2) * 1048576,
            transcendentals=0,
        ),
    )(where_z, gathered, *args)


def last_kernel(
    zs, g_ref, first_ref, up_ref, down_ref, total_ref, final_ref, onehot_ref,
    power_ref, *refs,
):
    piece_refs, (send_ref, local, acc_ref, *held, block, sems) = refs[:NX], refs[NX:]
    (waits,) = load(zs, (1,), g_ref, (first_ref,), held, block, sems)
    half = NX * ROWS // 2
    waits.append(
        pltpu.make_async_copy(up_ref, block.at[0, 1, pl.ds(0, half)], sems.at[0, NX + 1])
    )
    waits.append(
        pltpu.make_async_copy(down_ref, block.at[0, 1, pl.ds(half, half)], sems.at[0, NX + 2])
    )
    for copy in waits[NX:] + waits[:NX]:
        copy.start()
    fetch = []
    for s in range(NX):
        rows = pl.ds(s * ROWS, ROWS)
        fetch.append(
            pltpu.make_async_copy(total_ref.at[rows], acc_ref.at[rows], sems.at[0, 2 * NX + s])
        )
        fetch[s].start()
    for copy in waits[NX:]:
        copy.wait()
    for s in range(NX):
        waits[s].wait()
        fetch[s].wait()
        rows = pl.ds(s * ROWS, ROWS)
        local[s] = (acc_ref[rows, :] + term(zs, held, block, 0, s)).astype(BF16)
    for d in range(NX):
        piece_refs[d][...] = local[lax.rem(zs[0] + d, NX)]
    for s in range(NX):
        rows = slice(s * ROWS, (s + 1) * ROWS)
        end = None
        for half in range(2):
            ends = lax.dot_general(
                final_ref[...], local[s, :, half * CH : (half + 1) * CH],
                (((1,), (1,)), ((), ())), preferred_element_type=F32,
            )
            picked = onehot_ref[0:1, rows] * ends[0:4]
            for k in range(1, 4):
                picked = picked + onehot_ref[k : k + 1, rows] * ends[k * 8 : k * 8 + 4]
            end = (
                apply_power([power_ref[b, :, rows] for b in range(4)], end) + picked
                if half
                else picked
            )
        for t in range(s, NY * NCORE * NX, NX):
            send_ref[t] = end


def last_product(scalars, gathered, noise, total, *args):
    out_shape = [jax.ShapeDtypeStruct((ROWS, SLAB), BF16)] * NX
    out_shape.append(jax.ShapeDtypeStruct((NY * NCORE * NX, 4, ROWS), F32))
    return pl.pallas_call(
        last_kernel,
        grid_spec=pltpu.PrefetchScalarGridSpec(
            num_scalar_prefetch=1,
            grid=(1,),
            in_specs=[ANYWHERE] * 5 + [whole(a) for a in args],
            out_specs=[whole(a) for a in out_shape],
            scratch_shapes=[
                pltpu.VMEM((NX, ROWS, SLAB), BF16),
                pltpu.VMEM((NX * ROWS, SLAB), F32),
                *scratch(1),
            ],
        ),
        out_shape=out_shape,
        compiler_params=pltpu.CompilerParams(vmem_limit_bytes=VMEM_LIMIT),
        cost_estimate=pl.CostEstimate(
            flops=2 * 11 * ROWS * CH * SLAB, bytes_accessed=6 * 1048576, transcendentals=0
        ),
    )(scalars, gathered, *noise, total, *args)


def filter_kernel(
    place, own_ref, by_one_ref, by_two_ref, by_three_ref, slabs_ref, mask_ref, onehot_ref,
    one_ref, two_ref, eight_ref, toeplitz_ref, final_ref, gain_ref, out_ref, state_ref, local_ref, spread_ref,
):
    step = pl.program_id(0)

    @pl.when(step == 0)
    def _():
        for d, ref in enumerate((own_ref, by_one_ref, by_two_ref, by_three_ref)):
            local_ref[lax.rem(place[1] + NX - d, NX)] = ref[...]
        for k in range(4):
            spread_ref[k] = jnp.broadcast_to(mask_ref[:, k : k + 1], (ROWS, CH))
        slabs = slabs_ref[...].reshape(NY * NCORE, NX, 4, ROWS)
        ends = slabs[:, 0]
        for s in range(1, NX):
            moved = slabs[:, s]
            for b in range(4):
                moved = moved + two_ref[b][None] * ends[:, b : b + 1, :]
            ends = moved
        eight = [eight_ref[b] for b in range(4)]
        state = jnp.zeros((4, ROWS), F32)
        for t in range(NY * NCORE - 1):
            state = jnp.where(t < place[0], apply_power(eight, state) + ends[t], state)
        state_ref[...] = state

    one = [one_ref[b] for b in range(4)]
    state = state_ref[...]
    for half in range(2):
        local = local_ref[step, :, half * CH : (half + 1) * CH]
        masked = jnp.concatenate([local * spread_ref[k] for k in range(4)], axis=1)
        spread = jnp.concatenate([onehot_ref[k : k + 1, :] * state for k in range(4)], axis=0)
        high = spread.astype(BF16)
        low = (spread - high.astype(F32)).astype(BF16)
        stacked = jnp.concatenate([high, high, low], axis=0)
        carried = lax.dot_general(
            stacked, gain_ref[...], (((0,), (0,)), ((), ())), preferred_element_type=F32
        )
        out_ref[:, half * CH : (half + 1) * CH] = (
            jnp.dot(masked, toeplitz_ref[...], preferred_element_type=F32) + carried
        )
        ends = lax.dot_general(
            final_ref[...], local, (((1,), (1,)), ((), ())), preferred_element_type=F32
        )
        entered = onehot_ref[0:1, :] * ends[0:4]
        for k in range(1, 4):
            entered = entered + onehot_ref[k : k + 1, :] * ends[k * 8 : k * 8 + 4]
        state = apply_power(one, state) + entered
    state_ref[...] = state


def filtered(place, *args):
    return pl.pallas_call(
        filter_kernel,
        grid_spec=pltpu.PrefetchScalarGridSpec(
            num_scalar_prefetch=1,
            grid=(NX,),
            in_specs=[whole(a) for a in args],
            out_specs=pl.BlockSpec((ROWS, SLAB), lambda i, zs: (0, i)),
            scratch_shapes=[
                pltpu.VMEM((4, ROWS), F32),
                pltpu.VMEM((NX, ROWS, SLAB), BF16),
                pltpu.VMEM((4, ROWS, CH), BF16),
            ],
        ),
        out_shape=jax.ShapeDtypeStruct((ROWS, NX * SLAB), F32),
        compiler_params=pltpu.CompilerParams(vmem_limit_bytes=VMEM_LIMIT),
        cost_estimate=pl.CostEstimate(
            flops=8 * 2 * ROWS * CH * 1100, bytes_accessed=4 * 1024 * 1024, transcendentals=0
        ),
    )(place, *args)


def ring(value, by):
    return lax.ppermute(value, "z", [(i, (i + by) % NZ) for i in range(NZ)])


def round_x(value, by):
    return lax.ppermute(value, "x", [(i, (i + by) % NX) for i in range(NX)])


def together(*lists):
    return lax.optimization_barrier(lists)


def body(factor, white_noise, site_class, site_decay, site_angle, site_mix):
    x = lax.axis_index("x")
    z = lax.axis_index("z")
    tm = lax.axis_index("y") * NCORE + lax.axis_index("c")

    share = lax.dynamic_slice(factor, (tm * 32, 0), (32, factor.shape[1]))
    gathered = lax.all_gather(share, ("x", "y", "c"), tiled=True)
    gathered = gathered.reshape(NX, ROWS, factor.shape[1])

    def cut(by):
        first = lax.rem(x + by, NX) * SLAB
        return lax.dynamic_slice(white_noise, (0, first), (ROWS, SLAB))

    parts = [cut(0)] + [round_x(cut(d), d) for d in (1, 2, 3)]
    steps = []
    for half in range(2):
        start = jnp.concatenate([p[:, half * CH : (half + 1) * CH] for p in parts], axis=0)
        steps.append([start, ring(start, 1), ring(start, -1)])
    first, second = steps
    site_class, site_decay, site_angle, site_mix, *first[1:] = lax.optimization_barrier(
        (site_class, site_decay, site_angle, site_mix, *first[1:])
    )
    for _ in range(2):
        first += [ring(first[-2], 1), ring(first[-1], -1)]
        second[-2:], first[-4:-2] = together(second[-2:], first[-4:-2])
        second += [ring(second[-2], 1), ring(second[-1], -1)]
        first[-2:], second[-4:-2] = together(first[-2:], second[-4:-2])

    toeplitz, final, gain, one, two, eight = tables(site_decay, site_angle, site_mix)
    by_block = site_class.reshape(NX, NZ, ROWS)
    ids = jnp.arange(4, dtype=jnp.int32)
    tile_class = lax.dynamic_slice(by_block, (0, z, 0), (NX, 1, ROWS)).reshape(1, NX * ROWS)
    tile_hot = (tile_class == ids[:, None]).astype(F32)
    own_class = lax.dynamic_slice(by_block, (x, z, 0), (1, 1, ROWS)).reshape(1, ROWS)
    own_hot = (own_class == ids[:, None]).astype(F32)
    own_mask = (own_class.reshape(ROWS, 1) == ids[None, :]).astype(BF16)
    scalars = [
        jnp.stack([x] + [(z + by) % NZ for by in away]).astype(jnp.int32)
        for away in (AWAY[:5], AWAY[5:], (4,))
    ]
    place = jnp.stack([tm, x]).astype(jnp.int32)
    for_last = (final, tile_hot, per_row(one, tile_hot))
    for_filter = (
        own_mask, own_hot, per_row(one, own_hot), per_row(two, own_hot), per_row(eight, own_hot),
        toeplitz, final, gain,
    )
    scalars, place, for_last, for_filter, first[5] = lax.optimization_barrier(
        (scalars, place, for_last, for_filter, first[5])
    )
    pairs = [n for pair in zip(*steps) for n in pair]
    opposite = [ring(first[5], 1)]
    total = product(scalars[0], gathered, pairs[:10])
    second[5], second[6], total = lax.optimization_barrier((second[5], second[6], total))
    opposite += [ring(second[5][:512], 1), ring(second[6][512:], -1)]
    opposite[0], total = lax.optimization_barrier((opposite[0], total))
    total = product(scalars[1], gathered, pairs[10:], total)
    *pieces, to_send = last_product(scalars[2], gathered, opposite, total, *for_last)
    excitation = [pieces[0]] + [round_x(pieces[d], d) for d in (1, 2, 3)]
    own_ends = lax.all_to_all(to_send, ("y", "c", "x"), 0, 0, tiled=True)
    return filtered(place, *excitation, own_ends, *for_filter)


def solution(mesh):
    fine = Mesh(mesh.devices.reshape(NX, NZ, NY, NCORE), ("x", "z", "y", "c"))
    rows = ("x", "z")
    in_specs = (P(rows, None), P(rows, ("y", "c")), P(), P(), P(), P())
    return jax.shard_map(
        body, mesh=fine, in_specs=in_specs, out_specs=P(rows, ("y", "c")), check_vma=False
    )
```

```python
import functools

import jax
import jax.numpy as jnp
from jax import lax
from jax.experimental import pallas as pl
from jax.experimental.pallas import tpu as pltpu
from jax.sharding import Mesh, PartitionSpec as P

CH = 256
NX, NZ, NY, NCORE = 4, 8, 4, 2
ROWS = 256
SLAB = 512
AWAY = (0, 7, 1, 6, 2, 5, 3)
AHEAD = 3
VMEM_LIMIT = 44 * 1024 * 1024
F32 = jnp.float32
BF16 = jnp.bfloat16
PRECISE = lax.Precision.HIGHEST


def system(site_decay, site_angle, site_mix):
    radius = 1.0 - site_decay
    norm_gain = jnp.sqrt(site_decay * (2.0 - site_decay))
    cos_ground = radius[0] * jnp.cos(site_angle[0])
    sin_ground = radius[0] * jnp.sin(site_angle[0])
    cos_high = radius[1] * jnp.cos(site_angle[1])
    sin_high = radius[1] * jnp.sin(site_angle[1])
    zeros_row = jnp.zeros_like(cos_ground)
    ones_row = jnp.ones_like(cos_ground)
    mix_a, mix_b, out_a, out_b = (site_mix[0], site_mix[1], site_mix[2], site_mix[3])
    row_list = [
        [cos_ground, -sin_ground, zeros_row, zeros_row],
        [sin_ground, cos_ground, zeros_row, zeros_row],
        [
            norm_gain[0] * (mix_a * cos_ground + mix_b * sin_ground),
            norm_gain[0] * (mix_b * cos_ground - mix_a * sin_ground),
            cos_high,
            -sin_high,
        ],
        [zeros_row, zeros_row, sin_high, cos_high],
    ]
    matrix = jnp.stack([jnp.stack(entries, axis=-1) for entries in row_list], axis=1)
    entry_vec = jnp.stack([ones_row, zeros_row, norm_gain[0] * mix_a, zeros_row], axis=-1)
    readout = jnp.stack([zeros_row, zeros_row, norm_gain[1] * out_a, norm_gain[1] * out_b], axis=-1)
    return (matrix, entry_vec, readout)


def tables(site_decay, site_angle, site_mix):
    matrix, entry_vec, readout = system(site_decay, site_angle, site_mix)
    classes = matrix.shape[0]
    powers = matrix[None]
    while powers.shape[0] < CH:
        further = jnp.einsum("kab,jkbc->jkac", powers[-1], powers, precision=PRECISE)
        powers = jnp.concatenate([powers, further], axis=0)
    gains = jnp.einsum("ka,jkab->kbj", readout, powers, precision=PRECISE)
    responses = jnp.einsum("jkab,kb->kja", powers[: CH - 1], entry_vec, precision=PRECISE)
    responses = jnp.concatenate([entry_vec[:, None, :], responses], axis=1)
    impulse = jnp.einsum("ka,kma->km", readout, responses, precision=PRECISE)
    padded_len = 2 * CH
    padded = jnp.concatenate([impulse, jnp.zeros((classes, CH), F32)], axis=1)
    tiled = jnp.tile(padded, (1, CH))[:, : CH * (padded_len - 1)]
    toeplitz = tiled.reshape(classes, CH, padded_len - 1)[:, :, :CH]
    toeplitz = toeplitz.reshape(classes * CH, CH).astype(BF16)
    final = responses[:, ::-1, :].transpose(0, 2, 1).astype(BF16)
    final = jnp.concatenate([final, jnp.zeros_like(final)], axis=1).reshape(classes * 8, CH)
    gains = gains.reshape(classes * 4, CH)
    gains_hi = lax.reduce_precision(gains, 8, 7)
    gains_lo = (gains - gains_hi).astype(BF16)
    gains_hi = gains_hi.astype(BF16)
    gain_stack = jnp.concatenate([gains_hi, gains_lo, gains_hi], axis=0)
    power = powers[-1]
    twice = [power]
    for _ in range(3):
        twice.append(jnp.einsum("kab,kbc->kac", twice[-1], twice[-1], precision=PRECISE))
    return toeplitz, final, gain_stack, power, twice[1], twice[3]


def per_row(power, onehot):
    return jnp.sum(power.transpose(2, 1, 0)[:, :, :, None] * onehot[None, None], axis=2)


def apply_power(table, state):
    out = table[0] * state[0:1]
    for b in range(1, 4):
        out = out + table[b] * state[b : b + 1]
    return out


def load(zs, where, g_ref, noise, held, block, sems):
    every = []
    for b, z in enumerate(where):
        copies = []
        for q in range(NX):
            columns = pl.ds(pl.multiple_of(q * NZ * CH + zs[z] * CH, CH), CH)
            copies.append(
                pltpu.make_async_copy(
                    g_ref.at[pl.ds(q, NX - q), :, columns], held[q].at[b], sems.at[b, q]
                )
            )
        for half in range(2):
            copies.append(
                pltpu.make_async_copy(
                    noise[2 * b + half], block.at[b, half], sems.at[b, NX + half]
                )
            )
        every.append(copies)
    return every


def term(zs, held, block, b, s):
    parts = [held[q][b, s - q] for q in range(s + 1)]
    rows = jnp.concatenate(parts, axis=1) if s else parts[0]
    turns = [pl.multiple_of(lax.rem(zs[0] + NX - q, NX) * ROWS, ROWS) for q in range(s + 1)]
    noise = jnp.concatenate(
        [
            jnp.concatenate([block[b, half, pl.ds(t, ROWS), :] for half in range(2)], axis=1)
            for t in turns
        ],
        axis=0,
    )
    return jnp.dot(rows, noise, preferred_element_type=F32)


def product_kernel(zs, g_ref, *refs):
    count = 2 * len(AWAY)
    noise_refs, (out_ref, *held, block, sems) = refs[:count], refs[count:]
    copies = load(zs, range(1, 8), g_ref, noise_refs, held, block, sems)
    for b in range(AHEAD):
        for copy in copies[b]:
            copy.start()
    for b in range(len(AWAY)):
        for copy in copies[b]:
            copy.wait()
        if b + AHEAD < len(AWAY):
            for copy in copies[b + AHEAD]:
                copy.start()
        for s in range(NX):
            rows = pl.ds(s * ROWS, ROWS)
            value = term(zs, held, block, b, s)
            out_ref[rows, :] = value if b == 0 else out_ref[rows, :] + value


def scratch(blocks):
    return [pltpu.VMEM((blocks, NX - q, ROWS, CH), BF16) for q in range(NX)] + [
        pltpu.VMEM((blocks, 2, NX * ROWS, CH), BF16),
        pltpu.SemaphoreType.DMA((blocks, 3 * NX)),
    ]


def whole(a):
    return pl.BlockSpec(a.shape, lambda i, zs: (0,) * len(a.shape))


ANYWHERE = pl.BlockSpec(memory_space=pl.ANY)


def product(scalars, gathered, noise_blocks):
    out = jax.ShapeDtypeStruct((NX * ROWS, SLAB), F32)
    return pl.pallas_call(
        product_kernel,
        grid_spec=pltpu.PrefetchScalarGridSpec(
            num_scalar_prefetch=1,
            grid=(1,),
            in_specs=[ANYWHERE] * (1 + len(noise_blocks)),
            out_specs=whole(out),
            scratch_shapes=scratch(len(AWAY)),
        ),
        out_shape=out,
        compiler_params=pltpu.CompilerParams(vmem_limit_bytes=VMEM_LIMIT),
        cost_estimate=pl.CostEstimate(
            flops=7 * 2 * 10 * ROWS * CH * SLAB, bytes_accessed=19 * 1048576, transcendentals=0
        ),
    )(scalars, gathered, *noise_blocks)


def last_kernel(
    zs, g_ref, first_ref, second_ref, total_ref, final_ref, onehot_ref,
    power_ref, *refs,
):
    piece_refs, (send_ref, local, acc_ref, *held, block, sems) = refs[:NX], refs[NX:]
    (waits,) = load(zs, (8,), g_ref, (first_ref, second_ref), held, block, sems)
    for copy in waits[NX:] + waits[:NX]:
        copy.start()
    fetch = []
    for s in range(NX):
        rows = pl.ds(s * ROWS, ROWS)
        fetch.append(
            pltpu.make_async_copy(total_ref.at[rows], acc_ref.at[rows], sems.at[0, 2 * NX + s])
        )
        fetch[s].start()
    for copy in waits[NX:]:
        copy.wait()
    for s in range(NX):
        waits[s].wait()
        fetch[s].wait()
        rows = pl.ds(s * ROWS, ROWS)
        local[s] = (acc_ref[rows, :] + term(zs, held, block, 0, s)).astype(BF16)
    for d in range(NX):
        piece_refs[d][...] = local[lax.rem(zs[0] + d, NX)]
    for s in range(NX):
        rows = slice(s * ROWS, (s + 1) * ROWS)
        end = None
        for half in range(2):
            ends = lax.dot_general(
                final_ref[...], local[s, :, half * CH : (half + 1) * CH],
                (((1,), (1,)), ((), ())), preferred_element_type=F32,
            )
            picked = onehot_ref[0:1, rows] * ends[0:4]
            for k in range(1, 4):
                picked = picked + onehot_ref[k : k + 1, rows] * ends[k * 8 : k * 8 + 4]
            end = (
                apply_power([power_ref[b, :, rows] for b in range(4)], end) + picked
                if half
                else picked
            )
        for t in range(s, NY * NCORE * NX, NX):
            send_ref[t] = end


def last_product(scalars, gathered, noise, total, *args):
    out_shape = [jax.ShapeDtypeStruct((ROWS, SLAB), BF16)] * NX
    out_shape.append(jax.ShapeDtypeStruct((NY * NCORE * NX, 4, ROWS), F32))
    return pl.pallas_call(
        last_kernel,
        grid_spec=pltpu.PrefetchScalarGridSpec(
            num_scalar_prefetch=1,
            grid=(1,),
            in_specs=[ANYWHERE] * 4 + [whole(a) for a in args],
            out_specs=[whole(a) for a in out_shape],
            scratch_shapes=[
                pltpu.VMEM((NX, ROWS, SLAB), BF16),
                pltpu.VMEM((NX * ROWS, SLAB), F32),
                *scratch(1),
            ],
        ),
        out_shape=out_shape,
        compiler_params=pltpu.CompilerParams(vmem_limit_bytes=VMEM_LIMIT),
        cost_estimate=pl.CostEstimate(
            flops=2 * 11 * ROWS * CH * SLAB, bytes_accessed=6 * 1048576, transcendentals=0
        ),
    )(scalars, gathered, *noise, total, *args)


def filter_kernel(
    place, own_ref, by_one_ref, by_two_ref, by_three_ref, slabs_ref, mask_ref, onehot_ref,
    one_ref, two_ref, eight_ref, toeplitz_ref, final_ref, gain_ref, out_ref, state_ref, local_ref, spread_ref,
):
    step = pl.program_id(0)

    @pl.when(step == 0)
    def _():
        for d, ref in enumerate((own_ref, by_one_ref, by_two_ref, by_three_ref)):
            local_ref[lax.rem(place[1] + NX - d, NX)] = ref[...]
        for k in range(4):
            spread_ref[k] = jnp.broadcast_to(mask_ref[:, k : k + 1], (ROWS, CH))
        slabs = slabs_ref[...].reshape(NY * NCORE, NX, 4, ROWS)
        ends = slabs[:, 0]
        for s in range(1, NX):
            moved = slabs[:, s]
            for b in range(4):
                moved = moved + two_ref[b][None] * ends[:, b : b + 1, :]
            ends = moved
        eight = [eight_ref[b] for b in range(4)]
        state = jnp.zeros((4, ROWS), F32)
        for t in range(NY * NCORE - 1):
            state = jnp.where(t < place[0], apply_power(eight, state) + ends[t], state)
        state_ref[...] = state

    one = [one_ref[b] for b in range(4)]
    state = state_ref[...]
    for half in range(2):
        local = local_ref[step, :, half * CH : (half + 1) * CH]
        masked = jnp.concatenate([local * spread_ref[k] for k in range(4)], axis=1)
        spread = jnp.concatenate([onehot_ref[k : k + 1, :] * state for k in range(4)], axis=0)
        high = spread.astype(BF16)
        low = (spread - high.astype(F32)).astype(BF16)
        stacked = jnp.concatenate([high, high, low], axis=0)
        carried = lax.dot_general(
            stacked, gain_ref[...], (((0,), (0,)), ((), ())), preferred_element_type=F32
        )
        out_ref[:, half * CH : (half + 1) * CH] = (
            jnp.dot(masked, toeplitz_ref[...], preferred_element_type=F32) + carried
        )
        ends = lax.dot_general(
            final_ref[...], local, (((1,), (1,)), ((), ())), preferred_element_type=F32
        )
        entered = onehot_ref[0:1, :] * ends[0:4]
        for k in range(1, 4):
            entered = entered + onehot_ref[k : k + 1, :] * ends[k * 8 : k * 8 + 4]
        state = apply_power(one, state) + entered
    state_ref[...] = state


def filtered(place, *args):
    return pl.pallas_call(
        filter_kernel,
        grid_spec=pltpu.PrefetchScalarGridSpec(
            num_scalar_prefetch=1,
            grid=(NX,),
            in_specs=[whole(a) for a in args],
            out_specs=pl.BlockSpec((ROWS, SLAB), lambda i, zs: (0, i)),
            scratch_shapes=[
                pltpu.VMEM((4, ROWS), F32),
                pltpu.VMEM((NX, ROWS, SLAB), BF16),
                pltpu.VMEM((4, ROWS, CH), BF16),
            ],
        ),
        out_shape=jax.ShapeDtypeStruct((ROWS, NX * SLAB), F32),
        compiler_params=pltpu.CompilerParams(vmem_limit_bytes=VMEM_LIMIT),
        cost_estimate=pl.CostEstimate(
            flops=8 * 2 * ROWS * CH * 1100, bytes_accessed=4 * 1024 * 1024, transcendentals=0
        ),
    )(place, *args)


def ring(value, by):
    return lax.ppermute(value, "z", [(i, (i + by) % NZ) for i in range(NZ)])


def round_x(value, by):
    return lax.ppermute(value, "x", [(i, (i + by) % NX) for i in range(NX)])


def together(*lists):
    return lax.optimization_barrier(lists)


def body(factor, white_noise, site_class, site_decay, site_angle, site_mix):
    x = lax.axis_index("x")
    z = lax.axis_index("z")
    tm = lax.axis_index("y") * NCORE + lax.axis_index("c")

    share = lax.dynamic_slice(factor, (tm * 32, 0), (32, factor.shape[1]))
    gathered = lax.all_gather(share, ("x", "y", "c"), tiled=True)
    gathered = gathered.reshape(NX, ROWS, factor.shape[1])

    def cut(by):
        first = lax.rem(x + by, NX) * SLAB
        return lax.dynamic_slice(white_noise, (0, first), (ROWS, SLAB))

    parts = [cut(0)] + [round_x(cut(d), d) for d in (1, 2, 3)]
    steps = []
    for half in range(2):
        start = jnp.concatenate([p[:, half * CH : (half + 1) * CH] for p in parts], axis=0)
        steps.append([start, ring(start, 1), ring(start, -1)])
    first, second = steps
    site_class, site_decay, site_angle, site_mix, *first[1:] = lax.optimization_barrier(
        (site_class, site_decay, site_angle, site_mix, *first[1:])
    )
    for _ in range(2):
        first += [ring(first[-2], 1), ring(first[-1], -1)]
        second[-2:], first[-4:-2] = together(second[-2:], first[-4:-2])
        second += [ring(second[-2], 1), ring(second[-1], -1)]
        first[-2:], second[-4:-2] = together(first[-2:], second[-4:-2])

    toeplitz, final, gain, one, two, eight = tables(site_decay, site_angle, site_mix)
    by_block = site_class.reshape(NX, NZ, ROWS)
    ids = jnp.arange(4, dtype=jnp.int32)
    tile_class = lax.dynamic_slice(by_block, (0, z, 0), (NX, 1, ROWS)).reshape(1, NX * ROWS)
    tile_hot = (tile_class == ids[:, None]).astype(F32)
    own_class = lax.dynamic_slice(by_block, (x, z, 0), (1, 1, ROWS)).reshape(1, ROWS)
    own_hot = (own_class == ids[:, None]).astype(F32)
    own_mask = (own_class.reshape(ROWS, 1) == ids[None, :]).astype(BF16)
    scalars = jnp.stack([x] + [(z + by) % NZ for by in AWAY + (4,)]).astype(jnp.int32)
    place = jnp.stack([tm, x]).astype(jnp.int32)
    for_last = (final, tile_hot, per_row(one, tile_hot))
    for_filter = (
        own_mask, own_hot, per_row(one, own_hot), per_row(two, own_hot), per_row(eight, own_hot),
        toeplitz, final, gain,
    )
    scalars, place, for_last, for_filter, first[5] = lax.optimization_barrier(
        (scalars, place, for_last, for_filter, first[5])
    )
    second[6], _ = together(second[6], first[5])
    opposite = [ring(first[5], 1), ring(second[6], -1)]

    total = product(scalars, gathered, [n for pair in zip(*steps) for n in pair])
    *pieces, to_send = last_product(scalars, gathered, opposite, total, *for_last)
    excitation = [pieces[0]] + [round_x(pieces[d], d) for d in (1, 2, 3)]
    own_ends = lax.all_to_all(to_send, ("y", "c", "x"), 0, 0, tiled=True)
    return filtered(place, *excitation, own_ends, *for_filter)


def solution(mesh):
    fine = Mesh(mesh.devices.reshape(NX, NZ, NY, NCORE), ("x", "z", "y", "c"))
    rows = ("x", "z")
    in_specs = (P(rows, None), P(rows, ("y", "c")), P(), P(), P(), P())
    return jax.shard_map(
        body, mesh=fine, in_specs=in_specs, out_specs=P(rows, ("y", "c")), check_vma=False
    )
```

```python
import functools

import jax
import jax.numpy as jnp
from jax import lax
from jax.experimental import pallas as pl
from jax.experimental.pallas import tpu as pltpu
from jax.sharding import Mesh, PartitionSpec as P

CH = 256
NX, NZ, NY, NCORE = 4, 8, 4, 2
ROWS = 256
SLAB = 512
AWAY = (0, 7, 1, 6, 2, 5, 3)
AHEAD = 3
VMEM_LIMIT = 36 * 1024 * 1024
F32 = jnp.float32
BF16 = jnp.bfloat16
PRECISE = lax.Precision.HIGHEST


def system(site_decay, site_angle, site_mix):
    radius = 1.0 - site_decay
    norm_gain = jnp.sqrt(site_decay * (2.0 - site_decay))
    cos_ground = radius[0] * jnp.cos(site_angle[0])
    sin_ground = radius[0] * jnp.sin(site_angle[0])
    cos_high = radius[1] * jnp.cos(site_angle[1])
    sin_high = radius[1] * jnp.sin(site_angle[1])
    zeros_row = jnp.zeros_like(cos_ground)
    ones_row = jnp.ones_like(cos_ground)
    mix_a, mix_b, out_a, out_b = (site_mix[0], site_mix[1], site_mix[2], site_mix[3])
    row_list = [
        [cos_ground, -sin_ground, zeros_row, zeros_row],
        [sin_ground, cos_ground, zeros_row, zeros_row],
        [
            norm_gain[0] * (mix_a * cos_ground + mix_b * sin_ground),
            norm_gain[0] * (mix_b * cos_ground - mix_a * sin_ground),
            cos_high,
            -sin_high,
        ],
        [zeros_row, zeros_row, sin_high, cos_high],
    ]
    matrix = jnp.stack([jnp.stack(entries, axis=-1) for entries in row_list], axis=1)
    entry_vec = jnp.stack([ones_row, zeros_row, norm_gain[0] * mix_a, zeros_row], axis=-1)
    readout = jnp.stack([zeros_row, zeros_row, norm_gain[1] * out_a, norm_gain[1] * out_b], axis=-1)
    return (matrix, entry_vec, readout)


def tables(site_decay, site_angle, site_mix):
    matrix, entry_vec, readout = system(site_decay, site_angle, site_mix)
    classes = matrix.shape[0]
    powers = matrix[None]
    while powers.shape[0] < CH:
        further = jnp.einsum("kab,jkbc->jkac", powers[-1], powers, precision=PRECISE)
        powers = jnp.concatenate([powers, further], axis=0)
    gains = jnp.einsum("ka,jkab->kbj", readout, powers, precision=PRECISE)
    responses = jnp.einsum("jkab,kb->kja", powers[: CH - 1], entry_vec, precision=PRECISE)
    responses = jnp.concatenate([entry_vec[:, None, :], responses], axis=1)
    impulse = jnp.einsum("ka,kma->km", readout, responses, precision=PRECISE)
    padded_len = 2 * CH
    padded = jnp.concatenate([impulse, jnp.zeros((classes, CH), F32)], axis=1)
    tiled = jnp.tile(padded, (1, CH))[:, : CH * (padded_len - 1)]
    toeplitz = tiled.reshape(classes, CH, padded_len - 1)[:, :, :CH]
    toeplitz = toeplitz.reshape(classes * CH, CH).astype(BF16)
    final = responses[:, ::-1, :].transpose(0, 2, 1).astype(BF16)
    final = jnp.concatenate([final, jnp.zeros_like(final)], axis=1).reshape(classes * 8, CH)
    gains = gains.reshape(classes * 4, CH)
    gains_hi = lax.reduce_precision(gains, 8, 7)
    gains_lo = (gains - gains_hi).astype(BF16)
    gains_hi = gains_hi.astype(BF16)
    gain_stack = jnp.concatenate([gains_hi, gains_lo, gains_hi], axis=0)
    power = powers[-1]
    twice = [power]
    for _ in range(3):
        twice.append(jnp.einsum("kab,kbc->kac", twice[-1], twice[-1], precision=PRECISE))
    return toeplitz, final, gain_stack, power, twice[1], twice[3]


def per_row(power, onehot):
    return jnp.sum(power.transpose(2, 1, 0)[:, :, :, None] * onehot[None, None], axis=2)


def apply_power(table, state):
    out = table[0] * state[0:1]
    for b in range(1, 4):
        out = out + table[b] * state[b : b + 1]
    return out


def load(zs, where, g_ref, noise, held, block, sems):
    every = []
    for b, z in enumerate(where):
        copies = []
        for q in range(NX):
            columns = pl.ds(pl.multiple_of(q * NZ * CH + zs[z] * CH, CH), CH)
            copies.append(
                pltpu.make_async_copy(
                    g_ref.at[pl.ds(q, NX - q), :, columns], held[q].at[b], sems.at[b, q]
                )
            )
        for half in range(2):
            copies.append(
                pltpu.make_async_copy(
                    noise[2 * b + half], block.at[b, half], sems.at[b, NX + half]
                )
            )
        every.append(copies)
    return every


def term(zs, held, block, b, s):
    parts = [held[q][b, s - q] for q in range(s + 1)]
    rows = jnp.concatenate(parts, axis=1) if s else parts[0]
    turns = [pl.multiple_of(lax.rem(zs[0] + NX - q, NX) * ROWS, ROWS) for q in range(s + 1)]
    noise = jnp.concatenate(
        [
            jnp.concatenate([block[b, half, pl.ds(t, ROWS), :] for half in range(2)], axis=1)
            for t in turns
        ],
        axis=0,
    )
    return jnp.dot(rows, noise, preferred_element_type=F32)


def product_kernel(zs, g_ref, *refs):
    count = 2 * len(AWAY)
    noise_refs, (out_ref, *held, block, sems) = refs[:count], refs[count:]
    copies = load(zs, range(1, 8), g_ref, noise_refs, held, block, sems)
    for b in range(AHEAD):
        for copy in copies[b]:
            copy.start()
    for b in range(len(AWAY)):
        for copy in copies[b]:
            copy.wait()
        if b + AHEAD < len(AWAY):
            for copy in copies[b + AHEAD]:
                copy.start()
        for s in range(NX):
            rows = pl.ds(s * ROWS, ROWS)
            value = term(zs, held, block, b, s)
            out_ref[rows, :] = value if b == 0 else out_ref[rows, :] + value


def scratch(blocks):
    return [pltpu.VMEM((blocks, NX - q, ROWS, CH), BF16) for q in range(NX)] + [
        pltpu.VMEM((blocks, 2, NX * ROWS, CH), BF16),
        pltpu.SemaphoreType.DMA((blocks, 3 * NX)),
    ]


def whole(a):
    return pl.BlockSpec(a.shape, lambda i, zs: (0,) * len(a.shape))


ANYWHERE = pl.BlockSpec(memory_space=pl.ANY)


def product(scalars, gathered, noise_blocks):
    out = jax.ShapeDtypeStruct((NX * ROWS, SLAB), F32)
    return pl.pallas_call(
        product_kernel,
        grid_spec=pltpu.PrefetchScalarGridSpec(
            num_scalar_prefetch=1,
            grid=(1,),
            in_specs=[ANYWHERE] * (1 + len(noise_blocks)),
            out_specs=whole(out),
            scratch_shapes=scratch(len(AWAY)),
        ),
        out_shape=out,
        compiler_params=pltpu.CompilerParams(vmem_limit_bytes=VMEM_LIMIT),
        cost_estimate=pl.CostEstimate(
            flops=7 * 2 * 10 * ROWS * CH * SLAB, bytes_accessed=19 * 1048576, transcendentals=0
        ),
    )(scalars, gathered, *noise_blocks)


def last_kernel(
    zs, g_ref, first_ref, second_ref, total_ref, final_ref, onehot_ref,
    power_ref, *refs,
):
    piece_refs, (send_ref, local, acc_ref, *held, block, sems) = refs[:NX], refs[NX:]
    (waits,) = load(zs, (8,), g_ref, (first_ref, second_ref), held, block, sems)
    for copy in waits[NX:] + waits[:NX]:
        copy.start()
    fetch = []
    for s in range(NX):
        rows = pl.ds(s * ROWS, ROWS)
        fetch.append(
            pltpu.make_async_copy(total_ref.at[rows], acc_ref.at[rows], sems.at[0, 2 * NX + s])
        )
        fetch[s].start()
    for copy in waits[NX:]:
        copy.wait()
    for s in range(NX):
        waits[s].wait()
        fetch[s].wait()
        rows = pl.ds(s * ROWS, ROWS)
        local[s] = (acc_ref[rows, :] + term(zs, held, block, 0, s)).astype(BF16)
    for d in range(NX):
        piece_refs[d][...] = local[lax.rem(zs[0] + d, NX)]
    for s in range(NX):
        rows = slice(s * ROWS, (s + 1) * ROWS)
        end = None
        for half in range(2):
            ends = lax.dot_general(
                final_ref[...], local[s, :, half * CH : (half + 1) * CH],
                (((1,), (1,)), ((), ())), preferred_element_type=F32,
            )
            picked = onehot_ref[0:1, rows] * ends[0:4]
            for k in range(1, 4):
                picked = picked + onehot_ref[k : k + 1, rows] * ends[k * 8 : k * 8 + 4]
            end = (
                apply_power([power_ref[b, :, rows] for b in range(4)], end) + picked
                if half
                else picked
            )
        for t in range(s, NY * NCORE * NX, NX):
            send_ref[t] = end


def last_product(scalars, gathered, noise, total, *args):
    out_shape = [jax.ShapeDtypeStruct((ROWS, SLAB), BF16)] * NX
    out_shape.append(jax.ShapeDtypeStruct((NY * NCORE * NX, 4, ROWS), F32))
    return pl.pallas_call(
        last_kernel,
        grid_spec=pltpu.PrefetchScalarGridSpec(
            num_scalar_prefetch=1,
            grid=(1,),
            in_specs=[ANYWHERE] * 4 + [whole(a) for a in args],
            out_specs=[whole(a) for a in out_shape],
            scratch_shapes=[
                pltpu.VMEM((NX, ROWS, SLAB), BF16),
                pltpu.VMEM((NX * ROWS, SLAB), F32),
                *scratch(1),
            ],
        ),
        out_shape=out_shape,
        compiler_params=pltpu.CompilerParams(vmem_limit_bytes=VMEM_LIMIT),
        cost_estimate=pl.CostEstimate(
            flops=2 * 11 * ROWS * CH * SLAB, bytes_accessed=6 * 1048576, transcendentals=0
        ),
    )(scalars, gathered, *noise, total, *args)


def filter_kernel(
    place, own_ref, by_one_ref, by_two_ref, by_three_ref, slabs_ref, mask_ref, onehot_ref,
    one_ref, two_ref, eight_ref, toeplitz_ref, final_ref, gain_ref, out_ref, state_ref, local_ref, spread_ref,
):
    step = pl.program_id(0)

    @pl.when(step == 0)
    def _():
        for d, ref in enumerate((own_ref, by_one_ref, by_two_ref, by_three_ref)):
            local_ref[lax.rem(place[1] + NX - d, NX)] = ref[...]
        for k in range(4):
            spread_ref[k] = jnp.broadcast_to(mask_ref[:, k : k + 1], (ROWS, CH))
        slabs = slabs_ref[...].reshape(NY * NCORE, NX, 4, ROWS)
        ends = slabs[:, 0]
        for s in range(1, NX):
            moved = slabs[:, s]
            for b in range(4):
                moved = moved + two_ref[b][None] * ends[:, b : b + 1, :]
            ends = moved
        eight = [eight_ref[b] for b in range(4)]
        state = jnp.zeros((4, ROWS), F32)
        for t in range(NY * NCORE - 1):
            state = jnp.where(t < place[0], apply_power(eight, state) + ends[t], state)
        state_ref[...] = state

    one = [one_ref[b] for b in range(4)]
    state = state_ref[...]
    for half in range(2):
        local = local_ref[step, :, half * CH : (half + 1) * CH]
        masked = jnp.concatenate([local * spread_ref[k] for k in range(4)], axis=1)
        spread = jnp.concatenate([onehot_ref[k : k + 1, :] * state for k in range(4)], axis=0)
        high = spread.astype(BF16)
        low = (spread - high.astype(F32)).astype(BF16)
        stacked = jnp.concatenate([high, high, low], axis=0)
        carried = lax.dot_general(
            stacked, gain_ref[...], (((0,), (0,)), ((), ())), preferred_element_type=F32
        )
        out_ref[:, half * CH : (half + 1) * CH] = (
            jnp.dot(masked, toeplitz_ref[...], preferred_element_type=F32) + carried
        )
        ends = lax.dot_general(
            final_ref[...], local, (((1,), (1,)), ((), ())), preferred_element_type=F32
        )
        entered = onehot_ref[0:1, :] * ends[0:4]
        for k in range(1, 4):
            entered = entered + onehot_ref[k : k + 1, :] * ends[k * 8 : k * 8 + 4]
        state = apply_power(one, state) + entered
    state_ref[...] = state


def filtered(place, *args):
    return pl.pallas_call(
        filter_kernel,
        grid_spec=pltpu.PrefetchScalarGridSpec(
            num_scalar_prefetch=1,
            grid=(NX,),
            in_specs=[whole(a) for a in args],
            out_specs=pl.BlockSpec((ROWS, SLAB), lambda i, zs: (0, i)),
            scratch_shapes=[
                pltpu.VMEM((4, ROWS), F32),
                pltpu.VMEM((NX, ROWS, SLAB), BF16),
                pltpu.VMEM((4, ROWS, CH), BF16),
            ],
        ),
        out_shape=jax.ShapeDtypeStruct((ROWS, NX * SLAB), F32),
        compiler_params=pltpu.CompilerParams(vmem_limit_bytes=VMEM_LIMIT),
        cost_estimate=pl.CostEstimate(
            flops=8 * 2 * ROWS * CH * 1100, bytes_accessed=4 * 1024 * 1024, transcendentals=0
        ),
    )(place, *args)


def ring(value, by):
    return lax.ppermute(value, "z", [(i, (i + by) % NZ) for i in range(NZ)])


def round_x(value, by):
    return lax.ppermute(value, "x", [(i, (i + by) % NX) for i in range(NX)])


def together(*lists):
    return lax.optimization_barrier(lists)


def body(factor, white_noise, site_class, site_decay, site_angle, site_mix):
    x = lax.axis_index("x")
    z = lax.axis_index("z")
    tm = lax.axis_index("y") * NCORE + lax.axis_index("c")

    share = lax.dynamic_slice(factor, (tm * 32, 0), (32, factor.shape[1]))
    gathered = lax.all_gather(share, ("x", "y", "c"), tiled=True)
    gathered = gathered.reshape(NX, ROWS, factor.shape[1])

    def cut(by):
        first = lax.rem(x + by, NX) * SLAB
        return lax.dynamic_slice(white_noise, (0, first), (ROWS, SLAB))

    parts = [cut(0)] + [round_x(cut(d), d) for d in (1, 2, 3)]
    steps = []
    for half in range(2):
        start = jnp.concatenate([p[:, half * CH : (half + 1) * CH] for p in parts], axis=0)
        steps.append([start, ring(start, 1), ring(start, -1)])
    first, second = steps
    site_class, site_decay, site_angle, site_mix, *first[1:] = lax.optimization_barrier(
        (site_class, site_decay, site_angle, site_mix, *first[1:])
    )
    for _ in range(2):
        first += [ring(first[-2], 1), ring(first[-1], -1)]
        second[-2:], first[-4:-2] = together(second[-2:], first[-4:-2])
        second += [ring(second[-2], 1), ring(second[-1], -1)]
        first[-2:], second[-4:-2] = together(first[-2:], second[-4:-2])

    toeplitz, final, gain, one, two, eight = tables(site_decay, site_angle, site_mix)
    by_block = site_class.reshape(NX, NZ, ROWS)
    ids = jnp.arange(4, dtype=jnp.int32)
    tile_class = lax.dynamic_slice(by_block, (0, z, 0), (NX, 1, ROWS)).reshape(1, NX * ROWS)
    tile_hot = (tile_class == ids[:, None]).astype(F32)
    own_class = lax.dynamic_slice(by_block, (x, z, 0), (1, 1, ROWS)).reshape(1, ROWS)
    own_hot = (own_class == ids[:, None]).astype(F32)
    own_mask = (own_class.reshape(ROWS, 1) == ids[None, :]).astype(BF16)
    scalars = jnp.stack([x] + [(z + by) % NZ for by in AWAY + (4,)]).astype(jnp.int32)
    place = jnp.stack([tm, x]).astype(jnp.int32)
    for_last = (final, tile_hot, per_row(one, tile_hot))
    for_filter = (
        own_mask, own_hot, per_row(one, own_hot), per_row(two, own_hot), per_row(eight, own_hot),
        toeplitz, final, gain,
    )
    scalars, place, for_last, for_filter, first[5] = lax.optimization_barrier(
        (scalars, place, for_last, for_filter, first[5])
    )
    second[6], _ = together(second[6], first[5])
    opposite = [ring(first[5], 1), ring(second[6], -1)]

    total = product(scalars, gathered, [n for pair in zip(*steps) for n in pair])
    *pieces, to_send = last_product(scalars, gathered, opposite, total, *for_last)
    excitation = [pieces[0]] + [round_x(pieces[d], d) for d in (1, 2, 3)]
    own_ends = lax.all_to_all(to_send, ("y", "c", "x"), 0, 0, tiled=True)
    return filtered(place, *excitation, own_ends, *for_filter)


def solution(mesh):
    fine = Mesh(mesh.devices.reshape(NX, NZ, NY, NCORE), ("x", "z", "y", "c"))
    rows = ("x", "z")
    in_specs = (P(rows, None), P(rows, ("y", "c")), P(), P(), P(), P())
    return jax.shard_map(
        body, mesh=fine, in_specs=in_specs, out_specs=P(rows, ("y", "c")), check_vma=False
    )
```

```python
import functools

import jax
import jax.numpy as jnp
from jax import lax
from jax.experimental import pallas as pl
from jax.experimental.pallas import tpu as pltpu
from jax.sharding import Mesh, PartitionSpec as P

CH = 256
NX, NZ, NY, NCORE = 4, 8, 4, 2
ROWS = 256
SLAB = 512
AWAY = (0, 7, 1, 6, 2, 5, 3)
AHEAD = 3
VMEM_LIMIT = 36 * 1024 * 1024
F32 = jnp.float32
BF16 = jnp.bfloat16
PRECISE = lax.Precision.HIGHEST


def system(site_decay, site_angle, site_mix):
    radius = 1.0 - site_decay
    norm_gain = jnp.sqrt(site_decay * (2.0 - site_decay))
    cos_ground = radius[0] * jnp.cos(site_angle[0])
    sin_ground = radius[0] * jnp.sin(site_angle[0])
    cos_high = radius[1] * jnp.cos(site_angle[1])
    sin_high = radius[1] * jnp.sin(site_angle[1])
    zeros_row = jnp.zeros_like(cos_ground)
    ones_row = jnp.ones_like(cos_ground)
    mix_a, mix_b, out_a, out_b = (site_mix[0], site_mix[1], site_mix[2], site_mix[3])
    row_list = [
        [cos_ground, -sin_ground, zeros_row, zeros_row],
        [sin_ground, cos_ground, zeros_row, zeros_row],
        [
            norm_gain[0] * (mix_a * cos_ground + mix_b * sin_ground),
            norm_gain[0] * (mix_b * cos_ground - mix_a * sin_ground),
            cos_high,
            -sin_high,
        ],
        [zeros_row, zeros_row, sin_high, cos_high],
    ]
    matrix = jnp.stack([jnp.stack(entries, axis=-1) for entries in row_list], axis=1)
    entry_vec = jnp.stack([ones_row, zeros_row, norm_gain[0] * mix_a, zeros_row], axis=-1)
    readout = jnp.stack([zeros_row, zeros_row, norm_gain[1] * out_a, norm_gain[1] * out_b], axis=-1)
    return (matrix, entry_vec, readout)


def tables(site_decay, site_angle, site_mix):
    matrix, entry_vec, readout = system(site_decay, site_angle, site_mix)
    classes = matrix.shape[0]
    powers = matrix[None]
    while powers.shape[0] < CH:
        further = jnp.einsum("kab,jkbc->jkac", powers[-1], powers, precision=PRECISE)
        powers = jnp.concatenate([powers, further], axis=0)
    gains = jnp.einsum("ka,jkab->kbj", readout, powers, precision=PRECISE)
    responses = jnp.einsum("jkab,kb->kja", powers[: CH - 1], entry_vec, precision=PRECISE)
    responses = jnp.concatenate([entry_vec[:, None, :], responses], axis=1)
    impulse = jnp.einsum("ka,kma->km", readout, responses, precision=PRECISE)
    padded_len = 2 * CH
    padded = jnp.concatenate([impulse, jnp.zeros((classes, CH), F32)], axis=1)
    tiled = jnp.tile(padded, (1, CH))[:, : CH * (padded_len - 1)]
    toeplitz = tiled.reshape(classes, CH, padded_len - 1)[:, :, :CH]
    toeplitz = toeplitz.reshape(classes * CH, CH).astype(BF16)
    final = responses[:, ::-1, :].transpose(0, 2, 1).astype(BF16)
    final = jnp.concatenate([final, jnp.zeros_like(final)], axis=1).reshape(classes * 8, CH)
    gains = gains.reshape(classes * 4, CH)
    gains_hi = lax.reduce_precision(gains, 8, 7)
    gains_lo = (gains - gains_hi).astype(BF16)
    gains_hi = gains_hi.astype(BF16)
    gain_stack = jnp.concatenate([gains_hi, gains_lo, gains_hi], axis=0)
    power = powers[-1]
    twice = [power]
    for _ in range(3):
        twice.append(jnp.einsum("kab,kbc->kac", twice[-1], twice[-1], precision=PRECISE))
    return toeplitz, final, gain_stack, power, twice[1], twice[3]


def per_row(power, onehot):
    return jnp.sum(power.transpose(2, 1, 0)[:, :, :, None] * onehot[None, None], axis=2)


def apply_power(table, state):
    out = table[0] * state[0:1]
    for b in range(1, 4):
        out = out + table[b] * state[b : b + 1]
    return out


def load(zs, where, g_ref, noise, held, block, sems):
    every = []
    for b, z in enumerate(where):
        copies = []
        for q in range(NX):
            columns = pl.ds(pl.multiple_of(q * NZ * CH + zs[z] * CH, CH), CH)
            copies.append(
                pltpu.make_async_copy(
                    g_ref.at[pl.ds(q, NX - q), :, columns], held[q].at[b], sems.at[b, q]
                )
            )
        for half in range(2):
            copies.append(
                pltpu.make_async_copy(
                    noise[2 * b + half], block.at[b, half], sems.at[b, NX + half]
                )
            )
        every.append(copies)
    return every


def term(zs, held, block, b, s):
    parts = [held[q][b, s - q] for q in range(s + 1)]
    rows = jnp.concatenate(parts, axis=1) if s else parts[0]
    turns = [pl.multiple_of(lax.rem(zs[0] + NX - q, NX) * ROWS, ROWS) for q in range(s + 1)]
    noise = jnp.concatenate(
        [
            jnp.concatenate([block[b, half, pl.ds(t, ROWS), :] for half in range(2)], axis=1)
            for t in turns
        ],
        axis=0,
    )
    return jnp.dot(rows, noise, preferred_element_type=F32)


def product_kernel(zs, g_ref, *refs):
    count = 2 * len(AWAY)
    noise_refs, (out_ref, *held, block, sems) = refs[:count], refs[count:]
    copies = load(zs, range(1, 8), g_ref, noise_refs, held, block, sems)
    for b in range(AHEAD):
        for copy in copies[b]:
            copy.start()
    for b in range(len(AWAY)):
        for copy in copies[b]:
            copy.wait()
        if b + AHEAD < len(AWAY):
            for copy in copies[b + AHEAD]:
                copy.start()
        for s in range(NX):
            rows = pl.ds(s * ROWS, ROWS)
            value = term(zs, held, block, b, s)
            out_ref[rows, :] = value if b == 0 else out_ref[rows, :] + value


def scratch(blocks):
    return [pltpu.VMEM((blocks, NX - q, ROWS, CH), BF16) for q in range(NX)] + [
        pltpu.VMEM((blocks, 2, NX * ROWS, CH), BF16),
        pltpu.SemaphoreType.DMA((blocks, 3 * NX)),
    ]


def whole(a):
    return pl.BlockSpec(a.shape, lambda i, zs: (0,) * len(a.shape))


ANYWHERE = pl.BlockSpec(memory_space=pl.ANY)


def product(scalars, gathered, noise_blocks):
    out = jax.ShapeDtypeStruct((NX * ROWS, SLAB), F32)
    return pl.pallas_call(
        product_kernel,
        grid_spec=pltpu.PrefetchScalarGridSpec(
            num_scalar_prefetch=1,
            grid=(1,),
            in_specs=[ANYWHERE] * (1 + len(noise_blocks)),
            out_specs=whole(out),
            scratch_shapes=scratch(len(AWAY)),
        ),
        out_shape=out,
        compiler_params=pltpu.CompilerParams(vmem_limit_bytes=VMEM_LIMIT),
        cost_estimate=pl.CostEstimate(
            flops=7 * 2 * 10 * ROWS * CH * SLAB, bytes_accessed=19 * 1048576, transcendentals=0
        ),
    )(scalars, gathered, *noise_blocks)


def last_kernel(
    zs, g_ref, first_ref, second_ref, total_ref, final_ref, onehot_ref,
    power_ref, *refs,
):
    piece_refs, (send_ref, local, acc_ref, *held, block, sems) = refs[:NX], refs[NX:]
    (waits,) = load(zs, (8,), g_ref, (first_ref, second_ref), held, block, sems)
    for copy in waits[NX:] + waits[:NX]:
        copy.start()
    fetch = []
    for s in range(NX):
        rows = pl.ds(s * ROWS, ROWS)
        fetch.append(
            pltpu.make_async_copy(total_ref.at[rows], acc_ref.at[rows], sems.at[0, 2 * NX + s])
        )
        fetch[s].start()
    for copy in waits[NX:]:
        copy.wait()
    for s in range(NX):
        waits[s].wait()
        fetch[s].wait()
        rows = pl.ds(s * ROWS, ROWS)
        local[s] = (acc_ref[rows, :] + term(zs, held, block, 0, s)).astype(BF16)
    for d in range(NX):
        piece_refs[d][...] = local[lax.rem(zs[0] + d, NX)]
    for s in range(NX):
        rows = slice(s * ROWS, (s + 1) * ROWS)
        end = None
        for half in range(2):
            ends = lax.dot_general(
                final_ref[...], local[s, :, half * CH : (half + 1) * CH],
                (((1,), (1,)), ((), ())), preferred_element_type=F32,
            )
            picked = onehot_ref[0:1, rows] * ends[0:4]
            for k in range(1, 4):
                picked = picked + onehot_ref[k : k + 1, rows] * ends[k * 8 : k * 8 + 4]
            end = (
                apply_power([power_ref[b, :, rows] for b in range(4)], end) + picked
                if half
                else picked
            )
        for t in range(s, NY * NCORE * NX, NX):
            send_ref[t] = end


def last_product(scalars, gathered, noise, total, *args):
    out_shape = [jax.ShapeDtypeStruct((ROWS, SLAB), BF16)] * NX
    out_shape.append(jax.ShapeDtypeStruct((NY * NCORE * NX, 4, ROWS), F32))
    return pl.pallas_call(
        last_kernel,
        grid_spec=pltpu.PrefetchScalarGridSpec(
            num_scalar_prefetch=1,
            grid=(1,),
            in_specs=[ANYWHERE] * 4 + [whole(a) for a in args],
            out_specs=[whole(a) for a in out_shape],
            scratch_shapes=[
                pltpu.VMEM((NX, ROWS, SLAB), BF16),
                pltpu.VMEM((NX * ROWS, SLAB), F32),
                *scratch(1),
            ],
        ),
        out_shape=out_shape,
        compiler_params=pltpu.CompilerParams(vmem_limit_bytes=VMEM_LIMIT),
        cost_estimate=pl.CostEstimate(
            flops=2 * 11 * ROWS * CH * SLAB, bytes_accessed=6 * 1048576, transcendentals=0
        ),
    )(scalars, gathered, *noise, total, *args)


def filter_kernel(
    place, own_ref, by_one_ref, by_two_ref, by_three_ref, slabs_ref, mask_ref, onehot_ref,
    one_ref, two_ref, eight_ref, toeplitz_ref, final_ref, gain_ref, out_ref, state_ref, local_ref, spread_ref,
):
    step = pl.program_id(0)

    @pl.when(step == 0)
    def _():
        for d, ref in enumerate((own_ref, by_one_ref, by_two_ref, by_three_ref)):
            local_ref[lax.rem(place[1] + NX - d, NX)] = ref[...]
        for k in range(4):
            spread_ref[k] = jnp.broadcast_to(mask_ref[:, k : k + 1], (ROWS, CH))
        slabs = slabs_ref[...].reshape(NY * NCORE, NX, 4, ROWS)
        ends = slabs[:, 0]
        for s in range(1, NX):
            moved = slabs[:, s]
            for b in range(4):
                moved = moved + two_ref[b][None] * ends[:, b : b + 1, :]
            ends = moved
        eight = [eight_ref[b] for b in range(4)]
        state = jnp.zeros((4, ROWS), F32)
        for t in range(NY * NCORE - 1):
            state = jnp.where(t < place[0], apply_power(eight, state) + ends[t], state)
        state_ref[...] = state

    one = [one_ref[b] for b in range(4)]
    state = state_ref[...]
    for half in range(2):
        local = local_ref[step, :, half * CH : (half + 1) * CH]
        masked = jnp.concatenate([local * spread_ref[k] for k in range(4)], axis=1)
        spread = jnp.concatenate([onehot_ref[k : k + 1, :] * state for k in range(4)], axis=0)
        high = spread.astype(BF16)
        low = (spread - high.astype(F32)).astype(BF16)
        stacked = jnp.concatenate([high, high, low], axis=0)
        carried = lax.dot_general(
            stacked, gain_ref[...], (((0,), (0,)), ((), ())), preferred_element_type=F32
        )
        out_ref[:, half * CH : (half + 1) * CH] = (
            jnp.dot(masked, toeplitz_ref[...], preferred_element_type=F32) + carried
        )
        ends = lax.dot_general(
            final_ref[...], local, (((1,), (1,)), ((), ())), preferred_element_type=F32
        )
        entered = onehot_ref[0:1, :] * ends[0:4]
        for k in range(1, 4):
            entered = entered + onehot_ref[k : k + 1, :] * ends[k * 8 : k * 8 + 4]
        state = apply_power(one, state) + entered
    state_ref[...] = state


def filtered(place, *args):
    return pl.pallas_call(
        filter_kernel,
        grid_spec=pltpu.PrefetchScalarGridSpec(
            num_scalar_prefetch=1,
            grid=(NX,),
            in_specs=[whole(a) for a in args],
            out_specs=pl.BlockSpec((ROWS, SLAB), lambda i, zs: (0, i)),
            scratch_shapes=[
                pltpu.VMEM((4, ROWS), F32),
                pltpu.VMEM((NX, ROWS, SLAB), BF16),
                pltpu.VMEM((4, ROWS, CH), BF16),
            ],
        ),
        out_shape=jax.ShapeDtypeStruct((ROWS, NX * SLAB), F32),
        compiler_params=pltpu.CompilerParams(vmem_limit_bytes=VMEM_LIMIT),
        cost_estimate=pl.CostEstimate(
            flops=8 * 2 * ROWS * CH * 1100, bytes_accessed=4 * 1024 * 1024, transcendentals=0
        ),
    )(place, *args)


def ring(value, by):
    return lax.ppermute(value, "z", [(i, (i + by) % NZ) for i in range(NZ)])


def round_x(value, by):
    return lax.ppermute(value, "x", [(i, (i + by) % NX) for i in range(NX)])


def together(*lists):
    return lax.optimization_barrier(lists)


def body(factor, white_noise, site_class, site_decay, site_angle, site_mix):
    x = lax.axis_index("x")
    z = lax.axis_index("z")
    tm = lax.axis_index("y") * NCORE + lax.axis_index("c")

    share = lax.dynamic_slice(factor, (tm * 32, 0), (32, factor.shape[1]))
    gathered = lax.all_gather(share, ("x", "y", "c"), tiled=True)
    gathered = gathered.reshape(NX, ROWS, factor.shape[1])

    def cut(by):
        first = lax.rem(x + by, NX) * SLAB
        return lax.dynamic_slice(white_noise, (0, first), (ROWS, SLAB))

    parts = [cut(0)] + [round_x(cut(d), d) for d in (1, 2, 3)]
    site_class, site_decay, site_angle, site_mix, *parts[1:] = lax.optimization_barrier(
        (site_class, site_decay, site_angle, site_mix, *parts[1:])
    )
    steps = []
    for half in range(2):
        start = jnp.concatenate([p[:, half * CH : (half + 1) * CH] for p in parts], axis=0)
        steps.append([start, ring(start, 1), ring(start, -1)])
    first, second = steps
    for _ in range(2):
        first += [ring(first[-2], 1), ring(first[-1], -1)]
        second[-2:], first[-4:-2] = together(second[-2:], first[-4:-2])
        second += [ring(second[-2], 1), ring(second[-1], -1)]
        first[-2:], second[-4:-2] = together(first[-2:], second[-4:-2])

    toeplitz, final, gain, one, two, eight = tables(site_decay, site_angle, site_mix)
    by_block = site_class.reshape(NX, NZ, ROWS)
    ids = jnp.arange(4, dtype=jnp.int32)
    tile_class = lax.dynamic_slice(by_block, (0, z, 0), (NX, 1, ROWS)).reshape(1, NX * ROWS)
    tile_hot = (tile_class == ids[:, None]).astype(F32)
    own_class = lax.dynamic_slice(by_block, (x, z, 0), (1, 1, ROWS)).reshape(1, ROWS)
    own_hot = (own_class == ids[:, None]).astype(F32)
    own_mask = (own_class.reshape(ROWS, 1) == ids[None, :]).astype(BF16)
    scalars = jnp.stack([x] + [(z + by) % NZ for by in AWAY + (4,)]).astype(jnp.int32)
    place = jnp.stack([tm, x]).astype(jnp.int32)
    for_last = (final, tile_hot, per_row(one, tile_hot))
    for_filter = (
        own_mask, own_hot, per_row(one, own_hot), per_row(two, own_hot), per_row(eight, own_hot),
        toeplitz, final, gain,
    )
    scalars, place, for_last, for_filter, first[5] = lax.optimization_barrier(
        (scalars, place, for_last, for_filter, first[5])
    )
    second[6], _ = together(second[6], first[5])
    opposite = [ring(first[5], 1), ring(second[6], -1)]

    total = product(scalars, gathered, [n for pair in zip(*steps) for n in pair])
    *pieces, to_send = last_product(scalars, gathered, opposite, total, *for_last)
    excitation = [pieces[0]] + [round_x(pieces[d], d) for d in (1, 2, 3)]
    own_ends = lax.all_to_all(to_send, ("y", "c", "x"), 0, 0, tiled=True)
    return filtered(place, *excitation, own_ends, *for_filter)


def solution(mesh):
    fine = Mesh(mesh.devices.reshape(NX, NZ, NY, NCORE), ("x", "z", "y", "c"))
    rows = ("x", "z")
    in_specs = (P(rows, None), P(rows, ("y", "c")), P(), P(), P(), P())
    return jax.shard_map(
        body, mesh=fine, in_specs=in_specs, out_specs=P(rows, ("y", "c")), check_vma=False
    )
```

```python
import functools

import jax
import jax.numpy as jnp
from jax import lax
from jax.experimental import pallas as pl
from jax.experimental.pallas import tpu as pltpu
from jax.sharding import Mesh, PartitionSpec as P

CH = 256
NX, NZ, NY, NCORE = 4, 8, 4, 2
ROWS = 256
SLAB = 512
AWAY = (0, 7, 1, 6, 2, 5, 3)
AHEAD = 5
VMEM_LIMIT = 36 * 1024 * 1024
F32 = jnp.float32
BF16 = jnp.bfloat16
PRECISE = lax.Precision.HIGHEST


def system(site_decay, site_angle, site_mix):
    radius = 1.0 - site_decay
    norm_gain = jnp.sqrt(site_decay * (2.0 - site_decay))
    cos_ground = radius[0] * jnp.cos(site_angle[0])
    sin_ground = radius[0] * jnp.sin(site_angle[0])
    cos_high = radius[1] * jnp.cos(site_angle[1])
    sin_high = radius[1] * jnp.sin(site_angle[1])
    zeros_row = jnp.zeros_like(cos_ground)
    ones_row = jnp.ones_like(cos_ground)
    mix_a, mix_b, out_a, out_b = (site_mix[0], site_mix[1], site_mix[2], site_mix[3])
    row_list = [
        [cos_ground, -sin_ground, zeros_row, zeros_row],
        [sin_ground, cos_ground, zeros_row, zeros_row],
        [
            norm_gain[0] * (mix_a * cos_ground + mix_b * sin_ground),
            norm_gain[0] * (mix_b * cos_ground - mix_a * sin_ground),
            cos_high,
            -sin_high,
        ],
        [zeros_row, zeros_row, sin_high, cos_high],
    ]
    matrix = jnp.stack([jnp.stack(entries, axis=-1) for entries in row_list], axis=1)
    entry_vec = jnp.stack([ones_row, zeros_row, norm_gain[0] * mix_a, zeros_row], axis=-1)
    readout = jnp.stack([zeros_row, zeros_row, norm_gain[1] * out_a, norm_gain[1] * out_b], axis=-1)
    return (matrix, entry_vec, readout)


def tables(site_decay, site_angle, site_mix):
    matrix, entry_vec, readout = system(site_decay, site_angle, site_mix)
    classes = matrix.shape[0]
    powers = matrix[None]
    while powers.shape[0] < CH:
        further = jnp.einsum("kab,jkbc->jkac", powers[-1], powers, precision=PRECISE)
        powers = jnp.concatenate([powers, further], axis=0)
    gains = jnp.einsum("ka,jkab->kbj", readout, powers, precision=PRECISE)
    responses = jnp.einsum("jkab,kb->kja", powers[: CH - 1], entry_vec, precision=PRECISE)
    responses = jnp.concatenate([entry_vec[:, None, :], responses], axis=1)
    impulse = jnp.einsum("ka,kma->km", readout, responses, precision=PRECISE)
    padded_len = 2 * CH
    padded = jnp.concatenate([impulse, jnp.zeros((classes, CH), F32)], axis=1)
    tiled = jnp.tile(padded, (1, CH))[:, : CH * (padded_len - 1)]
    toeplitz = tiled.reshape(classes, CH, padded_len - 1)[:, :, :CH]
    toeplitz = toeplitz.reshape(classes * CH, CH).astype(BF16)
    final = responses[:, ::-1, :].transpose(0, 2, 1).astype(BF16)
    final = jnp.concatenate([final, jnp.zeros_like(final)], axis=1).reshape(classes * 8, CH)
    gains = gains.reshape(classes * 4, CH)
    gains_hi = lax.reduce_precision(gains, 8, 7)
    gains_lo = (gains - gains_hi).astype(BF16)
    gains_hi = gains_hi.astype(BF16)
    gain_stack = jnp.concatenate([gains_hi, gains_lo, gains_hi], axis=0)
    power = powers[-1]
    twice = [power]
    for _ in range(3):
        twice.append(jnp.einsum("kab,kbc->kac", twice[-1], twice[-1], precision=PRECISE))
    return toeplitz, final, gain_stack, power, twice[1], twice[3]


def per_row(power, onehot):
    return jnp.sum(power.transpose(2, 1, 0)[:, :, :, None] * onehot[None, None], axis=2)


def apply_power(table, state):
    out = table[0] * state[0:1]
    for b in range(1, 4):
        out = out + table[b] * state[b : b + 1]
    return out


def load(zs, where, g_ref, noise, held, block, sems):
    every = []
    for b, z in enumerate(where):
        copies = []
        for q in range(NX):
            columns = pl.ds(pl.multiple_of(q * NZ * CH + zs[z] * CH, CH), CH)
            copies.append(
                pltpu.make_async_copy(
                    g_ref.at[pl.ds(q, NX - q), :, columns], held[q].at[b], sems.at[b, q]
                )
            )
        for half in range(2):
            copies.append(
                pltpu.make_async_copy(
                    noise[2 * b + half], block.at[b, half], sems.at[b, NX + half]
                )
            )
        every.append(copies)
    return every


def term(zs, held, block, b, s):
    parts = [held[q][b, s - q] for q in range(s + 1)]
    rows = jnp.concatenate(parts, axis=1) if s else parts[0]
    turns = [pl.multiple_of(lax.rem(zs[0] + NX - q, NX) * ROWS, ROWS) for q in range(s + 1)]
    noise = jnp.concatenate(
        [
            jnp.concatenate([block[b, half, pl.ds(t, ROWS), :] for half in range(2)], axis=1)
            for t in turns
        ],
        axis=0,
    )
    return jnp.dot(rows, noise, preferred_element_type=F32)


def product_kernel(zs, g_ref, *refs):
    count = 2 * len(AWAY)
    noise_refs, (out_ref, *held, block, sems) = refs[:count], refs[count:]
    copies = load(zs, range(1, 8), g_ref, noise_refs, held, block, sems)
    for b in range(AHEAD):
        for copy in copies[b]:
            copy.start()
    for b in range(len(AWAY)):
        for copy in copies[b]:
            copy.wait()
        if b + AHEAD < len(AWAY):
            for copy in copies[b + AHEAD]:
                copy.start()
        for s in range(NX):
            rows = pl.ds(s * ROWS, ROWS)
            value = term(zs, held, block, b, s)
            out_ref[rows, :] = value if b == 0 else out_ref[rows, :] + value


def scratch(blocks):
    return [pltpu.VMEM((blocks, NX - q, ROWS, CH), BF16) for q in range(NX)] + [
        pltpu.VMEM((blocks, 2, NX * ROWS, CH), BF16),
        pltpu.SemaphoreType.DMA((blocks, 3 * NX)),
    ]


def whole(a):
    return pl.BlockSpec(a.shape, lambda i, zs: (0,) * len(a.shape))


ANYWHERE = pl.BlockSpec(memory_space=pl.ANY)


def product(scalars, gathered, noise_blocks):
    out = jax.ShapeDtypeStruct((NX * ROWS, SLAB), F32)
    return pl.pallas_call(
        product_kernel,
        grid_spec=pltpu.PrefetchScalarGridSpec(
            num_scalar_prefetch=1,
            grid=(1,),
            in_specs=[ANYWHERE] * (1 + len(noise_blocks)),
            out_specs=whole(out),
            scratch_shapes=scratch(len(AWAY)),
        ),
        out_shape=out,
        compiler_params=pltpu.CompilerParams(vmem_limit_bytes=VMEM_LIMIT),
        cost_estimate=pl.CostEstimate(
            flops=7 * 2 * 10 * ROWS * CH * SLAB, bytes_accessed=19 * 1048576, transcendentals=0
        ),
    )(scalars, gathered, *noise_blocks)


def last_kernel(
    zs, g_ref, first_ref, second_ref, total_ref, final_ref, onehot_ref,
    power_ref, *refs,
):
    piece_refs, (send_ref, local, acc_ref, *held, block, sems) = refs[:NX], refs[NX:]
    (waits,) = load(zs, (8,), g_ref, (first_ref, second_ref), held, block, sems)
    for copy in waits[NX:] + waits[:NX]:
        copy.start()
    fetch = []
    for s in range(NX):
        rows = pl.ds(s * ROWS, ROWS)
        fetch.append(
            pltpu.make_async_copy(total_ref.at[rows], acc_ref.at[rows], sems.at[0, 2 * NX + s])
        )
        fetch[s].start()
    for copy in waits[NX:]:
        copy.wait()
    for s in range(NX):
        waits[s].wait()
        fetch[s].wait()
        rows = pl.ds(s * ROWS, ROWS)
        local[s] = (acc_ref[rows, :] + term(zs, held, block, 0, s)).astype(BF16)
    for d in range(NX):
        piece_refs[d][...] = local[lax.rem(zs[0] + d, NX)]
    for s in range(NX):
        rows = slice(s * ROWS, (s + 1) * ROWS)
        end = None
        for half in range(2):
            ends = lax.dot_general(
                final_ref[...], local[s, :, half * CH : (half + 1) * CH],
                (((1,), (1,)), ((), ())), preferred_element_type=F32,
            )
            picked = onehot_ref[0:1, rows] * ends[0:4]
            for k in range(1, 4):
                picked = picked + onehot_ref[k : k + 1, rows] * ends[k * 8 : k * 8 + 4]
            end = (
                apply_power([power_ref[b, :, rows] for b in range(4)], end) + picked
                if half
                else picked
            )
        for t in range(s, NY * NCORE * NX, NX):
            send_ref[t] = end


def last_product(scalars, gathered, noise, total, *args):
    out_shape = [jax.ShapeDtypeStruct((ROWS, SLAB), BF16)] * NX
    out_shape.append(jax.ShapeDtypeStruct((NY * NCORE * NX, 4, ROWS), F32))
    return pl.pallas_call(
        last_kernel,
        grid_spec=pltpu.PrefetchScalarGridSpec(
            num_scalar_prefetch=1,
            grid=(1,),
            in_specs=[ANYWHERE] * 4 + [whole(a) for a in args],
            out_specs=[whole(a) for a in out_shape],
            scratch_shapes=[
                pltpu.VMEM((NX, ROWS, SLAB), BF16),
                pltpu.VMEM((NX * ROWS, SLAB), F32),
                *scratch(1),
            ],
        ),
        out_shape=out_shape,
        compiler_params=pltpu.CompilerParams(vmem_limit_bytes=VMEM_LIMIT),
        cost_estimate=pl.CostEstimate(
            flops=2 * 11 * ROWS * CH * SLAB, bytes_accessed=6 * 1048576, transcendentals=0
        ),
    )(scalars, gathered, *noise, total, *args)


def filter_kernel(
    place, own_ref, by_one_ref, by_two_ref, by_three_ref, slabs_ref, mask_ref, onehot_ref,
    one_ref, two_ref, eight_ref, toeplitz_ref, final_ref, gain_ref, out_ref, state_ref, local_ref, spread_ref,
):
    step = pl.program_id(0)

    @pl.when(step == 0)
    def _():
        for d, ref in enumerate((own_ref, by_one_ref, by_two_ref, by_three_ref)):
            local_ref[lax.rem(place[1] + NX - d, NX)] = ref[...]
        for k in range(4):
            spread_ref[k] = jnp.broadcast_to(mask_ref[:, k : k + 1], (ROWS, CH))
        slabs = slabs_ref[...].reshape(NY * NCORE, NX, 4, ROWS)
        ends = slabs[:, 0]
        for s in range(1, NX):
            moved = slabs[:, s]
            for b in range(4):
                moved = moved + two_ref[b][None] * ends[:, b : b + 1, :]
            ends = moved
        eight = [eight_ref[b] for b in range(4)]
        state = jnp.zeros((4, ROWS), F32)
        for t in range(NY * NCORE - 1):
            state = jnp.where(t < place[0], apply_power(eight, state) + ends[t], state)
        state_ref[...] = state

    one = [one_ref[b] for b in range(4)]
    state = state_ref[...]
    for half in range(2):
        local = local_ref[step, :, half * CH : (half + 1) * CH]
        masked = jnp.concatenate([local * spread_ref[k] for k in range(4)], axis=1)
        spread = jnp.concatenate([onehot_ref[k : k + 1, :] * state for k in range(4)], axis=0)
        high = spread.astype(BF16)
        low = (spread - high.astype(F32)).astype(BF16)
        stacked = jnp.concatenate([high, high, low], axis=0)
        carried = lax.dot_general(
            stacked, gain_ref[...], (((0,), (0,)), ((), ())), preferred_element_type=F32
        )
        out_ref[:, half * CH : (half + 1) * CH] = (
            jnp.dot(masked, toeplitz_ref[...], preferred_element_type=F32) + carried
        )
        ends = lax.dot_general(
            final_ref[...], local, (((1,), (1,)), ((), ())), preferred_element_type=F32
        )
        entered = onehot_ref[0:1, :] * ends[0:4]
        for k in range(1, 4):
            entered = entered + onehot_ref[k : k + 1, :] * ends[k * 8 : k * 8 + 4]
        state = apply_power(one, state) + entered
    state_ref[...] = state


def filtered(place, *args):
    return pl.pallas_call(
        filter_kernel,
        grid_spec=pltpu.PrefetchScalarGridSpec(
            num_scalar_prefetch=1,
            grid=(NX,),
            in_specs=[whole(a) for a in args],
            out_specs=pl.BlockSpec((ROWS, SLAB), lambda i, zs: (0, i)),
            scratch_shapes=[
                pltpu.VMEM((4, ROWS), F32),
                pltpu.VMEM((NX, ROWS, SLAB), BF16),
                pltpu.VMEM((4, ROWS, CH), BF16),
            ],
        ),
        out_shape=jax.ShapeDtypeStruct((ROWS, NX * SLAB), F32),
        compiler_params=pltpu.CompilerParams(vmem_limit_bytes=VMEM_LIMIT),
        cost_estimate=pl.CostEstimate(
            flops=8 * 2 * ROWS * CH * 1100, bytes_accessed=4 * 1024 * 1024, transcendentals=0
        ),
    )(place, *args)


def ring(value, by):
    return lax.ppermute(value, "z", [(i, (i + by) % NZ) for i in range(NZ)])


def round_x(value, by):
    return lax.ppermute(value, "x", [(i, (i + by) % NX) for i in range(NX)])


def together(*lists):
    return lax.optimization_barrier(lists)


def body(factor, white_noise, site_class, site_decay, site_angle, site_mix):
    x = lax.axis_index("x")
    z = lax.axis_index("z")
    tm = lax.axis_index("y") * NCORE + lax.axis_index("c")

    share = lax.dynamic_slice(factor, (tm * 32, 0), (32, factor.shape[1]))
    gathered = lax.all_gather(share, ("x", "y", "c"), tiled=True)
    gathered = gathered.reshape(NX, ROWS, factor.shape[1])

    def cut(by):
        first = lax.rem(x + by, NX) * SLAB
        return lax.dynamic_slice(white_noise, (0, first), (ROWS, SLAB))

    parts = [cut(0)] + [round_x(cut(d), d) for d in (1, 2, 3)]
    steps = []
    for half in range(2):
        start = jnp.concatenate([p[:, half * CH : (half + 1) * CH] for p in parts], axis=0)
        steps.append([start, ring(start, 1), ring(start, -1)])
    first, second = steps
    site_class, site_decay, site_angle, site_mix, *first[1:] = lax.optimization_barrier(
        (site_class, site_decay, site_angle, site_mix, *first[1:])
    )
    for _ in range(2):
        first += [ring(first[-2], 1), ring(first[-1], -1)]
        second[-2:], first[-4:-2] = together(second[-2:], first[-4:-2])
        second += [ring(second[-2], 1), ring(second[-1], -1)]
        first[-2:], second[-4:-2] = together(first[-2:], second[-4:-2])

    toeplitz, final, gain, one, two, eight = tables(site_decay, site_angle, site_mix)
    by_block = site_class.reshape(NX, NZ, ROWS)
    ids = jnp.arange(4, dtype=jnp.int32)
    tile_class = lax.dynamic_slice(by_block, (0, z, 0), (NX, 1, ROWS)).reshape(1, NX * ROWS)
    tile_hot = (tile_class == ids[:, None]).astype(F32)
    own_class = lax.dynamic_slice(by_block, (x, z, 0), (1, 1, ROWS)).reshape(1, ROWS)
    own_hot = (own_class == ids[:, None]).astype(F32)
    own_mask = (own_class.reshape(ROWS, 1) == ids[None, :]).astype(BF16)
    scalars = jnp.stack([x] + [(z + by) % NZ for by in AWAY + (4,)]).astype(jnp.int32)
    place = jnp.stack([tm, x]).astype(jnp.int32)
    for_last = (final, tile_hot, per_row(one, tile_hot))
    for_filter = (
        own_mask, own_hot, per_row(one, own_hot), per_row(two, own_hot), per_row(eight, own_hot),
        toeplitz, final, gain,
    )
    scalars, place, for_last, for_filter, first[5] = lax.optimization_barrier(
        (scalars, place, for_last, for_filter, first[5])
    )
    second[6], _ = together(second[6], first[5])
    opposite = [ring(first[5], 1), ring(second[6], -1)]

    total = product(scalars, gathered, [n for pair in zip(*steps) for n in pair])
    *pieces, to_send = last_product(scalars, gathered, opposite, total, *for_last)
    excitation = [pieces[0]] + [round_x(pieces[d], d) for d in (1, 2, 3)]
    own_ends = lax.all_to_all(to_send, ("y", "c", "x"), 0, 0, tiled=True)
    return filtered(place, *excitation, own_ends, *for_filter)


def solution(mesh):
    fine = Mesh(mesh.devices.reshape(NX, NZ, NY, NCORE), ("x", "z", "y", "c"))
    rows = ("x", "z")
    in_specs = (P(rows, None), P(rows, ("y", "c")), P(), P(), P(), P())
    return jax.shard_map(
        body, mesh=fine, in_specs=in_specs, out_specs=P(rows, ("y", "c")), check_vma=False
    )
```
